32 devices in a mesh: seq: 8 (over z, y), fsdp: 4 (over x, core).
Axes of the slice: x: 2, y: 2, z: 4, core: 2. Of those that a mesh axis runs over, the one named last changes fastest.
Arguments:
- latents: float32 [8, 1024, 64], P('fsdp', 'seq'), may hold values from -6 to 6
- gaussian_noise: float32 [8, 1024, 64], P('fsdp', 'seq'), may hold values from -6 to 6
- timesteps: float32 [8], P('fsdp'), may hold values from 0.05 to 0.95
- lengths: int32 [8], P('fsdp'), may hold values from 385 to 1024, as said below
- buckets: int32 [8], P('fsdp'), may hold values from 0 to 3
- context: bfloat16 [8, 128, 768], P('fsdp'), may hold values from -6 to 6
- attention_weights: float32 [6, 1536, 1536], P(None, None, ('seq', 'fsdp')), may hold values from -0.15625 to 0.15625
- attention_moment: float32 [6, 1536, 1536], P(None, None, ('seq', 'fsdp')), may hold values from -2.2888184e-05 to 2.2888184e-05
- cross_weights: float32 [2, 1536, 768], P(None, None, ('seq', 'fsdp')), may hold values from -0.21875 to 0.21875
- cross_moment: float32 [2, 1536, 768], P(None, None, ('seq', 'fsdp')), may hold values from -2.2888184e-05 to 2.2888184e-05
- gate_up_weights: float32 [12288, 1536], P(('seq', 'fsdp')), may hold values from -0.15625 to 0.15625
- gate_up_first: float32 [12288, 1536], P(('seq', 'fsdp')), may hold values from -2.3841858e-06 to 2.3841858e-06
- gate_up_second: float32 [12288, 1536], P(('seq', 'fsdp')), may hold values from 1.1667414e-13 to 4.622937e-13
- down_weights: float32 [6144, 1536], P(('seq', 'fsdp')), may hold values from -0.078125 to 0.078125
- down_first: float32 [6144, 1536], P(('seq', 'fsdp')), may hold values from -2.3841858e-06 to 2.3841858e-06
- down_second: float32 [6144, 1536], P(('seq', 'fsdp')), may hold values from 1.1667414e-13 to 4.622937e-13
- latent_weights: float32 [2, 64, 1536], P(None, None, ('seq', 'fsdp')), may hold values from -0.375 to 0.375
- latent_first: float32 [2, 64, 1536], P(None, None, ('seq', 'fsdp')), may hold values from -2.3841858e-06 to 2.3841858e-06
- latent_second: float32 [2, 64, 1536], P(None, None, ('seq', 'fsdp')), may hold values from 1.1667414e-13 to 4.622937e-13
- timing_weights: float32 [256, 1536], P(None, ('seq', 'fsdp')), may hold values from -0.375 to 0.375
- timing_first: float32 [256, 1536], P(None, ('seq', 'fsdp')), may hold values from -2.3841858e-06 to 2.3841858e-06
- timing_second: float32 [256, 1536], P(None, ('seq', 'fsdp')), may hold values from 1.1667414e-13 to 4.622937e-13
- norm_params: float32 [6, 1536], P(None, ('seq', 'fsdp'))
- norm_first: float32 [6, 1536], P(None, ('seq', 'fsdp')), may hold values from -7.6293945e-06 to 7.6293945e-06
- norm_second: float32 [6, 1536], P(None, ('seq', 'fsdp')), may hold values from 1.0566714e-12 to 4.1826577e-12
Outputs:
- loss_value: float32 [], replicated
- clip_norm: float32 [], replicated
- attention_new: float32 [6, 1536, 1536], P(None, None, ('seq', 'fsdp'))
- attention_moment_new: float32 [6, 1536, 1536], P(None, None, ('seq', 'fsdp'))
- attention_copy: bfloat16 [6, 1536, 1536], P(None, None, ('seq', 'fsdp'))
- cross_new: float32 [2, 1536, 768], P(None, None, ('seq', 'fsdp'))
- cross_moment_new: float32 [2, 1536, 768], P(None, None, ('seq', 'fsdp'))
- cross_copy: bfloat16 [2, 1536, 768], P(None, None, ('seq', 'fsdp'))
- gate_up_new: float32 [12288, 1536], P(('seq', 'fsdp'))
- gate_up_first_new: float32 [12288, 1536], P(('seq', 'fsdp'))
- gate_up_second_new: float32 [12288, 1536], P(('seq', 'fsdp'))
- gate_up_copy: bfloat16 [12288, 1536], P(('seq', 'fsdp'))
- down_new: float32 [6144, 1536], P(('seq', 'fsdp'))
- down_first_new: float32 [6144, 1536], P(('seq', 'fsdp'))
- down_second_new: float32 [6144, 1536], P(('seq', 'fsdp'))
- down_copy: bfloat16 [6144, 1536], P(('seq', 'fsdp'))
- latent_new: float32 [2, 64, 1536], P(None, None, ('seq', 'fsdp'))
- latent_first_new: float32 [2, 64, 1536], P(None, None, ('seq', 'fsdp'))
- latent_second_new: float32 [2, 64, 1536], P(None, None, ('seq', 'fsdp'))
- latent_copy: bfloat16 [2, 64, 1536], P(None, None, ('seq', 'fsdp'))
- timing_new: float32 [256, 1536], P(None, ('seq', 'fsdp'))
- timing_first_new: float32 [256, 1536], P(None, ('seq', 'fsdp'))
- timing_second_new: float32 [256, 1536], P(None, ('seq', 'fsdp'))
- timing_copy: bfloat16 [256, 1536], P(None, ('seq', 'fsdp'))
- norm_new: float32 [6, 1536], P(None, ('seq', 'fsdp'))
- norm_first_new: float32 [6, 1536], P(None, ('seq', 'fsdp'))
- norm_second_new: float32 [6, 1536], P(None, ('seq', 'fsdp'))
The draws below stay inside these ranges and needn't reach their ends.
Inputs may be any that keep to these rules, and one draw needn't show every extreme that they name: `lengths`: in each block of 2 consecutive items at least one item has the full length 1024, which one drawn.
All inputs are finite; a program needn't handle non-finite values.
Results may differ from the reference program's by a relative error of at most 0.0015.
The reference program's roundings to bfloat16 on the way count: a program that leaves them out, or rounds other values in their place, can miss the bound.
Values may be sent and summed in bfloat16 or wider, within the bound.
A program may use at most 512 MiB of HBM per device.

```python
import math
import jax
import jax.numpy as jnp
from jax import lax

D = 1536
HEADS = 24
HEAD_DIM = 64
FF = 6144
E = 768
LAT = 64
CTX = 128
FOUR = 256
NBUCK = 4
STEP = 10
B_DEV = 2
SPAN = 128
LEN = 1024
ITEMS = 8
NPARAM = 45425664


def draw_lengths(key, part):
    key = jax.random.fold_in(key, 3)
    first, second, third = jax.random.split(key, 3)
    groups = ITEMS // B_DEV
    long_item = jax.random.randint(first, (groups,), 0, B_DEV)
    halves = jax.random.randint(second, (groups, B_DEV), 1, 3)
    trims = jax.random.randint(third, (groups, B_DEV), 0, SPAN)
    base = LEN // 2 * halves - trims
    full = jnp.arange(B_DEV)[None, :] == long_item[:, None]
    return jnp.where(full, LEN, base).reshape(ITEMS).astype(jnp.int32)


def draw_norm_params(key, part):
    key = jax.random.fold_in(key, 5)
    first, second = jax.random.split(key)
    gains = jax.random.uniform(first, (3, D), jnp.float32, 0.7, 1.3)
    shifts = 0.3 * jax.random.normal(second, (3, D), jnp.float32)
    return jnp.stack([gains, shifts], axis=1).reshape(6, D)


def touch_ends(array, stream_key, low, high):
    longest = array.shape.index(max(array.shape))
    spots = []
    for shift in (0, 1):
        where = [jax.random.randint(jax.random.fold_in(stream_key, axis), (), 0, length) for axis, length in enumerate(array.shape)]
        where[longest] = (where[longest] + shift) % array.shape[longest]
        spots.append(tuple(where))
    return array.at[spots[0]].set(low).at[spots[1]].set(high)


def shard_levels(own_key, extent, shards, low, high):
    level = 1.0
    for axis_at, blocks in shards:
        draws = jax.random.uniform(jax.random.fold_in(jax.random.fold_in(own_key, 6), axis_at), (blocks,), jnp.float32, low / len(shards), high / len(shards))
        level = level * jnp.repeat(jnp.exp(draws), extent[axis_at] // blocks).reshape((-1,) + (1,) * (len(extent) - 1 - axis_at))
    return level


def bell_draw(own_key, extent, deviation, most, pieces=(), kind=jnp.bfloat16):
    drawn = jax.random.normal(own_key, extent, jnp.float32) * deviation
    if len(pieces) > 0:
        drawn = shard_levels(own_key, extent, pieces, -0.22, 0.18) * drawn
    return jnp.clip(drawn, min=-most, max=most).astype(kind)


def setup_inputs(seed: int = 0) -> dict:
    arg_keys = jax.random.split(jax.random.key(seed), 26)
    latents = bell_draw(arg_keys[0], (ITEMS, LEN, LAT), 1.0, 6.0, ((0, 4), (1, 8)), jnp.float32)
    gaussian_noise = bell_draw(arg_keys[1], (ITEMS, LEN, LAT), 1.0, 6.0, ((0, 4), (1, 8)), jnp.float32)
    timesteps = jnp.clip(0.05 + 0.9 * jax.random.uniform(arg_keys[2], (ITEMS,), jnp.float32) ** shard_levels(arg_keys[2], (ITEMS,), ((0, 4),), -0.2, 0.2), 0.05, 0.95)
    lengths = draw_lengths(jax.random.fold_in(arg_keys[25], 71), 0)
    buckets = touch_ends(jax.random.randint(arg_keys[4], (ITEMS,), 0, NBUCK), jax.random.fold_in(arg_keys[4], 1), 0, NBUCK - 1).astype(jnp.int32)
    context = bell_draw(arg_keys[5], (ITEMS, CTX, E), 1.0, 6.0, ((0, 4),))
    attention_weights = bell_draw(arg_keys[6], (6, D, D), D ** -0.5, 0.15625, ((2, 32),), jnp.float32)
    attention_moment = bell_draw(arg_keys[7], (6, D, D), (0.01 * NPARAM ** -0.5), 2.288818359375e-05, ((2, 32),), jnp.float32)
    cross_weights = bell_draw(arg_keys[8], (2, D, E), E ** -0.5, 0.21875, ((2, 32),), jnp.float32)
    cross_moment = bell_draw(arg_keys[9], (2, D, E), (0.01 * NPARAM ** -0.5), 2.288818359375e-05, ((2, 32),), jnp.float32)
    gate_up_weights = bell_draw(arg_keys[10], (2 * FF, D), D ** -0.5, 0.15625, ((0, 32),), jnp.float32)
    gate_up_first = bell_draw(arg_keys[11], (2 * FF, D), (0.0011 * NPARAM ** -0.5), 2.384185791015625e-06, ((0, 32),), jnp.float32)
    gate_up_second = jnp.clip(jnp.exp(math.log(4.62293723267615e-13) - 1.3768155 * jax.random.uniform(arg_keys[12], (2 * FF, D), jnp.float32) ** shard_levels(arg_keys[12], (2 * FF, D), ((0, 32),), -0.2, 0.2)), 1.1667413996746534e-13, 4.62293723267615e-13)
    down_weights = bell_draw(arg_keys[13], (FF, D), FF ** -0.5, 0.078125, ((0, 32),), jnp.float32)
    down_first = bell_draw(arg_keys[14], (FF, D), (0.0011 * NPARAM ** -0.5), 2.384185791015625e-06, ((0, 32),), jnp.float32)
    down_second = jnp.clip(jnp.exp(math.log(4.62293723267615e-13) - 1.3768155 * jax.random.uniform(arg_keys[15], (FF, D), jnp.float32) ** shard_levels(arg_keys[15], (FF, D), ((0, 32),), -0.2, 0.2)), 1.1667413996746534e-13, 4.62293723267615e-13)
    latent_weights = bell_draw(arg_keys[16], (2, LAT, D), (4 * LAT) ** -0.5, 0.375, ((2, 32),), jnp.float32)
    latent_first = bell_draw(arg_keys[17], (2, LAT, D), (0.0011 * NPARAM ** -0.5), 2.384185791015625e-06, ((2, 32),), jnp.float32)
    latent_second = jnp.clip(jnp.exp(math.log(4.62293723267615e-13) - 1.3768155 * jax.random.uniform(arg_keys[18], (2, LAT, D), jnp.float32) ** shard_levels(arg_keys[18], (2, LAT, D), ((2, 32),), -0.2, 0.2)), 1.1667413996746534e-13, 4.62293723267615e-13)
    timing_weights = bell_draw(arg_keys[19], (FOUR, D), FOUR ** -0.5, 0.375, ((1, 32),), jnp.float32)
    timing_first = bell_draw(arg_keys[20], (FOUR, D), (0.0011 * NPARAM ** -0.5), 2.384185791015625e-06, ((1, 32),), jnp.float32)
    timing_second = jnp.clip(jnp.exp(math.log(4.62293723267615e-13) - 1.3768155 * jax.random.uniform(arg_keys[21], (FOUR, D), jnp.float32) ** shard_levels(arg_keys[21], (FOUR, D), ((1, 32),), -0.2, 0.2)), 1.1667413996746534e-13, 4.62293723267615e-13)
    norm_params = draw_norm_params(jax.random.fold_in(arg_keys[25], 71), 0)
    norm_first = bell_draw(arg_keys[23], (6, D), (0.0033 * NPARAM ** -0.5), 7.62939453125e-06, ((1, 32),), jnp.float32)
    norm_second = jnp.clip(jnp.exp(math.log(4.182657692419767e-12) - 1.3758231 * jax.random.uniform(arg_keys[24], (6, D), jnp.float32) ** shard_levels(arg_keys[24], (6, D), ((1, 32),), -0.2, 0.2)), 1.0566713519802318e-12, 4.182657692419767e-12)
    return dict(latents=latents, gaussian_noise=gaussian_noise, timesteps=timesteps, lengths=lengths, buckets=buckets, context=context, attention_weights=attention_weights, attention_moment=attention_moment, cross_weights=cross_weights, cross_moment=cross_moment, gate_up_weights=gate_up_weights, gate_up_first=gate_up_first, gate_up_second=gate_up_second, down_weights=down_weights, down_first=down_first, down_second=down_second, latent_weights=latent_weights, latent_first=latent_first, latent_second=latent_second, timing_weights=timing_weights, timing_first=timing_first, timing_second=timing_second, norm_params=norm_params, norm_first=norm_first, norm_second=norm_second)


@jax.custom_vjp
def low(v):
    return lax.optimization_barrier(v.astype(jnp.bfloat16)).astype(jnp.float32)

@jax.custom_vjp
def low_back(v):
    return v

def low_keep(v):
    return (low(v), None)

def low_pass(kept, grad):
    return (grad,)

def back_keep(v):
    return (v, None)

def back_low(kept, grad):
    return (low(grad),)
low.defvjp(low_keep, low_pass)
low_back.defvjp(back_keep, back_low)
HIGHEST = lax.Precision.HIGHEST
NS_COEF = (3.4445, -4.775, 2.0315)
CLIP_AT = 0.01
MUON_RATE = 0.5
ADAM_RATE = 0.02
GAIN_RATE = 0.2
DECAY_RATE = 0.01

def matmul(left, right):
    return jnp.dot(left, right, precision=HIGHEST)

def layer_norm(hidden, gain, shift):
    centred = hidden - lax.optimization_barrier(jnp.mean(hidden, axis=-1, keepdims=True))
    spread = lax.optimization_barrier(jnp.mean(centred * centred, axis=-1, keepdims=True))
    return centred * lax.rsqrt(spread + 1e-05) * gain + shift

def rotate(values, cosine, sine_table):
    half_dim = values.shape[-1] // 2
    first = values[..., :half_dim]
    second = values[..., half_dim:]
    return jnp.concatenate([first * cosine - second * sine_table, second * cosine + first * sine_table], axis=-1)

def time_features(timesteps):
    count = FOUR // 2
    freqs = jnp.exp(jnp.arange(count, dtype=jnp.float32) * (math.log(100.0) / max(count - 1, 1)))
    phases = 2.0 * math.pi * timesteps[:, None] * freqs[None, :]
    return jnp.concatenate([jnp.cos(phases), jnp.sin(phases)], axis=1)

def self_attend(queries, key_rows, values, live_mask):
    block = min(512, LEN)
    score_scale = math.sqrt(HEAD_DIM)

    def one_block(query_rows):
        scores = low_back(jnp.einsum('qhd,khd->hqk', query_rows, key_rows, precision=HIGHEST) / score_scale)
        scores = jnp.where(live_mask[None, None, :], scores, -1e+30)
        weights = jax.nn.softmax(scores, axis=-1)
        return jnp.einsum('hqk,khd->qhd', low(weights), values, precision=HIGHEST)
    blocks = queries.reshape(LEN // block, block, HEADS, HEAD_DIM)
    return lax.map(jax.checkpoint(one_block), blocks).reshape(LEN, HEADS, HEAD_DIM)

def item_error(weights, item):
    attention, cross, gate_up, down, latent, timing, norms = weights
    noisy_input, target, features, length, context = item
    half_dim = HEAD_DIM // 2
    inverse = 10000.0 ** (-jnp.arange(half_dim, dtype=jnp.float32) / half_dim)
    angles = jnp.arange(LEN, dtype=jnp.float32)[:, None] * inverse[None, :]
    cosine = jnp.cos(angles)[:, None, :]
    sine_table = jnp.sin(angles)[:, None, :]
    score_scale = math.sqrt(HEAD_DIM)
    hidden = low_back(matmul(low(noisy_input), latent[0])) + matmul(low(features)[None, :], timing)
    normed = low(layer_norm(hidden, norms[0], norms[1]))
    queries = rotate(low_back(matmul(normed, attention[0].T)).reshape(LEN, HEADS, HEAD_DIM), cosine, sine_table)
    key_rows = rotate(low_back(matmul(normed, attention[1].T)).reshape(LEN, HEADS, HEAD_DIM), cosine, sine_table)
    values = low(low_back(matmul(normed, attention[2].T))).reshape(LEN, HEADS, HEAD_DIM)
    live_mask = jnp.arange(LEN) < length
    mixed = self_attend(low(queries), low(key_rows), values, live_mask)
    mixed = low(low_back(mixed)).reshape(LEN, D)
    hidden = hidden + low_back(matmul(mixed, attention[3].T))
    normed = low(layer_norm(hidden, norms[2], norms[3]))
    cross_query = low(low_back(matmul(normed, attention[4].T))).reshape(LEN, HEADS, HEAD_DIM)
    cross_key = low(matmul(context, cross[0].T)).reshape(CTX, HEADS, HEAD_DIM)
    cross_value = low(matmul(context, cross[1].T)).reshape(CTX, HEADS, HEAD_DIM)
    scores = low_back(jnp.einsum('qhd,khd->hqk', cross_query, cross_key, precision=HIGHEST) / score_scale)
    weights_cross = low(jax.nn.softmax(scores, axis=-1))
    mixed = jnp.einsum('hqk,khd->qhd', weights_cross, cross_value, precision=HIGHEST)
    mixed = low(low_back(mixed)).reshape(LEN, D)
    hidden = hidden + low_back(matmul(mixed, attention[5].T))
    normed = low(layer_norm(hidden, norms[4], norms[5]))
    gate_both = low_back(matmul(normed, gate_up.T))
    inner_act = low(jax.nn.silu(gate_both[:, :FF]) * gate_both[:, FF:])
    hidden = hidden + low_back(matmul(inner_act, down))
    predicted = low_back(matmul(low(hidden), latent[1].T))
    return lax.optimization_barrier(jnp.sum((predicted - target) ** 2, axis=1))

def orthogonalize(moment):
    stacks, rows, cols = moment.shape
    blocks = moment.reshape(stacks, rows // HEAD_DIM, HEAD_DIM, cols)
    gram = jnp.einsum('sbik,sbjk->sbij', blocks, blocks, precision=HIGHEST)
    block_norm = jnp.sqrt(jnp.trace(gram, axis1=2, axis2=3))[..., None, None] + 1e-07
    current = blocks / block_norm
    products = gram / (block_norm * block_norm)
    for newton_step in range(5):
        if newton_step > 0:
            products = jnp.einsum('sbik,sbjk->sbij', current, current, precision=HIGHEST)
        squared = jnp.einsum('sbij,sbjk->sbik', products, products, precision=HIGHEST)
        mixer = NS_COEF[1] * products + NS_COEF[2] * squared
        current = NS_COEF[0] * current + jnp.einsum('sbij,sbjk->sbik', mixer, current, precision=HIGHEST)
    return current.reshape(stacks, rows, cols)

def muon_update(weight, moment, grad):
    moment_new = 0.95 * moment + grad
    weight_new = weight * (1.0 - MUON_RATE * DECAY_RATE) - MUON_RATE * orthogonalize(moment_new)
    return (weight_new, moment_new)

def adam_update(weight, first, second, grad, rate, decay):
    first_new = 0.9 * first + 0.1 * grad
    second_new = 0.95 * second + 0.05 * grad * grad
    first_hat = first_new / (1.0 - 0.9 ** STEP)
    second_hat = second_new / (1.0 - 0.95 ** STEP)
    weight_new = weight - rate * (first_hat / (jnp.sqrt(second_hat) + 1e-08) + decay * weight)
    return (weight_new, first_new, second_new)

def reference(latents, gaussian_noise, timesteps, lengths, buckets, context, attention_weights, attention_moment, cross_weights, cross_moment, gate_up_weights, gate_up_first, gate_up_second, down_weights, down_first, down_second, latent_weights, latent_first, latent_second, timing_weights, timing_first, timing_second, norm_params, norm_first, norm_second):
    signal = jnp.cos(0.5 * math.pi * timesteps)[:, None, None]
    noise_level = jnp.sin(0.5 * math.pi * timesteps)[:, None, None]
    noisy_input = signal * latents + noise_level * gaussian_noise
    target = signal * gaussian_noise - noise_level * latents
    features = time_features(timesteps)
    context_f = context.astype(jnp.float32)
    onehot = (buckets[:, None] == jnp.arange(NBUCK)[None, :]).astype(jnp.float32)
    counts = matmul(lengths.astype(jnp.float32), onehot)
    present = jnp.sum((counts > 0).astype(jnp.float32))
    bucket_scale = 1.0 / (present * LAT * jnp.maximum(counts, 1.0))
    live_mask = jnp.arange(LEN)[None, :] < lengths[:, None]

    def loss_of(masters):
        weights = tuple((low(weight) for weight in masters))
        errors = lax.map(jax.checkpoint(lambda item: item_error(weights, item)), (noisy_input, target, features, lengths, context_f))
        per_item = lax.optimization_barrier(jnp.sum(jnp.where(live_mask, errors, 0.0), axis=1))
        return jnp.sum(matmul(per_item, onehot) * bucket_scale)
    masters = (attention_weights, cross_weights, gate_up_weights, down_weights, latent_weights, timing_weights, norm_params)
    loss_value, pullback = jax.vjp(loss_of, masters)
    grads = pullback(jnp.ones_like(loss_value))[0]
    total = sum((jnp.sum(grad * grad) for grad in grads))
    clip_norm = jnp.sqrt(total)
    factor = CLIP_AT / jnp.maximum(clip_norm, CLIP_AT)
    grads = [grad * factor for grad in grads]
    attention_new, attention_moment_new = muon_update(attention_weights, attention_moment, grads[0])
    cross_new, cross_moment_new = muon_update(cross_weights, cross_moment, grads[1])
    gate_up_new, gate_up_first_new, gate_up_second_new = adam_update(gate_up_weights, gate_up_first, gate_up_second, grads[2], ADAM_RATE, DECAY_RATE)
    down_new, down_first_new, down_second_new = adam_update(down_weights, down_first, down_second, grads[3], ADAM_RATE, DECAY_RATE)
    latent_new, latent_first_new, latent_second_new = adam_update(latent_weights, latent_first, latent_second, grads[4], ADAM_RATE, DECAY_RATE)
    timing_new, timing_first_new, timing_second_new = adam_update(timing_weights, timing_first, timing_second, grads[5], ADAM_RATE, DECAY_RATE)
    norm_new, norm_first_new, norm_second_new = adam_update(norm_params, norm_first, norm_second, grads[6], GAIN_RATE, 0.0)
    low_type = jnp.bfloat16
    return (loss_value, clip_norm, attention_new, attention_moment_new, attention_new.astype(low_type), cross_new, cross_moment_new, cross_new.astype(low_type), gate_up_new, gate_up_first_new, gate_up_second_new, gate_up_new.astype(low_type), down_new, down_first_new, down_second_new, down_new.astype(low_type), latent_new, latent_first_new, latent_second_new, latent_new.astype(low_type), timing_new, timing_first_new, timing_second_new, timing_new.astype(low_type), norm_new, norm_first_new, norm_second_new)
```

```python
import math

import jax
import jax.numpy as jnp
from jax import lax
from jax.experimental import pallas as pl
from jax.experimental.pallas import tpu as pltpu
from jax.sharding import PartitionSpec as P

D = 1536
HEADS = 24
HEAD_DIM = 64
FF = 6144
E = 768
LAT = 64
FOUR = 256
NBUCK = 4
STEP = 10


HIGHEST = lax.Precision.HIGHEST
NS_COEF = (3.4445, -4.775, 2.0315)
CLIP_AT = 0.01
MUON_RATE = 0.5
ADAM_RATE = 0.02
GAIN_RATE = 0.2
DECAY_RATE = 0.01


def times_transposed(left, weight):
    return lax.dot_general(
        left, weight, (((left.ndim - 1,), (1,)), ((), ())), preferred_element_type=jnp.float32
    )


def matmul_low(left, right):
    return jnp.dot(left, right, preferred_element_type=jnp.float32)


def rows_product(left, right):
    return lax.dot_general(
        left, right, (((0,), (0,)), ((), ())), preferred_element_type=jnp.float32
    )


def rows_precise(left, right):
    return lax.dot_general(left, right, (((0,), (0,)), ((), ())), precision=HIGHEST)


def layer_norm(hidden, gain, shift):
    centred = hidden - jnp.mean(hidden, axis=-1, keepdims=True)
    spread = jnp.mean(centred * centred, axis=-1, keepdims=True)
    return centred * lax.rsqrt(spread + 1e-05) * gain + shift


def rotate(values, cosine, sine_table):
    half_dim = values.shape[-1] // 2
    first = values[..., :half_dim]
    second = values[..., half_dim:]
    return jnp.concatenate(
        [first * cosine - second * sine_table, second * cosine + first * sine_table], axis=-1
    )


def time_features(timesteps):
    count = FOUR // 2
    freqs = jnp.exp(jnp.arange(count, dtype=jnp.float32) * (math.log(100.0) / max(count - 1, 1)))
    phases = 2.0 * math.pi * timesteps[:, None] * freqs[None, :]
    return jnp.concatenate([jnp.cos(phases), jnp.sin(phases)], axis=1)


def split_heads(values):
    return values.reshape(values.shape[0], values.shape[1], HEADS, HEAD_DIM)


def scores_of(queries, key_rows):
    return jnp.einsum(
        "bqhd,bkhd->bhqk", queries, key_rows, preferred_element_type=jnp.float32
    ) / math.sqrt(HEAD_DIM)


def masked_scores(queries, key_rows, lengths):
    key_live = jnp.arange(key_rows.shape[1])[None, :] < lengths[:, None]
    return jnp.where(key_live[:, None, None, :], scores_of(queries, key_rows), -1e30)


def attention_forward(queries, key_low, value_low, lengths):
    item_count, frames = (queries.shape[0], queries.shape[1])
    running_top = jnp.full((item_count, HEADS, frames), -1e29, jnp.float32)
    scores = masked_scores(
        queries, split_heads(lax.all_gather(key_low, "seq", axis=1, tiled=True)), lengths
    )
    new_top = jnp.maximum(running_top, jnp.max(scores, axis=-1))
    running_sum = jnp.sum(jnp.exp(scores - new_top[..., None]), axis=-1)
    running_top, running_sum = (new_top, running_sum)
    log_total = running_top + jnp.log(running_sum)
    scores = masked_scores(
        queries, split_heads(lax.all_gather(key_low, "seq", axis=1, tiled=True)), lengths
    )
    weights = jnp.exp(scores - log_total[..., None]).astype(jnp.bfloat16)
    mixed = jnp.einsum(
        "bhqk,bkhd->bqhd",
        weights,
        split_heads(lax.all_gather(value_low, "seq", axis=1, tiled=True)),
        preferred_element_type=jnp.float32,
    )
    return (mixed, log_total)


def attention_backward(
    queries, key_low, value_low, grad_out, log_total, row_delta, lengths, position
):
    key_heads = split_heads(key_low)
    value_heads = split_heads(value_low)
    local_live = (position[None, :] < lengths[:, None])[:, None, None, :]
    query_flat = queries.reshape(key_low.shape).astype(jnp.float32)
    grad_flat = grad_out.reshape(key_low.shape).astype(jnp.float32)
    total_flat = jnp.transpose(log_total, (0, 2, 1))
    pieces = (
        lax.all_gather(query_flat.astype(jnp.bfloat16), "seq", axis=1, tiled=True).astype(
            jnp.float32
        ),
        lax.all_gather(grad_flat.astype(jnp.bfloat16), "seq", axis=1, tiled=True).astype(
            jnp.float32
        ),
        lax.all_gather(total_flat.astype(jnp.bfloat16), "seq", axis=1, tiled=True).astype(
            jnp.float32
        ),
        lax.all_gather(row_delta.astype(jnp.bfloat16), "seq", axis=1, tiled=True).astype(
            jnp.float32
        ),
    )
    query_rows = split_heads(pieces[0].astype(jnp.bfloat16))
    grad_rows = split_heads(pieces[1].astype(jnp.bfloat16))
    total_rows = jnp.transpose(pieces[2], (0, 2, 1))[..., None]
    delta_rows = jnp.transpose(pieces[3], (0, 2, 1))[..., None]
    scores = jnp.where(local_live, scores_of(query_rows, key_heads), -1e30)
    weights = jnp.exp(scores - total_rows)
    grad_value = jnp.einsum(
        "bhqk,bqhd->bkhd",
        weights.astype(jnp.bfloat16),
        grad_rows,
        preferred_element_type=jnp.float32,
    )
    grad_scores = jnp.einsum(
        "bqhd,bkhd->bhqk", grad_rows, value_heads, preferred_element_type=jnp.float32
    )
    pushed = (weights * (grad_scores - delta_rows)).astype(jnp.bfloat16)
    grad_key = jnp.einsum("bhqk,bqhd->bkhd", pushed, query_rows, preferred_element_type=jnp.float32)
    grad_key, grad_value = (grad_key, grad_value)
    delta_heads = jnp.transpose(row_delta, (0, 2, 1))[..., None]
    pieces = (
        lax.all_gather(key_low, "seq", axis=1, tiled=True),
        lax.all_gather(value_low, "seq", axis=1, tiled=True),
    )
    key_rows = split_heads(pieces[0])
    scores = masked_scores(queries, key_rows, lengths)
    weights = jnp.exp(scores - log_total[..., None])
    grad_scores = jnp.einsum(
        "bqhd,bkhd->bhqk", grad_out, split_heads(pieces[1]), preferred_element_type=jnp.float32
    )
    pushed = (weights * (grad_scores - delta_heads)).astype(jnp.bfloat16)
    grad_query = jnp.einsum("bhqk,bkhd->bqhd", pushed, key_rows, preferred_element_type=jnp.float32)
    score_scale = math.sqrt(HEAD_DIM)
    return (grad_query / score_scale, grad_key / score_scale, grad_value)


def layer_forward(weights, noisy_input, features, context, lengths, cosine, sine_table):
    attention, cross, gate_up, down, latent, timing, norms = weights
    norms = norms.astype(jnp.float32)
    item_count, frames, latent_dim = noisy_input.shape
    tokens = item_count * frames
    noisy_low = noisy_input.reshape(tokens, latent_dim).astype(jnp.bfloat16)
    feat_low = features.astype(jnp.bfloat16)
    timed = matmul_low(feat_low, timing)
    start_state = (
        matmul_low(noisy_low, latent[0]).reshape(item_count, frames, D) + timed[:, None, :]
    ).reshape(tokens, D)
    normed_one, back_one = jax.vjp(layer_norm, start_state, norms[0], norms[1])
    normed_one = normed_one.astype(jnp.bfloat16)
    triple = times_transposed(normed_one, attention[:3].reshape(3 * D, D)).reshape(
        item_count, frames, 3, HEADS, HEAD_DIM
    )
    queries = rotate(triple[:, :, 0], cosine, sine_table).astype(jnp.bfloat16)
    key_low = (
        rotate(triple[:, :, 1], cosine, sine_table)
        .astype(jnp.bfloat16)
        .reshape(item_count, frames, D)
    )
    value_low = triple[:, :, 2].astype(jnp.bfloat16).reshape(item_count, frames, D)
    mixed, log_total = attention_forward(queries, key_low, value_low, lengths)
    mixed_low = mixed.reshape(tokens, D).astype(jnp.bfloat16)
    after_self = start_state + times_transposed(mixed_low, attention[3])
    normed_two, back_two = jax.vjp(layer_norm, after_self, norms[2], norms[3])
    normed_two = normed_two.astype(jnp.bfloat16)
    cross_query = (
        times_transposed(normed_two, attention[4])
        .astype(jnp.bfloat16)
        .reshape(item_count, frames, HEADS, HEAD_DIM)
    )
    context_len = context.shape[1]
    cross_pair = times_transposed(
        context.reshape(item_count * context_len, E), cross.reshape(2 * D, E)
    ).astype(jnp.bfloat16)
    cross_pair = cross_pair.reshape(item_count, context_len, 2, HEADS, HEAD_DIM)
    cross_key, cross_value = (cross_pair[:, :, 0], cross_pair[:, :, 1])
    cross_weights = jax.nn.softmax(scores_of(cross_query, cross_key), axis=-1)
    cross_low = cross_weights.astype(jnp.bfloat16)
    cross_out = (
        jnp.einsum("bhqk,bkhd->bqhd", cross_low, cross_value, preferred_element_type=jnp.float32)
        .reshape(tokens, D)
        .astype(jnp.bfloat16)
    )
    after_cross = after_self + times_transposed(cross_out, attention[5])
    normed_three, back_three = jax.vjp(layer_norm, after_cross, norms[4], norms[5])
    normed_three = normed_three.astype(jnp.bfloat16)
    gate_both = times_transposed(normed_three, gate_up)
    gate_half, up_half = (gate_both[:, :FF], gate_both[:, FF:])
    inner_act = (jax.nn.silu(gate_half) * up_half).astype(jnp.bfloat16)
    final_state = (after_cross + matmul_low(inner_act, down)).astype(jnp.bfloat16)
    predicted = times_transposed(final_state, latent[1])
    saved = (
        noisy_low,
        feat_low,
        back_one,
        normed_one,
        queries,
        key_low,
        value_low,
        mixed,
        log_total,
        mixed_low,
        back_two,
        normed_two,
        cross_query,
        cross_key,
        cross_value,
        cross_weights,
        cross_low,
        cross_out,
        back_three,
        normed_three,
        gate_half,
        up_half,
        inner_act,
        final_state,
    )
    return (predicted, saved)


def layer_backward(weights, saved, grad_pred, context, lengths, cosine, sine_table, position):
    attention, cross, gate_up, down, latent, timing, norms = weights
    (
        noisy_low,
        feat_low,
        back_one,
        normed_one,
        queries,
        key_low,
        value_low,
        mixed,
        log_total,
        mixed_low,
        back_two,
        normed_two,
        cross_query,
        cross_key,
        cross_value,
        cross_weights,
        cross_low,
        cross_out,
        back_three,
        normed_three,
        gate_half,
        up_half,
        inner_act,
        final_state,
    ) = saved
    item_count, frames = (queries.shape[0], queries.shape[1])
    tokens = item_count * frames
    grad_out_proj = rows_product(grad_pred, final_state)
    grad_state = matmul_low(grad_pred, latent[1])
    grad_branch = grad_state.astype(jnp.bfloat16)
    down_reduced = lax.psum_scatter(
        rows_product(inner_act, grad_branch), ("seq", "fsdp"), scatter_dimension=0, tiled=True
    )
    grad_inner = times_transposed(grad_branch, down)
    sigmoid_gate = jax.nn.sigmoid(gate_half)
    grad_gate = grad_inner * up_half * sigmoid_gate * (1.0 + gate_half * (1.0 - sigmoid_gate))
    grad_both = jnp.concatenate([grad_gate, grad_inner * gate_half * sigmoid_gate], axis=1).astype(
        jnp.bfloat16
    )
    gate_up_reduced = lax.psum_scatter(
        rows_product(grad_both, normed_three), ("seq", "fsdp"), scatter_dimension=0, tiled=True
    )
    residual_part, gain_three, shift_three = back_three(matmul_low(grad_both, gate_up))
    grad_state = grad_state + residual_part
    grad_branch = grad_state.astype(jnp.bfloat16)
    grad_cross_out = rows_product(grad_branch, cross_out)
    grad_mix = (
        matmul_low(grad_branch, attention[5])
        .astype(jnp.bfloat16)
        .reshape(item_count, frames, HEADS, HEAD_DIM)
    )
    grad_scores = jnp.einsum(
        "bqhd,bkhd->bhqk", grad_mix, cross_value, preferred_element_type=jnp.float32
    )
    grad_cross_value = jnp.einsum(
        "bhqk,bqhd->bkhd", cross_low, grad_mix, preferred_element_type=jnp.float32
    )
    pushed = (
        cross_weights * (grad_scores - jnp.sum(cross_weights * grad_scores, axis=-1, keepdims=True))
    ).astype(jnp.bfloat16)
    score_scale = math.sqrt(HEAD_DIM)
    grad_cross_query = (
        (
            jnp.einsum("bhqk,bkhd->bqhd", pushed, cross_key, preferred_element_type=jnp.float32)
            / score_scale
        )
        .astype(jnp.bfloat16)
        .reshape(tokens, D)
    )
    grad_cross_key = (
        jnp.einsum("bhqk,bqhd->bkhd", pushed, cross_query, preferred_element_type=jnp.float32)
        / score_scale
    )
    context_len = context.shape[1]
    grad_pair = jnp.stack([grad_cross_key, grad_cross_value], axis=2).reshape(
        item_count * context_len, 2 * D
    )
    grad_cross = rows_precise(
        grad_pair, context.reshape(item_count * context_len, E).astype(jnp.float32)
    ).reshape(2, D, E)
    grad_cross_q = rows_product(grad_cross_query, normed_two)
    residual_part, gain_two, shift_two = back_two(matmul_low(grad_cross_query, attention[4]))
    grad_state = grad_state + residual_part
    grad_branch = grad_state.astype(jnp.bfloat16)
    grad_self_out = rows_product(grad_branch, mixed_low)
    grad_mixed = (
        matmul_low(grad_branch, attention[3])
        .astype(jnp.bfloat16)
        .reshape(item_count, frames, HEADS, HEAD_DIM)
    )
    row_delta = jnp.sum(grad_mixed.astype(jnp.float32) * mixed, axis=-1)
    grad_query, grad_key, grad_value = attention_backward(
        queries, key_low, value_low, grad_mixed, log_total, row_delta, lengths, position
    )
    grad_query = rotate(grad_query, cosine, -sine_table)
    grad_key = rotate(grad_key, cosine, -sine_table)
    grad_triple = (
        jnp.stack([grad_query, grad_key, grad_value], axis=2)
        .astype(jnp.bfloat16)
        .reshape(tokens, 3 * D)
    )
    grad_qkv = rows_product(grad_triple, normed_one).reshape(3, D, D)
    residual_part, gain_one, shift_one = back_one(
        matmul_low(grad_triple, attention[:3].reshape(3 * D, D))
    )
    grad_state = grad_state + residual_part
    grad_in_proj = rows_product(noisy_low, grad_state.astype(jnp.bfloat16))
    grad_timed = jnp.sum(grad_state.reshape(item_count, frames, D), axis=1)
    grad_timing = rows_precise(feat_low.astype(jnp.float32), grad_timed)
    grad_attention = jnp.concatenate(
        [grad_qkv, jnp.stack([grad_self_out, grad_cross_q, grad_cross_out])], axis=0
    )
    grad_latent = jnp.stack([grad_in_proj, grad_out_proj])
    grad_norms = jnp.stack([gain_one, shift_one, gain_two, shift_two, gain_three, shift_three])
    return (
        (grad_attention, grad_cross, grad_latent, grad_timing, grad_norms),
        gate_up_reduced,
        down_reduced,
    )


def gram_of(blocks):
    return jnp.einsum("sbik,sbjk->sbij", blocks, blocks, precision=HIGHEST)


def gram_sum(first, second):
    return lax.psum((gram_of(first), gram_of(second)), ("seq", "fsdp"))


def newton_schulz(first_moment, second_moment):
    moments = (first_moment, second_moment)
    blocks = [
        moment.reshape(moment.shape[0], moment.shape[1] // HEAD_DIM, HEAD_DIM, moment.shape[2])
        for moment in moments
    ]
    gram_list = gram_sum(blocks[0], blocks[1])
    block_norm = [
        jnp.sqrt(jnp.trace(gram, axis1=2, axis2=3))[..., None, None] + 1e-07 for gram in gram_list
    ]
    current = [block / norm_value for block, norm_value in zip(blocks, block_norm)]
    products = [gram / (norm_value * norm_value) for gram, norm_value in zip(gram_list, block_norm)]
    for newton_step in range(5):
        if newton_step > 0:
            products = gram_sum(current[0], current[1])
        updated = []
        for block, product in zip(current, products):
            squared = jnp.einsum("sbij,sbjk->sbik", product, product, precision=HIGHEST)
            mixer = NS_COEF[1] * product + NS_COEF[2] * squared
            updated.append(
                NS_COEF[0] * block + jnp.einsum("sbij,sbjk->sbik", mixer, block, precision=HIGHEST)
            )
        current = updated
    return [block.reshape(moment.shape) for block, moment in zip(current, moments)]


def adam_update(weight, first, second, grad, rate, decay):
    first_new = 0.9 * first + 0.1 * grad
    second_new = 0.95 * second + 0.05 * grad * grad
    first_hat = first_new / (1.0 - 0.9**STEP)
    second_hat = second_new / (1.0 - 0.95**STEP)
    weight_new = weight - rate * (first_hat / (jnp.sqrt(second_hat) + 1e-08) + decay * weight)
    return (weight_new, first_new, second_new)


def body(
    latents,
    gaussian_noise,
    timesteps,
    lengths,
    buckets,
    context,
    attention_weights,
    attention_moment,
    cross_weights,
    cross_moment,
    gate_up_weights,
    gate_up_first,
    gate_up_second,
    down_weights,
    down_first,
    down_second,
    latent_weights,
    latent_first,
    latent_second,
    timing_weights,
    timing_first,
    timing_second,
    norm_params,
    norm_first,
    norm_second,
):
    low_type = jnp.bfloat16
    item_count, frames, latent_dim = latents.shape
    tokens = item_count * frames
    onehot = (buckets[:, None] == jnp.arange(NBUCK)[None, :]).astype(jnp.float32)
    counts = lax.psum(jnp.dot(lengths.astype(jnp.float32), onehot, precision=HIGHEST), "fsdp")
    present = jnp.sum((counts > 0).astype(jnp.float32))
    bucket_scale = 1.0 / (present * LAT * jnp.maximum(counts, 1.0))
    item_scale = jnp.dot(onehot, bucket_scale, precision=HIGHEST)
    shards = (
        attention_weights.astype(low_type),
        cross_weights.astype(low_type),
        gate_up_weights.astype(low_type),
        down_weights.astype(low_type),
        latent_weights.astype(low_type),
        timing_weights.astype(low_type),
        norm_params.astype(low_type),
    )
    weights = (
        lax.all_gather(shards[0], ("seq", "fsdp"), axis=2, tiled=True),
        lax.all_gather(shards[1], ("seq", "fsdp"), axis=2, tiled=True),
        lax.all_gather(shards[2], ("seq", "fsdp"), axis=0, tiled=True),
        lax.all_gather(shards[3], ("seq", "fsdp"), axis=0, tiled=True),
        lax.all_gather(shards[4], ("seq", "fsdp"), axis=2, tiled=True),
        lax.all_gather(shards[5], ("seq", "fsdp"), axis=1, tiled=True),
        lax.all_gather(shards[6], ("seq", "fsdp"), axis=1, tiled=True),
    )
    signal = jnp.cos(0.5 * math.pi * timesteps)[:, None, None]
    noise_level = jnp.sin(0.5 * math.pi * timesteps)[:, None, None]
    noisy_input = signal * latents + noise_level * gaussian_noise
    target = (signal * gaussian_noise - noise_level * latents).reshape(tokens, latent_dim)
    features = time_features(timesteps)
    position = lax.axis_index("seq") * frames + jnp.arange(frames)
    live_mask = position[None, :] < lengths[:, None]
    half_dim = HEAD_DIM // 2
    inverse = 10000.0 ** (-jnp.arange(half_dim, dtype=jnp.float32) / half_dim)
    angles = position.astype(jnp.float32)[:, None] * inverse[None, :]
    cosine = jnp.cos(angles)[None, :, None, :]
    sine_table = jnp.sin(angles)[None, :, None, :]
    predicted, saved = layer_forward(
        weights, noisy_input, features, context, lengths, cosine, sine_table
    )
    difference = predicted - target
    errors = jnp.sum(difference * difference, axis=1).reshape(item_count, frames)
    per_item = jnp.sum(jnp.where(live_mask, errors, 0.0), axis=1)
    partial_sums = jnp.dot(per_item, onehot, precision=HIGHEST)
    bucket_sums = lax.psum(partial_sums, ("seq", "fsdp"))
    frame_scale = jnp.where(live_mask, item_scale[:, None], 0.0).reshape(tokens, 1)
    grad_pred = (2.0 * difference * frame_scale).astype(low_type)
    local_grads, gate_up_grad, down_grad = layer_backward(
        weights, saved, grad_pred, context, lengths, cosine, sine_table, position
    )
    reduced = (
        lax.psum_scatter(local_grads[0], ("seq", "fsdp"), scatter_dimension=2, tiled=True),
        lax.psum_scatter(local_grads[1], ("seq", "fsdp"), scatter_dimension=2, tiled=True),
        lax.psum_scatter(local_grads[2], ("seq", "fsdp"), scatter_dimension=2, tiled=True),
        lax.psum_scatter(local_grads[3], ("seq", "fsdp"), scatter_dimension=1, tiled=True),
        lax.psum_scatter(local_grads[4], ("seq", "fsdp"), scatter_dimension=1, tiled=True),
    )
    everything = tuple(reduced) + (gate_up_grad, down_grad)
    squares = sum((jnp.sum(grad * grad) for grad in everything))
    squares = lax.psum(squares, ("seq", "fsdp"))
    loss_value = jnp.sum(bucket_sums * bucket_scale)
    clip_norm = jnp.sqrt(squares)
    factor = CLIP_AT / jnp.maximum(clip_norm, CLIP_AT)
    attention_moment_new = 0.95 * attention_moment + reduced[0] * factor
    cross_moment_new = 0.95 * cross_moment + reduced[1] * factor
    attention_orth, cross_orth = newton_schulz(attention_moment_new, cross_moment_new)
    attention_new = attention_weights * (1.0 - MUON_RATE * DECAY_RATE) - MUON_RATE * attention_orth
    cross_new = cross_weights * (1.0 - MUON_RATE * DECAY_RATE) - MUON_RATE * cross_orth
    gate_up_new, gate_up_first_new, gate_up_second_new = adam_update(
        gate_up_weights, gate_up_first, gate_up_second, gate_up_grad * factor, ADAM_RATE, DECAY_RATE
    )
    down_new, down_first_new, down_second_new = adam_update(
        down_weights, down_first, down_second, down_grad * factor, ADAM_RATE, DECAY_RATE
    )
    latent_new, latent_first_new, latent_second_new = adam_update(
        latent_weights, latent_first, latent_second, reduced[2] * factor, ADAM_RATE, DECAY_RATE
    )
    timing_new, timing_first_new, timing_second_new = adam_update(
        timing_weights, timing_first, timing_second, reduced[3] * factor, ADAM_RATE, DECAY_RATE
    )
    norm_new, norm_first_new, norm_second_new = adam_update(
        norm_params, norm_first, norm_second, reduced[4] * factor, GAIN_RATE, 0.0
    )
    return (
        loss_value,
        clip_norm,
        attention_new,
        attention_moment_new,
        attention_new.astype(low_type),
        cross_new,
        cross_moment_new,
        cross_new.astype(low_type),
        gate_up_new,
        gate_up_first_new,
        gate_up_second_new,
        gate_up_new.astype(low_type),
        down_new,
        down_first_new,
        down_second_new,
        down_new.astype(low_type),
        latent_new,
        latent_first_new,
        latent_second_new,
        latent_new.astype(low_type),
        timing_new,
        timing_first_new,
        timing_second_new,
        timing_new.astype(low_type),
        norm_new,
        norm_first_new,
        norm_second_new,
    )


def general(mesh):
    return jax.shard_map(
        body,
        mesh=mesh,
        in_specs=(
            P("fsdp", "seq", None),
            P("fsdp", "seq", None),
            P("fsdp"),
            P("fsdp"),
            P("fsdp"),
            P("fsdp", None, None),
            P(None, None, ("seq", "fsdp")),
            P(None, None, ("seq", "fsdp")),
            P(None, None, ("seq", "fsdp")),
            P(None, None, ("seq", "fsdp")),
            P(("seq", "fsdp"), None),
            P(("seq", "fsdp"), None),
            P(("seq", "fsdp"), None),
            P(("seq", "fsdp"), None),
            P(("seq", "fsdp"), None),
            P(("seq", "fsdp"), None),
            P(None, None, ("seq", "fsdp")),
            P(None, None, ("seq", "fsdp")),
            P(None, None, ("seq", "fsdp")),
            P(None, ("seq", "fsdp")),
            P(None, ("seq", "fsdp")),
            P(None, ("seq", "fsdp")),
            P(None, ("seq", "fsdp")),
            P(None, ("seq", "fsdp")),
            P(None, ("seq", "fsdp")),
        ),
        out_specs=(
            P(),
            P(),
            P(None, None, ("seq", "fsdp")),
            P(None, None, ("seq", "fsdp")),
            P(None, None, ("seq", "fsdp")),
            P(None, None, ("seq", "fsdp")),
            P(None, None, ("seq", "fsdp")),
            P(None, None, ("seq", "fsdp")),
            P(("seq", "fsdp"), None),
            P(("seq", "fsdp"), None),
            P(("seq", "fsdp"), None),
            P(("seq", "fsdp"), None),
            P(("seq", "fsdp"), None),
            P(("seq", "fsdp"), None),
            P(("seq", "fsdp"), None),
            P(("seq", "fsdp"), None),
            P(None, None, ("seq", "fsdp")),
            P(None, None, ("seq", "fsdp")),
            P(None, None, ("seq", "fsdp")),
            P(None, None, ("seq", "fsdp")),
            P(None, ("seq", "fsdp")),
            P(None, ("seq", "fsdp")),
            P(None, ("seq", "fsdp")),
            P(None, ("seq", "fsdp")),
            P(None, ("seq", "fsdp")),
            P(None, ("seq", "fsdp")),
            P(None, ("seq", "fsdp")),
        ),
        check_vma=False,
    )


LAYER = ("y", "f")
ALL = ("z", "y", "f")
RANKS = 8
LOCAL_HEADS = HEADS // RANKS
COLS = LOCAL_HEADS * HEAD_DIM
LOW = jnp.bfloat16


def attend_kernel(lengths_ref, q_ref, k_ref, v_ref, o_ref, lse_ref):
    frames = q_ref.shape[1]
    length = lengths_ref[pl.program_id(0) // LOCAL_HEADS]
    keys = k_ref[0]
    values = v_ref[0]
    chunk = 256
    live = lax.broadcasted_iota(jnp.int32, (chunk, frames), 1) < length
    for part in range(frames // chunk):
        rows = pl.ds(part * chunk, chunk)
        scores = lax.dot_general(
            q_ref[0, rows, :], keys, (((1,), (1,)), ((), ())), preferred_element_type=jnp.float32
        ) * (1.0 / math.sqrt(HEAD_DIM))
        scores = jnp.where(live, scores, -1e30)
        top = jnp.max(scores, axis=1, keepdims=True)
        grown = jnp.exp(scores - top)
        total = jnp.sum(grown, axis=1, keepdims=True)
        weights = (grown * (1.0 / total)).astype(LOW)
        o_ref[0, rows, :] = jnp.dot(weights, values, preferred_element_type=jnp.float32)
        lse_ref[0, rows, :] = top + jnp.log(total)


def attend(queries, key_rows, values, lengths):
    count, frames, width = queries.shape
    block = pl.BlockSpec((1, frames, width), lambda i: (i, 0, 0))
    return pl.pallas_call(
        attend_kernel,
        grid=(count,),
        out_shape=(
            jax.ShapeDtypeStruct((count, frames, width), jnp.float32),
            jax.ShapeDtypeStruct((count, frames, 1), jnp.float32),
        ),
        in_specs=[pl.BlockSpec(memory_space=pltpu.SMEM), block, block, block],
        out_specs=(block, pl.BlockSpec((1, frames, 1), lambda i: (i, 0, 0))),
        compiler_params=pltpu.CompilerParams(vmem_limit_bytes=48 << 20),
        cost_estimate=pl.CostEstimate(
            flops=4 * count * frames * frames * width,
            bytes_accessed=10 * count * frames * width,
            transcendentals=count * frames * frames,
        ),
    )(lengths, queries, key_rows, values)


def attend_back_kernel(
    lengths_ref, q_ref, k_ref, v_ref, o_ref, lse_ref, do_ref, dq_ref, dk_ref, dv_ref
):
    frames = q_ref.shape[1]
    length = lengths_ref[pl.program_id(0) // LOCAL_HEADS]
    keys = k_ref[0]
    values = v_ref[0]
    chunk = 256
    scale = 1.0 / math.sqrt(HEAD_DIM)
    live = lax.broadcasted_iota(jnp.int32, (chunk, frames), 1) < length
    grad_key = jnp.zeros((frames, HEAD_DIM), jnp.float32)
    grad_value = jnp.zeros((frames, HEAD_DIM), jnp.float32)
    for part in range(frames // chunk):
        rows = pl.ds(part * chunk, chunk)
        queries = q_ref[0, rows, :]
        grads = do_ref[0, rows, :]
        scores = (
            lax.dot_general(
                queries, keys, (((1,), (1,)), ((), ())), preferred_element_type=jnp.float32
            )
            * scale
        )
        scores = jnp.where(live, scores, -1e30)
        weights = jnp.exp(scores - lse_ref[0, rows, :])
        delta = jnp.sum(grads.astype(jnp.float32) * o_ref[0, rows, :], axis=1, keepdims=True)
        pulled = lax.dot_general(
            grads, values, (((1,), (1,)), ((), ())), preferred_element_type=jnp.float32
        )
        pushed = (weights * (pulled - delta)).astype(LOW)
        dq_ref[0, rows, :] = jnp.dot(pushed, keys, preferred_element_type=jnp.float32) * scale
        grad_key = grad_key + rows_product(pushed, queries)
        grad_value = grad_value + rows_product(weights.astype(LOW), grads)
    dk_ref[0] = grad_key * scale
    dv_ref[0] = grad_value


def attend_back(queries, key_rows, values, mixed, log_total, grads, lengths):
    count, frames, width = queries.shape
    block = pl.BlockSpec((1, frames, width), lambda i: (i, 0, 0))
    shape = jax.ShapeDtypeStruct((count, frames, width), jnp.float32)
    return pl.pallas_call(
        attend_back_kernel,
        grid=(count,),
        out_shape=(shape,) * 3,
        in_specs=[
            pl.BlockSpec(memory_space=pltpu.SMEM),
            block,
            block,
            block,
            block,
            pl.BlockSpec((1, frames, 1), lambda i: (i, 0, 0)),
            block,
        ],
        out_specs=(block,) * 3,
        compiler_params=pltpu.CompilerParams(vmem_limit_bytes=48 << 20),
        cost_estimate=pl.CostEstimate(
            flops=10 * count * frames * frames * width,
            bytes_accessed=24 * count * frames * width,
            transcendentals=count * frames * frames,
        ),
    )(lengths, queries, key_rows, values, mixed, log_total, grads)


def cross_forward(cross_query, cross_key, cross_value):
    probs = jax.nn.softmax(scores_of(cross_query, cross_key), axis=-1)
    probs_low = probs.astype(LOW)
    out = jnp.einsum("bhqk,bkhd->bqhd", probs_low, cross_value, preferred_element_type=jnp.float32)
    return probs, probs_low, out


def newton_products(gram):
    trace = jnp.trace(gram, axis1=1, axis2=2)[:, None, None]
    norm_value = jnp.sqrt(trace) + 1e-07
    product = gram / (norm_value * norm_value)
    eye = jnp.eye(HEAD_DIM, dtype=jnp.float32)[None]

    def mul(left, right):
        return jnp.einsum("bij,bjk->bik", left, right, precision=HIGHEST)

    total = None
    for newton_step in range(5):
        mixer = NS_COEF[0] * eye + NS_COEF[1] * product + NS_COEF[2] * mul(product, product)
        total = mixer if total is None else mul(mixer, total)
        if newton_step < 4:
            product = mul(mul(mixer, product), mixer)
    return total / norm_value


def fast_body(
    latents,
    gaussian_noise,
    timesteps,
    lengths,
    buckets,
    context,
    attention_weights,
    attention_moment,
    cross_weights,
    cross_moment,
    gate_up_weights,
    gate_up_first,
    gate_up_second,
    down_weights,
    down_first,
    down_second,
    latent_weights,
    latent_first,
    latent_second,
    timing_weights,
    timing_first,
    timing_second,
    norm_params,
    norm_first,
    norm_second,
):
    f32 = jnp.float32
    planes = lax.axis_size("z")
    z_at = lax.axis_index("z")
    rank = lax.axis_index("y") * lax.axis_size("f") + lax.axis_index("f")
    item_count, span, latent_dim = latents.shape
    frames = span * RANKS
    tokens = item_count * span
    group_tokens = item_count * frames
    flip = lambda array: jnp.swapaxes(array, 1, 2)

    attention_t = flip(attention_weights)
    cross_t = flip(cross_weights)
    attention_low = attention_t.astype(LOW)
    cross_low_t = cross_t.astype(LOW)
    small_low = jnp.concatenate(
        [
            latent_weights.reshape(-1, latent_weights.shape[2]),
            timing_weights,
            norm_params,
        ],
        axis=0,
    ).astype(LOW)
    small_all = lax.all_gather(small_low, ALL, axis=1, tiled=True)
    latent_in = small_all[:LAT]
    latent_out = small_all[LAT : 2 * LAT]
    timing = small_all[2 * LAT : 2 * LAT + FOUR]
    norms = small_all[2 * LAT + FOUR :].astype(f32)

    meta = lax.all_gather(
        jnp.stack([timesteps, lengths.astype(f32), buckets.astype(f32)]), "f", axis=1, tiled=True
    )
    times_all = meta[0]
    lengths_all = meta[1]
    onehot_all = (meta[2][:, None] == jnp.arange(NBUCK, dtype=f32)[None, :]).astype(f32)
    counts = jnp.dot(lengths_all, onehot_all, precision=HIGHEST)
    present = jnp.sum((counts > 0).astype(f32))
    bucket_scale = 1.0 / (present * LAT * jnp.maximum(counts, 1.0))
    own_at = z_at * item_count
    onehot = lax.dynamic_slice_in_dim(onehot_all, own_at, item_count, 0)
    item_scale = jnp.dot(onehot, bucket_scale, precision=HIGHEST)
    own_lengths = lax.dynamic_slice_in_dim(lengths_all, own_at, item_count, 0).astype(jnp.int32)
    features_all = time_features(times_all).astype(LOW)
    features = lax.dynamic_slice_in_dim(features_all, own_at, item_count, 0)

    signal = jnp.cos(0.5 * math.pi * timesteps)[:, None, None]
    noise_level = jnp.sin(0.5 * math.pi * timesteps)[:, None, None]
    noisy_own = (signal * latents + noise_level * gaussian_noise).astype(LOW)
    target_own = signal * gaussian_noise - noise_level * latents
    noisy_all = lax.all_gather(noisy_own, ALL, axis=0, tiled=False)
    noisy_all = noisy_all.reshape(RANKS, planes, item_count, span, latent_dim)
    noisy_low = jnp.swapaxes(
        lax.dynamic_index_in_dim(noisy_all, z_at, 1, keepdims=False), 0, 1
    ).reshape(item_count, frames, latent_dim)
    target = lax.ppermute(
        target_own, ALL, [(4 * s + g, RANKS * g + s) for s in range(RANKS) for g in range(planes)]
    ).reshape(tokens, latent_dim)
    context_all = lax.all_gather(context, "f", axis=0, tiled=True)
    context_own = lax.dynamic_slice_in_dim(context_all, own_at, item_count, 0).reshape(-1, E)
    context_len = context.shape[1]

    qkv_slab = lax.all_to_all(attention_low[:3], LAYER, split_axis=2, concat_axis=1, tiled=True)
    qkv_t = lax.all_gather(qkv_slab, "z", axis=1, tiled=True)
    cross_slab = lax.all_to_all(cross_low_t, LAYER, split_axis=2, concat_axis=1, tiled=True)
    cross_w = lax.all_gather(cross_slab, "z", axis=1, tiled=True)
    rest_t = lax.all_gather(attention_low[3:], ALL, axis=1, tiled=True)
    gate_up = lax.all_gather(gate_up_weights.astype(LOW), "z", axis=0, tiled=True)
    down_pairs = []
    for p in range(planes):
        for r in range(RANKS):
            down_pairs.append((2 * RANKS * (p // 2) + 2 * r + p % 2, RANKS * p + r))
    down = lax.all_gather(
        lax.ppermute(down_weights.astype(LOW), ALL, down_pairs), "z", axis=0, tiled=True
    )

    half_dim = HEAD_DIM // 2
    inverse = 10000.0 ** (-jnp.arange(half_dim, dtype=f32) / half_dim)
    angles = jnp.arange(frames, dtype=f32)[:, None] * inverse[None, :]
    cosine = jnp.cos(angles)[None, None]
    sine_table = jnp.sin(angles)[None, None]

    timed = matmul_low(features, timing)
    start_all = (
        matmul_low(noisy_low.reshape(group_tokens, latent_dim), latent_in).reshape(
            item_count, frames, D
        )
        + timed[:, None, :]
    )
    start_own = lax.dynamic_slice_in_dim(start_all, rank * span, span, 1).reshape(tokens, D)
    noisy_mine = lax.dynamic_slice_in_dim(noisy_low, rank * span, span, 1).reshape(
        tokens, latent_dim
    )
    normed_one, back_one = jax.vjp(
        layer_norm, start_all.reshape(group_tokens, D), norms[0], norms[1]
    )
    normed_one = normed_one.astype(LOW)

    def heads_of(flat):
        return jnp.swapaxes(
            flat.reshape(item_count, frames, LOCAL_HEADS, HEAD_DIM), 1, 2
        )

    def packed(heads):
        return heads.reshape(item_count * LOCAL_HEADS, frames, HEAD_DIM)

    def flat_of(heads):
        return jnp.swapaxes(
            heads.reshape(item_count, LOCAL_HEADS, frames, HEAD_DIM), 1, 2
        ).reshape(group_tokens, COLS)

    queries = packed(
        rotate(heads_of(matmul_low(normed_one, qkv_t[0])), cosine, sine_table).astype(LOW)
    )
    key_rows = packed(
        rotate(heads_of(matmul_low(normed_one, qkv_t[1])), cosine, sine_table).astype(LOW)
    )
    values = packed(heads_of(matmul_low(normed_one, qkv_t[2])).astype(LOW))
    mixed, log_total = attend(queries, key_rows, values, own_lengths)

    def to_tokens(flat):
        moved = flat.reshape(item_count, RANKS, span, COLS)
        return lax.all_to_all(moved, LAYER, split_axis=1, concat_axis=3, tiled=True).reshape(
            tokens, D
        )

    def to_heads(flat):
        moved = flat.reshape(item_count, 1, span, D)
        return lax.all_to_all(moved, LAYER, split_axis=3, concat_axis=1, tiled=True).reshape(
            group_tokens, COLS
        )

    mixed_low = to_tokens(flat_of(mixed.astype(LOW)))
    after_self = start_own + matmul_low(mixed_low, rest_t[0])
    normed_two, back_two = jax.vjp(layer_norm, after_self, norms[2], norms[3])
    normed_two = normed_two.astype(LOW)
    cross_query = (
        matmul_low(normed_two, rest_t[1]).astype(LOW).reshape(item_count, span, HEADS, HEAD_DIM)
    )
    pair_own = jnp.stack(
        [matmul_low(context_own, cross_w[0]), matmul_low(context_own, cross_w[1])]
    ).astype(LOW)
    pair_all = lax.all_gather(pair_own, LAYER, axis=2, tiled=True).reshape(
        2, item_count, context_len, HEADS, HEAD_DIM
    )
    cross_key, cross_value = (pair_all[0], pair_all[1])
    probs, probs_low, cross_mixed = cross_forward(cross_query, cross_key, cross_value)
    cross_out = cross_mixed.reshape(tokens, D).astype(LOW)
    after_cross = after_self + matmul_low(cross_out, rest_t[2])
    normed_three, back_three = jax.vjp(layer_norm, after_cross, norms[4], norms[5])
    normed_three = normed_three.astype(LOW)
    normed_group = lax.all_gather(normed_three, LAYER, axis=0, tiled=True)
    gate_both = times_transposed(normed_group, gate_up)
    units = gate_both.shape[1] // 2
    gate_half, up_half = (gate_both[:, :units], gate_both[:, units:])
    inner_act = (jax.nn.silu(gate_half) * up_half).astype(LOW)
    final_state = (
        after_cross
        + lax.psum_scatter(matmul_low(inner_act, down), LAYER, scatter_dimension=0, tiled=True)
    ).astype(LOW)
    predicted = times_transposed(final_state, latent_out)

    position = rank * span + jnp.arange(span)
    live_mask = position[None, :] < own_lengths[:, None]
    difference = predicted - target
    errors = jnp.sum(difference * difference, axis=1).reshape(item_count, span)
    per_item = jnp.sum(jnp.where(live_mask, errors, 0.0), axis=1)
    partial_loss = jnp.sum(per_item * item_scale)
    frame_scale = jnp.where(live_mask, item_scale[:, None], 0.0).reshape(tokens, 1)
    grad_pred = (2.0 * difference * frame_scale).astype(LOW)

    grad_out_proj = rows_product(grad_pred, final_state)
    grad_state = matmul_low(grad_pred, latent_out)
    grad_group = lax.all_gather(grad_state.astype(LOW), LAYER, axis=0, tiled=True)
    down_slab = lax.psum_scatter(
        rows_product(inner_act, grad_group), "z", scatter_dimension=0, tiled=True
    )
    down_grad = lax.ppermute(down_slab, ALL, [(b, a) for a, b in down_pairs])
    grad_inner = times_transposed(grad_group, down)
    sigmoid_gate = jax.nn.sigmoid(gate_half)
    grad_gate = grad_inner * up_half * sigmoid_gate * (1.0 + gate_half * (1.0 - sigmoid_gate))
    grad_both = jnp.concatenate([grad_gate, grad_inner * gate_half * sigmoid_gate], axis=1).astype(
        LOW
    )
    gate_up_grad = lax.psum_scatter(
        rows_product(grad_both, normed_group), "z", scatter_dimension=0, tiled=True
    )
    grad_three = lax.psum_scatter(
        matmul_low(grad_both, gate_up), LAYER, scatter_dimension=0, tiled=True
    )
    residual_part, gain_three, shift_three = back_three(grad_three)
    grad_state = grad_state + residual_part
    grad_branch = grad_state.astype(LOW)
    grad_cross_out = rows_product(cross_out, grad_branch)
    grad_mix = (
        times_transposed(grad_branch, rest_t[2])
        .astype(LOW)
        .reshape(item_count, span, HEADS, HEAD_DIM)
    )
    grad_scores = jnp.einsum("bqhd,bkhd->bhqk", grad_mix, cross_value, preferred_element_type=f32)
    grad_cross_value = jnp.einsum(
        "bhqk,bqhd->bkhd", probs_low, grad_mix, preferred_element_type=f32
    )
    pushed = (probs * (grad_scores - jnp.sum(probs * grad_scores, axis=-1, keepdims=True))).astype(
        LOW
    )
    score_scale = math.sqrt(HEAD_DIM)
    grad_cross_query = (
        (jnp.einsum("bhqk,bkhd->bqhd", pushed, cross_key, preferred_element_type=f32) / score_scale)
        .astype(LOW)
        .reshape(tokens, D)
    )
    grad_cross_key = (
        jnp.einsum("bhqk,bqhd->bkhd", pushed, cross_query, preferred_element_type=f32) / score_scale
    )
    grad_pair = jnp.stack([grad_cross_key, grad_cross_value]).reshape(
        2, item_count * context_len, D
    )
    grad_pair = lax.psum_scatter(grad_pair, LAYER, scatter_dimension=2, tiled=True)
    grad_cross_w = jnp.einsum(
        "te,ptc->pec", context_own.astype(f32), grad_pair, precision=HIGHEST
    )
    grad_cross_w = lax.psum_scatter(grad_cross_w, "z", scatter_dimension=1, tiled=True)
    cross_grad = lax.all_to_all(grad_cross_w, LAYER, split_axis=1, concat_axis=2, tiled=True)
    grad_cross_q = rows_product(normed_two, grad_cross_query)
    residual_part, gain_two, shift_two = back_two(times_transposed(grad_cross_query, rest_t[1]))
    grad_state = grad_state + residual_part
    grad_branch = grad_state.astype(LOW)
    grad_self_out = rows_product(mixed_low, grad_branch)
    grad_mixed = times_transposed(grad_branch, rest_t[0]).astype(LOW)
    rest_grad = lax.psum_scatter(
        jnp.stack([grad_self_out, grad_cross_q, grad_cross_out]),
        ALL,
        scatter_dimension=1,
        tiled=True,
    )
    grad_mixed = packed(heads_of(to_heads(grad_mixed)))
    grad_query, grad_key, grad_value = attend_back(
        queries, key_rows, values, mixed, log_total, grad_mixed, own_lengths
    )
    unpacked = lambda heads: heads.reshape(item_count, LOCAL_HEADS, frames, HEAD_DIM)
    grad_triple = [
        flat_of(rotate(unpacked(grad_query), cosine, -sine_table).astype(LOW)),
        flat_of(rotate(unpacked(grad_key), cosine, -sine_table).astype(LOW)),
        flat_of(grad_value.astype(LOW)),
    ]
    qkv_grad = jnp.stack([rows_product(normed_one, part) for part in grad_triple])
    qkv_grad = lax.psum_scatter(qkv_grad, "z", scatter_dimension=1, tiled=True)
    qkv_grad = lax.all_to_all(qkv_grad, LAYER, split_axis=1, concat_axis=2, tiled=True)
    grad_one = sum(times_transposed(part, qkv_t[i]) for i, part in enumerate(grad_triple))
    residual_part, gain_one, shift_one = back_one(grad_one)
    grad_in_proj = rows_precise(
        noisy_low.reshape(group_tokens, latent_dim).astype(f32), residual_part
    ) + rows_precise(noisy_mine.astype(f32), grad_state)
    grad_timed = jnp.sum(residual_part.reshape(item_count, frames, D), axis=1) + jnp.sum(
        grad_state.reshape(item_count, span, D), axis=1
    )
    timed_slots = lax.dynamic_update_slice(
        jnp.zeros((item_count * planes, D), f32), grad_timed, (own_at, 0)
    )
    small_grad = jnp.concatenate(
        [
            grad_in_proj,
            grad_out_proj,
            jnp.stack([gain_one, shift_one, gain_two, shift_two, gain_three, shift_three]),
            timed_slots,
        ],
        axis=0,
    )
    small_grad = lax.psum_scatter(small_grad, ALL, scatter_dimension=1, tiled=True)
    latent_grad = small_grad[: 2 * LAT].reshape(2, LAT, -1)
    norm_grad = small_grad[2 * LAT : 2 * LAT + 6]
    timing_grad = rows_precise(features_all.astype(f32), small_grad[2 * LAT + 6 :])
    attention_grad = jnp.concatenate([qkv_grad, rest_grad], axis=0)

    everything = (
        attention_grad,
        cross_grad,
        latent_grad,
        timing_grad,
        norm_grad,
        gate_up_grad,
        down_grad,
    )
    squares = sum((jnp.sum(grad * grad) for grad in everything))
    squares, loss_value = lax.psum((squares, partial_loss), ALL)
    clip_norm = jnp.sqrt(squares)
    factor = CLIP_AT / jnp.maximum(clip_norm, CLIP_AT)

    moment_t = 0.95 * flip(attention_moment) + attention_grad * factor
    cross_moment_t = 0.95 * flip(cross_moment) + cross_grad * factor
    blocks = [
        moment.reshape(moment.shape[0], moment.shape[1], D // HEAD_DIM, HEAD_DIM)
        for moment in (moment_t, cross_moment_t)
    ]
    grams = jnp.concatenate(
        [
            jnp.einsum("skbi,skbj->sbij", block, block, precision=HIGHEST).reshape(
                -1, HEAD_DIM, HEAD_DIM
            )
            for block in blocks
        ]
    )
    mixers = newton_products(lax.psum_scatter(grams, ALL, scatter_dimension=0, tiled=True))
    mixers = lax.all_gather(mixers, ALL, axis=0, tiled=True).reshape(
        -1, D // HEAD_DIM, HEAD_DIM, HEAD_DIM
    )
    stacks = attention_t.shape[0]
    orth = [
        jnp.einsum("skbj,sbji->skbi", block, mixer, precision=HIGHEST).reshape(moment.shape)
        for block, mixer, moment in zip(
            blocks, (mixers[:stacks], mixers[stacks:]), (moment_t, cross_moment_t)
        )
    ]
    attention_new = attention_t * (1.0 - MUON_RATE * DECAY_RATE) - MUON_RATE * orth[0]
    cross_new = cross_t * (1.0 - MUON_RATE * DECAY_RATE) - MUON_RATE * orth[1]
    gate_up_new, gate_up_first_new, gate_up_second_new = adam_update(
        gate_up_weights, gate_up_first, gate_up_second, gate_up_grad * factor, ADAM_RATE, DECAY_RATE
    )
    down_new, down_first_new, down_second_new = adam_update(
        down_weights, down_first, down_second, down_grad * factor, ADAM_RATE, DECAY_RATE
    )
    latent_new, latent_first_new, latent_second_new = adam_update(
        latent_weights, latent_first, latent_second, latent_grad * factor, ADAM_RATE, DECAY_RATE
    )
    timing_new, timing_first_new, timing_second_new = adam_update(
        timing_weights, timing_first, timing_second, timing_grad * factor, ADAM_RATE, DECAY_RATE
    )
    norm_new, norm_first_new, norm_second_new = adam_update(
        norm_params, norm_first, norm_second, norm_grad * factor, GAIN_RATE, 0.0
    )
    return (
        loss_value,
        clip_norm,
        flip(attention_new),
        flip(moment_t),
        flip(attention_new.astype(LOW)),
        flip(cross_new),
        flip(cross_moment_t),
        flip(cross_new.astype(LOW)),
        gate_up_new,
        gate_up_first_new,
        gate_up_second_new,
        gate_up_new.astype(LOW),
        down_new,
        down_first_new,
        down_second_new,
        down_new.astype(LOW),
        latent_new,
        latent_first_new,
        latent_second_new,
        latent_new.astype(LOW),
        timing_new,
        timing_first_new,
        timing_second_new,
        timing_new.astype(LOW),
        norm_new,
        norm_first_new,
        norm_second_new,
    )


def solution(mesh):
    if tuple(mesh.devices.shape) != (RANKS, 4):
        return general(mesh)
    mesh3 = jax.sharding.Mesh(mesh.devices.reshape(4, 2, 4), ALL)
    seq = ("z", "y")
    row = P(ALL, None)
    col2 = P(None, ALL)
    col3 = P(None, None, ALL)
    return jax.shard_map(
        fast_body,
        mesh=mesh3,
        in_specs=(P("f", seq, None),) * 2
        + (P("f"),) * 3
        + (P("f", None, None),)
        + (col3,) * 4
        + (row,) * 6
        + (col3,) * 3
        + (col2,) * 6,
        out_specs=(P(),) * 2 + (col3,) * 6 + (row,) * 8 + (col3,) * 4 + (col2,) * 7,
        check_vma=False,
    )
```

```python
import math

import jax
import jax.numpy as jnp
from jax import lax
from jax.experimental import pallas as pl
from jax.experimental.pallas import tpu as pltpu
from jax.sharding import PartitionSpec as P

D = 1536
HEADS = 24
HEAD_DIM = 64
FF = 6144
E = 768
LAT = 64
FOUR = 256
NBUCK = 4
STEP = 10


HIGHEST = lax.Precision.HIGHEST
NS_COEF = (3.4445, -4.775, 2.0315)
CLIP_AT = 0.01
MUON_RATE = 0.5
ADAM_RATE = 0.02
GAIN_RATE = 0.2
DECAY_RATE = 0.01


def times_transposed(left, weight):
    return lax.dot_general(
        left, weight, (((left.ndim - 1,), (1,)), ((), ())), preferred_element_type=jnp.float32
    )


def matmul_low(left, right):
    return jnp.dot(left, right, preferred_element_type=jnp.float32)


def rows_product(left, right):
    return lax.dot_general(
        left, right, (((0,), (0,)), ((), ())), preferred_element_type=jnp.float32
    )


def rows_precise(left, right):
    return lax.dot_general(left, right, (((0,), (0,)), ((), ())), precision=HIGHEST)


def layer_norm(hidden, gain, shift):
    centred = hidden - jnp.mean(hidden, axis=-1, keepdims=True)
    spread = jnp.mean(centred * centred, axis=-1, keepdims=True)
    return centred * lax.rsqrt(spread + 1e-05) * gain + shift


def rotate(values, cosine, sine_table):
    half_dim = values.shape[-1] // 2
    first = values[..., :half_dim]
    second = values[..., half_dim:]
    return jnp.concatenate(
        [first * cosine - second * sine_table, second * cosine + first * sine_table], axis=-1
    )


def time_features(timesteps):
    count = FOUR // 2
    freqs = jnp.exp(jnp.arange(count, dtype=jnp.float32) * (math.log(100.0) / max(count - 1, 1)))
    phases = 2.0 * math.pi * timesteps[:, None] * freqs[None, :]
    return jnp.concatenate([jnp.cos(phases), jnp.sin(phases)], axis=1)


def split_heads(values):
    return values.reshape(values.shape[0], values.shape[1], HEADS, HEAD_DIM)


def scores_of(queries, key_rows):
    return jnp.einsum(
        "bqhd,bkhd->bhqk", queries, key_rows, preferred_element_type=jnp.float32
    ) / math.sqrt(HEAD_DIM)


def masked_scores(queries, key_rows, lengths):
    key_live = jnp.arange(key_rows.shape[1])[None, :] < lengths[:, None]
    return jnp.where(key_live[:, None, None, :], scores_of(queries, key_rows), -1e30)


def attention_forward(queries, key_low, value_low, lengths):
    item_count, frames = (queries.shape[0], queries.shape[1])
    running_top = jnp.full((item_count, HEADS, frames), -1e29, jnp.float32)
    scores = masked_scores(
        queries, split_heads(lax.all_gather(key_low, "seq", axis=1, tiled=True)), lengths
    )
    new_top = jnp.maximum(running_top, jnp.max(scores, axis=-1))
    running_sum = jnp.sum(jnp.exp(scores - new_top[..., None]), axis=-1)
    running_top, running_sum = (new_top, running_sum)
    log_total = running_top + jnp.log(running_sum)
    scores = masked_scores(
        queries, split_heads(lax.all_gather(key_low, "seq", axis=1, tiled=True)), lengths
    )
    weights = jnp.exp(scores - log_total[..., None]).astype(jnp.bfloat16)
    mixed = jnp.einsum(
        "bhqk,bkhd->bqhd",
        weights,
        split_heads(lax.all_gather(value_low, "seq", axis=1, tiled=True)),
        preferred_element_type=jnp.float32,
    )
    return (mixed, log_total)


def attention_backward(
    queries, key_low, value_low, grad_out, log_total, row_delta, lengths, position
):
    key_heads = split_heads(key_low)
    value_heads = split_heads(value_low)
    local_live = (position[None, :] < lengths[:, None])[:, None, None, :]
    query_flat = queries.reshape(key_low.shape).astype(jnp.float32)
    grad_flat = grad_out.reshape(key_low.shape).astype(jnp.float32)
    total_flat = jnp.transpose(log_total, (0, 2, 1))
    pieces = (
        lax.all_gather(query_flat.astype(jnp.bfloat16), "seq", axis=1, tiled=True).astype(
            jnp.float32
        ),
        lax.all_gather(grad_flat.astype(jnp.bfloat16), "seq", axis=1, tiled=True).astype(
            jnp.float32
        ),
        lax.all_gather(total_flat.astype(jnp.bfloat16), "seq", axis=1, tiled=True).astype(
            jnp.float32
        ),
        lax.all_gather(row_delta.astype(jnp.bfloat16), "seq", axis=1, tiled=True).astype(
            jnp.float32
        ),
    )
    query_rows = split_heads(pieces[0].astype(jnp.bfloat16))
    grad_rows = split_heads(pieces[1].astype(jnp.bfloat16))
    total_rows = jnp.transpose(pieces[2], (0, 2, 1))[..., None]
    delta_rows = jnp.transpose(pieces[3], (0, 2, 1))[..., None]
    scores = jnp.where(local_live, scores_of(query_rows, key_heads), -1e30)
    weights = jnp.exp(scores - total_rows)
    grad_value = jnp.einsum(
        "bhqk,bqhd->bkhd",
        weights.astype(jnp.bfloat16),
        grad_rows,
        preferred_element_type=jnp.float32,
    )
    grad_scores = jnp.einsum(
        "bqhd,bkhd->bhqk", grad_rows, value_heads, preferred_element_type=jnp.float32
    )
    pushed = (weights * (grad_scores - delta_rows)).astype(jnp.bfloat16)
    grad_key = jnp.einsum("bhqk,bqhd->bkhd", pushed, query_rows, preferred_element_type=jnp.float32)
    grad_key, grad_value = (grad_key, grad_value)
    delta_heads = jnp.transpose(row_delta, (0, 2, 1))[..., None]
    pieces = (
        lax.all_gather(key_low, "seq", axis=1, tiled=True),
        lax.all_gather(value_low, "seq", axis=1, tiled=True),
    )
    key_rows = split_heads(pieces[0])
    scores = masked_scores(queries, key_rows, lengths)
    weights = jnp.exp(scores - log_total[..., None])
    grad_scores = jnp.einsum(
        "bqhd,bkhd->bhqk", grad_out, split_heads(pieces[1]), preferred_element_type=jnp.float32
    )
    pushed = (weights * (grad_scores - delta_heads)).astype(jnp.bfloat16)
    grad_query = jnp.einsum("bhqk,bkhd->bqhd", pushed, key_rows, preferred_element_type=jnp.float32)
    score_scale = math.sqrt(HEAD_DIM)
    return (grad_query / score_scale, grad_key / score_scale, grad_value)


def layer_forward(weights, noisy_input, features, context, lengths, cosine, sine_table):
    attention, cross, gate_up, down, latent, timing, norms = weights
    norms = norms.astype(jnp.float32)
    item_count, frames, latent_dim = noisy_input.shape
    tokens = item_count * frames
    noisy_low = noisy_input.reshape(tokens, latent_dim).astype(jnp.bfloat16)
    feat_low = features.astype(jnp.bfloat16)
    timed = matmul_low(feat_low, timing)
    start_state = (
        matmul_low(noisy_low, latent[0]).reshape(item_count, frames, D) + timed[:, None, :]
    ).reshape(tokens, D)
    normed_one, back_one = jax.vjp(layer_norm, start_state, norms[0], norms[1])
    normed_one = normed_one.astype(jnp.bfloat16)
    triple = times_transposed(normed_one, attention[:3].reshape(3 * D, D)).reshape(
        item_count, frames, 3, HEADS, HEAD_DIM
    )
    queries = rotate(triple[:, :, 0], cosine, sine_table).astype(jnp.bfloat16)
    key_low = (
        rotate(triple[:, :, 1], cosine, sine_table)
        .astype(jnp.bfloat16)
        .reshape(item_count, frames, D)
    )
    value_low = triple[:, :, 2].astype(jnp.bfloat16).reshape(item_count, frames, D)
    mixed, log_total = attention_forward(queries, key_low, value_low, lengths)
    mixed_low = mixed.reshape(tokens, D).astype(jnp.bfloat16)
    after_self = start_state + times_transposed(mixed_low, attention[3])
    normed_two, back_two = jax.vjp(layer_norm, after_self, norms[2], norms[3])
    normed_two = normed_two.astype(jnp.bfloat16)
    cross_query = (
        times_transposed(normed_two, attention[4])
        .astype(jnp.bfloat16)
        .reshape(item_count, frames, HEADS, HEAD_DIM)
    )
    context_len = context.shape[1]
    cross_pair = times_transposed(
        context.reshape(item_count * context_len, E), cross.reshape(2 * D, E)
    ).astype(jnp.bfloat16)
    cross_pair = cross_pair.reshape(item_count, context_len, 2, HEADS, HEAD_DIM)
    cross_key, cross_value = (cross_pair[:, :, 0], cross_pair[:, :, 1])
    cross_weights = jax.nn.softmax(scores_of(cross_query, cross_key), axis=-1)
    cross_low = cross_weights.astype(jnp.bfloat16)
    cross_out = (
        jnp.einsum("bhqk,bkhd->bqhd", cross_low, cross_value, preferred_element_type=jnp.float32)
        .reshape(tokens, D)
        .astype(jnp.bfloat16)
    )
    after_cross = after_self + times_transposed(cross_out, attention[5])
    normed_three, back_three = jax.vjp(layer_norm, after_cross, norms[4], norms[5])
    normed_three = normed_three.astype(jnp.bfloat16)
    gate_both = times_transposed(normed_three, gate_up)
    gate_half, up_half = (gate_both[:, :FF], gate_both[:, FF:])
    inner_act = (jax.nn.silu(gate_half) * up_half).astype(jnp.bfloat16)
    final_state = (after_cross + matmul_low(inner_act, down)).astype(jnp.bfloat16)
    predicted = times_transposed(final_state, latent[1])
    saved = (
        noisy_low,
        feat_low,
        back_one,
        normed_one,
        queries,
        key_low,
        value_low,
        mixed,
        log_total,
        mixed_low,
        back_two,
        normed_two,
        cross_query,
        cross_key,
        cross_value,
        cross_weights,
        cross_low,
        cross_out,
        back_three,
        normed_three,
        gate_half,
        up_half,
        inner_act,
        final_state,
    )
    return (predicted, saved)


def layer_backward(weights, saved, grad_pred, context, lengths, cosine, sine_table, position):
    attention, cross, gate_up, down, latent, timing, norms = weights
    (
        noisy_low,
        feat_low,
        back_one,
        normed_one,
        queries,
        key_low,
        value_low,
        mixed,
        log_total,
        mixed_low,
        back_two,
        normed_two,
        cross_query,
        cross_key,
        cross_value,
        cross_weights,
        cross_low,
        cross_out,
        back_three,
        normed_three,
        gate_half,
        up_half,
        inner_act,
        final_state,
    ) = saved
    item_count, frames = (queries.shape[0], queries.shape[1])
    tokens = item_count * frames
    grad_out_proj = rows_product(grad_pred, final_state)
    grad_state = matmul_low(grad_pred, latent[1])
    grad_branch = grad_state.astype(jnp.bfloat16)
    down_reduced = lax.psum_scatter(
        rows_product(inner_act, grad_branch), ("seq", "fsdp"), scatter_dimension=0, tiled=True
    )
    grad_inner = times_transposed(grad_branch, down)
    sigmoid_gate = jax.nn.sigmoid(gate_half)
    grad_gate = grad_inner * up_half * sigmoid_gate * (1.0 + gate_half * (1.0 - sigmoid_gate))
    grad_both = jnp.concatenate([grad_gate, grad_inner * gate_half * sigmoid_gate], axis=1).astype(
        jnp.bfloat16
    )
    gate_up_reduced = lax.psum_scatter(
        rows_product(grad_both, normed_three), ("seq", "fsdp"), scatter_dimension=0, tiled=True
    )
    residual_part, gain_three, shift_three = back_three(matmul_low(grad_both, gate_up))
    grad_state = grad_state + residual_part
    grad_branch = grad_state.astype(jnp.bfloat16)
    grad_cross_out = rows_product(grad_branch, cross_out)
    grad_mix = (
        matmul_low(grad_branch, attention[5])
        .astype(jnp.bfloat16)
        .reshape(item_count, frames, HEADS, HEAD_DIM)
    )
    grad_scores = jnp.einsum(
        "bqhd,bkhd->bhqk", grad_mix, cross_value, preferred_element_type=jnp.float32
    )
    grad_cross_value = jnp.einsum(
        "bhqk,bqhd->bkhd", cross_low, grad_mix, preferred_element_type=jnp.float32
    )
    pushed = (
        cross_weights * (grad_scores - jnp.sum(cross_weights * grad_scores, axis=-1, keepdims=True))
    ).astype(jnp.bfloat16)
    score_scale = math.sqrt(HEAD_DIM)
    grad_cross_query = (
        (
            jnp.einsum("bhqk,bkhd->bqhd", pushed, cross_key, preferred_element_type=jnp.float32)
            / score_scale
        )
        .astype(jnp.bfloat16)
        .reshape(tokens, D)
    )
    grad_cross_key = (
        jnp.einsum("bhqk,bqhd->bkhd", pushed, cross_query, preferred_element_type=jnp.float32)
        / score_scale
    )
    context_len = context.shape[1]
    grad_pair = jnp.stack([grad_cross_key, grad_cross_value], axis=2).reshape(
        item_count * context_len, 2 * D
    )
    grad_cross = rows_precise(
        grad_pair, context.reshape(item_count * context_len, E).astype(jnp.float32)
    ).reshape(2, D, E)
    grad_cross_q = rows_product(grad_cross_query, normed_two)
    residual_part, gain_two, shift_two = back_two(matmul_low(grad_cross_query, attention[4]))
    grad_state = grad_state + residual_part
    grad_branch = grad_state.astype(jnp.bfloat16)
    grad_self_out = rows_product(grad_branch, mixed_low)
    grad_mixed = (
        matmul_low(grad_branch, attention[3])
        .astype(jnp.bfloat16)
        .reshape(item_count, frames, HEADS, HEAD_DIM)
    )
    row_delta = jnp.sum(grad_mixed.astype(jnp.float32) * mixed, axis=-1)
    grad_query, grad_key, grad_value = attention_backward(
        queries, key_low, value_low, grad_mixed, log_total, row_delta, lengths, position
    )
    grad_query = rotate(grad_query, cosine, -sine_table)
    grad_key = rotate(grad_key, cosine, -sine_table)
    grad_triple = (
        jnp.stack([grad_query, grad_key, grad_value], axis=2)
        .astype(jnp.bfloat16)
        .reshape(tokens, 3 * D)
    )
    grad_qkv = rows_product(grad_triple, normed_one).reshape(3, D, D)
    residual_part, gain_one, shift_one = back_one(
        matmul_low(grad_triple, attention[:3].reshape(3 * D, D))
    )
    grad_state = grad_state + residual_part
    grad_in_proj = rows_product(noisy_low, grad_state.astype(jnp.bfloat16))
    grad_timed = jnp.sum(grad_state.reshape(item_count, frames, D), axis=1)
    grad_timing = rows_precise(feat_low.astype(jnp.float32), grad_timed)
    grad_attention = jnp.concatenate(
        [grad_qkv, jnp.stack([grad_self_out, grad_cross_q, grad_cross_out])], axis=0
    )
    grad_latent = jnp.stack([grad_in_proj, grad_out_proj])
    grad_norms = jnp.stack([gain_one, shift_one, gain_two, shift_two, gain_three, shift_three])
    return (
        (grad_attention, grad_cross, grad_latent, grad_timing, grad_norms),
        gate_up_reduced,
        down_reduced,
    )


def gram_of(blocks):
    return jnp.einsum("sbik,sbjk->sbij", blocks, blocks, precision=HIGHEST)


def gram_sum(first, second):
    return lax.psum((gram_of(first), gram_of(second)), ("seq", "fsdp"))


def newton_schulz(first_moment, second_moment):
    moments = (first_moment, second_moment)
    blocks = [
        moment.reshape(moment.shape[0], moment.shape[1] // HEAD_DIM, HEAD_DIM, moment.shape[2])
        for moment in moments
    ]
    gram_list = gram_sum(blocks[0], blocks[1])
    block_norm = [
        jnp.sqrt(jnp.trace(gram, axis1=2, axis2=3))[..., None, None] + 1e-07 for gram in gram_list
    ]
    current = [block / norm_value for block, norm_value in zip(blocks, block_norm)]
    products = [gram / (norm_value * norm_value) for gram, norm_value in zip(gram_list, block_norm)]
    for newton_step in range(5):
        if newton_step > 0:
            products = gram_sum(current[0], current[1])
        updated = []
        for block, product in zip(current, products):
            squared = jnp.einsum("sbij,sbjk->sbik", product, product, precision=HIGHEST)
            mixer = NS_COEF[1] * product + NS_COEF[2] * squared
            updated.append(
                NS_COEF[0] * block + jnp.einsum("sbij,sbjk->sbik", mixer, block, precision=HIGHEST)
            )
        current = updated
    return [block.reshape(moment.shape) for block, moment in zip(current, moments)]


def adam_update(weight, first, second, grad, rate, decay):
    first_new = 0.9 * first + 0.1 * grad
    second_new = 0.95 * second + 0.05 * grad * grad
    first_hat = first_new / (1.0 - 0.9**STEP)
    second_hat = second_new / (1.0 - 0.95**STEP)
    weight_new = weight - rate * (first_hat / (jnp.sqrt(second_hat) + 1e-08) + decay * weight)
    return (weight_new, first_new, second_new)


def body(
    latents,
    gaussian_noise,
    timesteps,
    lengths,
    buckets,
    context,
    attention_weights,
    attention_moment,
    cross_weights,
    cross_moment,
    gate_up_weights,
    gate_up_first,
    gate_up_second,
    down_weights,
    down_first,
    down_second,
    latent_weights,
    latent_first,
    latent_second,
    timing_weights,
    timing_first,
    timing_second,
    norm_params,
    norm_first,
    norm_second,
):
    low_type = jnp.bfloat16
    item_count, frames, latent_dim = latents.shape
    tokens = item_count * frames
    onehot = (buckets[:, None] == jnp.arange(NBUCK)[None, :]).astype(jnp.float32)
    counts = lax.psum(jnp.dot(lengths.astype(jnp.float32), onehot, precision=HIGHEST), "fsdp")
    present = jnp.sum((counts > 0).astype(jnp.float32))
    bucket_scale = 1.0 / (present * LAT * jnp.maximum(counts, 1.0))
    item_scale = jnp.dot(onehot, bucket_scale, precision=HIGHEST)
    shards = (
        attention_weights.astype(low_type),
        cross_weights.astype(low_type),
        gate_up_weights.astype(low_type),
        down_weights.astype(low_type),
        latent_weights.astype(low_type),
        timing_weights.astype(low_type),
        norm_params.astype(low_type),
    )
    weights = (
        lax.all_gather(shards[0], ("seq", "fsdp"), axis=2, tiled=True),
        lax.all_gather(shards[1], ("seq", "fsdp"), axis=2, tiled=True),
        lax.all_gather(shards[2], ("seq", "fsdp"), axis=0, tiled=True),
        lax.all_gather(shards[3], ("seq", "fsdp"), axis=0, tiled=True),
        lax.all_gather(shards[4], ("seq", "fsdp"), axis=2, tiled=True),
        lax.all_gather(shards[5], ("seq", "fsdp"), axis=1, tiled=True),
        lax.all_gather(shards[6], ("seq", "fsdp"), axis=1, tiled=True),
    )
    signal = jnp.cos(0.5 * math.pi * timesteps)[:, None, None]
    noise_level = jnp.sin(0.5 * math.pi * timesteps)[:, None, None]
    noisy_input = signal * latents + noise_level * gaussian_noise
    target = (signal * gaussian_noise - noise_level * latents).reshape(tokens, latent_dim)
    features = time_features(timesteps)
    position = lax.axis_index("seq") * frames + jnp.arange(frames)
    live_mask = position[None, :] < lengths[:, None]
    half_dim = HEAD_DIM // 2
    inverse = 10000.0 ** (-jnp.arange(half_dim, dtype=jnp.float32) / half_dim)
    angles = position.astype(jnp.float32)[:, None] * inverse[None, :]
    cosine = jnp.cos(angles)[None, :, None, :]
    sine_table = jnp.sin(angles)[None, :, None, :]
    predicted, saved = layer_forward(
        weights, noisy_input, features, context, lengths, cosine, sine_table
    )
    difference = predicted - target
    errors = jnp.sum(difference * difference, axis=1).reshape(item_count, frames)
    per_item = jnp.sum(jnp.where(live_mask, errors, 0.0), axis=1)
    partial_sums = jnp.dot(per_item, onehot, precision=HIGHEST)
    bucket_sums = lax.psum(partial_sums, ("seq", "fsdp"))
    frame_scale = jnp.where(live_mask, item_scale[:, None], 0.0).reshape(tokens, 1)
    grad_pred = (2.0 * difference * frame_scale).astype(low_type)
    local_grads, gate_up_grad, down_grad = layer_backward(
        weights, saved, grad_pred, context, lengths, cosine, sine_table, position
    )
    reduced = (
        lax.psum_scatter(local_grads[0], ("seq", "fsdp"), scatter_dimension=2, tiled=True),
        lax.psum_scatter(local_grads[1], ("seq", "fsdp"), scatter_dimension=2, tiled=True),
        lax.psum_scatter(local_grads[2], ("seq", "fsdp"), scatter_dimension=2, tiled=True),
        lax.psum_scatter(local_grads[3], ("seq", "fsdp"), scatter_dimension=1, tiled=True),
        lax.psum_scatter(local_grads[4], ("seq", "fsdp"), scatter_dimension=1, tiled=True),
    )
    everything = tuple(reduced) + (gate_up_grad, down_grad)
    squares = sum((jnp.sum(grad * grad) for grad in everything))
    squares = lax.psum(squares, ("seq", "fsdp"))
    loss_value = jnp.sum(bucket_sums * bucket_scale)
    clip_norm = jnp.sqrt(squares)
    factor = CLIP_AT / jnp.maximum(clip_norm, CLIP_AT)
    attention_moment_new = 0.95 * attention_moment + reduced[0] * factor
    cross_moment_new = 0.95 * cross_moment + reduced[1] * factor
    attention_orth, cross_orth = newton_schulz(attention_moment_new, cross_moment_new)
    attention_new = attention_weights * (1.0 - MUON_RATE * DECAY_RATE) - MUON_RATE * attention_orth
    cross_new = cross_weights * (1.0 - MUON_RATE * DECAY_RATE) - MUON_RATE * cross_orth
    gate_up_new, gate_up_first_new, gate_up_second_new = adam_update(
        gate_up_weights, gate_up_first, gate_up_second, gate_up_grad * factor, ADAM_RATE, DECAY_RATE
    )
    down_new, down_first_new, down_second_new = adam_update(
        down_weights, down_first, down_second, down_grad * factor, ADAM_RATE, DECAY_RATE
    )
    latent_new, latent_first_new, latent_second_new = adam_update(
        latent_weights, latent_first, latent_second, reduced[2] * factor, ADAM_RATE, DECAY_RATE
    )
    timing_new, timing_first_new, timing_second_new = adam_update(
        timing_weights, timing_first, timing_second, reduced[3] * factor, ADAM_RATE, DECAY_RATE
    )
    norm_new, norm_first_new, norm_second_new = adam_update(
        norm_params, norm_first, norm_second, reduced[4] * factor, GAIN_RATE, 0.0
    )
    return (
        loss_value,
        clip_norm,
        attention_new,
        attention_moment_new,
        attention_new.astype(low_type),
        cross_new,
        cross_moment_new,
        cross_new.astype(low_type),
        gate_up_new,
        gate_up_first_new,
        gate_up_second_new,
        gate_up_new.astype(low_type),
        down_new,
        down_first_new,
        down_second_new,
        down_new.astype(low_type),
        latent_new,
        latent_first_new,
        latent_second_new,
        latent_new.astype(low_type),
        timing_new,
        timing_first_new,
        timing_second_new,
        timing_new.astype(low_type),
        norm_new,
        norm_first_new,
        norm_second_new,
    )


def general(mesh):
    return jax.shard_map(
        body,
        mesh=mesh,
        in_specs=(
            P("fsdp", "seq", None),
            P("fsdp", "seq", None),
            P("fsdp"),
            P("fsdp"),
            P("fsdp"),
            P("fsdp", None, None),
            P(None, None, ("seq", "fsdp")),
            P(None, None, ("seq", "fsdp")),
            P(None, None, ("seq", "fsdp")),
            P(None, None, ("seq", "fsdp")),
            P(("seq", "fsdp"), None),
            P(("seq", "fsdp"), None),
            P(("seq", "fsdp"), None),
            P(("seq", "fsdp"), None),
            P(("seq", "fsdp"), None),
            P(("seq", "fsdp"), None),
            P(None, None, ("seq", "fsdp")),
            P(None, None, ("seq", "fsdp")),
            P(None, None, ("seq", "fsdp")),
            P(None, ("seq", "fsdp")),
            P(None, ("seq", "fsdp")),
            P(None, ("seq", "fsdp")),
            P(None, ("seq", "fsdp")),
            P(None, ("seq", "fsdp")),
            P(None, ("seq", "fsdp")),
        ),
        out_specs=(
            P(),
            P(),
            P(None, None, ("seq", "fsdp")),
            P(None, None, ("seq", "fsdp")),
            P(None, None, ("seq", "fsdp")),
            P(None, None, ("seq", "fsdp")),
            P(None, None, ("seq", "fsdp")),
            P(None, None, ("seq", "fsdp")),
            P(("seq", "fsdp"), None),
            P(("seq", "fsdp"), None),
            P(("seq", "fsdp"), None),
            P(("seq", "fsdp"), None),
            P(("seq", "fsdp"), None),
            P(("seq", "fsdp"), None),
            P(("seq", "fsdp"), None),
            P(("seq", "fsdp"), None),
            P(None, None, ("seq", "fsdp")),
            P(None, None, ("seq", "fsdp")),
            P(None, None, ("seq", "fsdp")),
            P(None, None, ("seq", "fsdp")),
            P(None, ("seq", "fsdp")),
            P(None, ("seq", "fsdp")),
            P(None, ("seq", "fsdp")),
            P(None, ("seq", "fsdp")),
            P(None, ("seq", "fsdp")),
            P(None, ("seq", "fsdp")),
            P(None, ("seq", "fsdp")),
        ),
        check_vma=False,
    )


LAYER = ("y", "f")
ALL = ("z", "y", "f")
RANKS = 8
LOCAL_HEADS = HEADS // RANKS
COLS = LOCAL_HEADS * HEAD_DIM
LOW = jnp.bfloat16


MESH = pl.DeviceIdType.MESH


def place():
    at = lax.axis_index("f")
    return lax.axis_index("z"), lax.axis_index("y"), at // 2, at % 2


def turned(me, flip):
    z_at, y_at, x_at, core = me
    low = z_at % 2
    high = z_at // 2
    low = 1 - low if flip[0] & 1 else low
    high = 1 - high if flip[0] & 2 else high
    return (
        2 * high + low,
        1 - y_at if flip[1] else y_at,
        1 - x_at if flip[2] else x_at,
        1 - core if flip[3] else core,
    )


def device_of(where):
    return (where[0], where[1], 2 * where[2] + where[3])


def rank_of(where):
    return 4 * where[1] + 2 * where[2] + where[3]


def greet(peers):
    barrier = pltpu.get_barrier_semaphore()
    for peer in peers:
        pl.semaphore_signal(barrier, inc=1, device_id=device_of(peer), device_id_type=MESH)
    pl.semaphore_wait(barrier, len(peers))


LAYER_FLIPS = [(0, y, x, c) for y in range(2) for x in range(2) for c in range(2)][1:]


def comm_call(kernel, out_shape, arrays, scratch, ident, vmem=False, cost_us=20):
    spec = pl.BlockSpec(memory_space=pl.ANY)
    return pl.pallas_call(
        kernel,
        out_shape=out_shape,
        in_specs=[spec] * len(arrays),
        out_specs=jax.tree.map(lambda _: spec, out_shape),
        scratch_shapes=scratch,
        compiler_params=pltpu.CompilerParams(
            collective_id=ident, has_side_effects=True, vmem_limit_bytes=(40 << 20) if vmem else None
        ),
        cost_estimate=pl.CostEstimate(
            flops=cost_us * 10**9, bytes_accessed=1 << 20, transcendentals=0
        ),
    )(*arrays)


LINE_FLIPS = [(1, 0, 0, 0), (2, 0, 0, 0), (3, 0, 0, 0)]


def line_start(me, ins, outs, sent, got):
    copies = []
    for i, (src, dst) in enumerate(zip(ins, outs)):
        for k, flip in enumerate(LINE_FLIPS):
            peer = turned(me, flip)
            copy = pltpu.make_async_remote_copy(
                src_ref=src if len(src.shape) == 2 else src.at[peer[0]],
                dst_ref=dst.at[k],
                send_sem=sent.at[i, k],
                recv_sem=got.at[i, k],
                device_id=device_of(peer),
                device_id_type=MESH,
            )
            copy.start()
            copies.append(copy)
    return copies


def line_shapes(arrays):
    return tuple(
        jax.ShapeDtypeStruct((3,) + (a.shape if a.ndim == 2 else a.shape[1:]), a.dtype)
        for a in arrays
    )


LEVELS = 32000.0


def line_pack(parts):
    tops = jnp.max(jnp.abs(parts), axis=2)
    codes = jnp.round(parts * (LEVELS / jnp.maximum(tops, 1e-30))[:, :, None]).astype(jnp.int32)
    half = parts.shape[1] // 2
    return tops, lax.shift_left(codes[:, :half], 16) | (codes[:, half:] & 65535)


def line_total(part, tops, words):
    z_at = lax.axis_index("z")
    total = lax.dynamic_index_in_dim(part, z_at, 0, keepdims=False)
    steps = lax.dynamic_index_in_dim(tops, z_at, 1, keepdims=False) * (1.0 / LEVELS)
    for k in range(3):
        high = lax.shift_right_arithmetic(words[k], 16)
        low = lax.shift_right_arithmetic(lax.shift_left(words[k], 16), 16)
        codes = jnp.concatenate([high, low], axis=0).astype(jnp.float32)
        total = total + codes * steps[k][:, None]
    return total


def layer_swap(arrays, ident):
    count = len(arrays)

    def kernel(*refs):
        x_refs, o_refs, (sent, got, own) = refs[:count], refs[count : 2 * count], refs[2 * count :]
        me = place()
        peers = [turned(me, flip) for flip in LAYER_FLIPS]
        greet(peers)
        mine = rank_of(me)
        copies = [
            pltpu.make_async_remote_copy(
                src_ref=x_refs[j].at[rank_of(peer)],
                dst_ref=o_refs[j].at[mine],
                send_sem=sent.at[j, i],
                recv_sem=got.at[j, i],
                device_id=device_of(peer),
                device_id_type=MESH,
            )
            for i, peer in enumerate(peers)
            for j in range(count)
        ]
        for copy in copies:
            copy.start()
        for j in range(count):
            local = pltpu.make_async_copy(x_refs[j].at[mine], o_refs[j].at[mine], own.at[j])
            local.start()
            local.wait()
        for copy in copies:
            copy.wait()

    dma = pltpu.SemaphoreType.DMA
    return comm_call(
        kernel,
        tuple(jax.ShapeDtypeStruct(a.shape, a.dtype) for a in arrays),
        tuple(arrays),
        [dma((count, 7)), dma((count, 7)), dma((count,))],
        ident,
    )


def layer_gather(array, ident, carry=()):
    half = array.shape[0] // 2
    extra = len(carry)

    def kernel(x_ref, *refs):
        carry_in, o_ref, carry_out = refs[:extra], refs[extra], refs[extra + 1 : 2 * extra + 1]
        sent, got, own, csent, cgot = refs[2 * extra + 1 :]
        me = place()
        by_x, by_y, by_xy = (turned(me, (0, y, x, 0)) for y, x in ((0, 1), (1, 0), (1, 1)))
        other = turned(me, (0, 0, 0, 1))
        line = [turned(me, flip) for flip in LINE_FLIPS] if extra else []
        greet([by_x, by_y, other] + line)
        carried = line_start(me, carry_in, carry_out, csent, cgot)

        def send(which, src, dst, peer):
            copy = pltpu.make_async_remote_copy(
                src_ref=src,
                dst_ref=dst,
                send_sem=sent.at[which],
                recv_sem=got.at[which],
                device_id=device_of(peer),
                device_id_type=MESH,
            )
            copy.start()
            return copy

        slot = o_ref.at[rank_of(me)]
        first, second = pl.ds(0, half), pl.ds(half, half)
        copies = [
            send(0, x_ref.at[first], slot.at[first], by_x),
            send(1, x_ref.at[second], slot.at[second], by_y),
            send(2, x_ref.at[second], slot.at[second], by_x),
            send(3, x_ref.at[first], slot.at[first], by_y),
            send(4, x_ref, slot, other),
        ]
        local = pltpu.make_async_copy(x_ref, slot, own)
        local.start()
        from_x, from_y, from_xy = (o_ref.at[rank_of(p)] for p in (by_x, by_y, by_xy))
        copies[0].wait_recv()
        copies.append(send(5, from_x.at[first], from_x.at[first], by_y))
        copies[1].wait_recv()
        copies.append(send(6, from_y.at[second], from_y.at[second], by_x))
        copies[2].wait_recv()
        copies.append(send(7, from_x, from_x, other))
        copies[3].wait_recv()
        copies.append(send(8, from_y, from_y, other))
        copies[5].wait_recv()
        copies[6].wait_recv()
        copies.append(send(9, from_xy, from_xy, other))
        local.wait()
        for i in (4, 7, 8, 9):
            copies[i].wait_recv()
        for copy in copies:
            copy.wait_send()
        for copy in carried:
            copy.wait()

    dma = pltpu.SemaphoreType.DMA
    out = comm_call(
        kernel,
        (jax.ShapeDtypeStruct((RANKS,) + array.shape, array.dtype),) + line_shapes(carry),
        (array,) + tuple(carry),
        [dma((10,)), dma((10,)), dma] + [dma((max(extra, 1), 3))] * 2,
        ident,
        cost_us=30,
    )
    return out if extra else out[0]


def layer_sum(array, ident, carry=(), low=jnp.float32):
    _, rows, width = array.shape
    half = rows // 2
    f32 = jnp.float32

    extra = len(carry)

    def kernel(p_ref, *refs):
        carry_in, o_ref, carry_out = refs[:extra], refs[extra], refs[extra + 1 : 2 * extra + 1]
        mine, theirs, out_one, in_one, out_two, in_two, sent, got, own, csent, cgot = refs[
            2 * extra + 1 :
        ]
        me = place()
        z_at, y_at, x_at, core = me
        by_x, by_y = (turned(me, flip) for flip in ((0, 0, 1, 0), (0, 1, 0, 0)))
        other = turned(me, (0, 0, 0, 1))
        line = [turned(me, flip) for flip in LINE_FLIPS] if extra else []
        greet([by_x, by_y, other] + line)
        carried = line_start(me, carry_in, carry_out, csent, cgot)

        def send(which, src, dst, peer):
            copy = pltpu.make_async_remote_copy(
                src_ref=src,
                dst_ref=dst,
                send_sem=sent.at[which],
                recv_sem=got.at[which],
                device_id=device_of(peer),
                device_id_type=MESH,
            )
            copy.start()
            return copy

        cores, locals_ = [], []
        for dy in (1, 0):
            for dx in (1, 0):
                slot = 2 * dy + dx
                chip = turned(me, (0, dy, dx, 0))
                local = pltpu.make_async_copy(p_ref.at[rank_of(chip)], mine.at[slot], own.at[slot])
                local.start()
                locals_.append(local)
                cores.append(
                    send(slot, p_ref.at[rank_of(turned(chip, (0, 0, 0, 1)))], theirs.at[slot], other)
                )
        first, second = pl.ds(0, half), pl.ds(half, half)
        for i, slot in enumerate((3, 2, 1, 0)):
            locals_[i].wait()
            cores[i].wait_recv()
            mine[slot] = mine[slot] + theirs[slot]
        for k, slot in enumerate((3, 1)):
            out_one[0, k] = mine[slot, first, :].astype(low)
        over_x = send(4, out_one.at[0], in_one.at[0], by_x)
        for k, slot in enumerate((3, 2)):
            out_one[1, k] = mine[slot, second, :].astype(low)
        over_y = send(5, out_one.at[1], in_one.at[1], by_y)
        over_x.wait_recv()
        out_two[0] = (mine[2, first, :] + in_one[0, 0].astype(f32)).astype(low)
        next_y = send(6, out_two.at[0], in_two.at[0], by_y)
        over_y.wait_recv()
        out_two[1] = (mine[1, second, :] + in_one[1, 0].astype(f32)).astype(low)
        next_x = send(7, out_two.at[1], in_two.at[1], by_x)
        mine[0, first, :] = mine[0, first, :] + in_one[0, 1].astype(f32)
        mine[0, second, :] = mine[0, second, :] + in_one[1, 1].astype(f32)
        next_y.wait_recv()
        mine[0, first, :] = mine[0, first, :] + in_two[0].astype(f32)
        next_x.wait_recv()
        mine[0, second, :] = mine[0, second, :] + in_two[1].astype(f32)
        done = pltpu.make_async_copy(mine.at[0], o_ref, own.at[4])
        done.start()
        done.wait()
        for copy in cores + [over_x, over_y, next_y, next_x]:
            copy.wait_send()
        for copy in carried:
            copy.wait()

    dma = pltpu.SemaphoreType.DMA
    out = comm_call(
        kernel,
        (jax.ShapeDtypeStruct((rows, width), f32),) + line_shapes(carry),
        (array,) + tuple(carry),
        [
            pltpu.VMEM((4, rows, width), f32),
            pltpu.VMEM((4, rows, width), f32),
            pltpu.VMEM((2, 2, half, width), low),
            pltpu.VMEM((2, 2, half, width), low),
            pltpu.VMEM((2, half, width), low),
            pltpu.VMEM((2, half, width), low),
            dma((8,)),
            dma((8,)),
            dma((5,)),
        ]
        + [dma((max(extra, 1), 3))] * 2,
        ident,
        vmem=True,
        cost_us=65 if rows * width > 300000 else 25,
    )
    return out if extra else out[0]


def all_fold(vector, ident, fold):
    flips = [(z, y, x, c) for z in range(4) for y in range(2) for x in range(2) for c in range(2)][1:]
    count = len(flips)

    def kernel(v_ref, o_ref, slots, sent, got):
        me = place()
        peers = [turned(me, flip) for flip in flips]
        greet(peers)
        mine = RANKS * me[0] + rank_of(me)
        slots[mine] = v_ref[...]
        copies = [
            pltpu.make_async_remote_copy(
                src_ref=v_ref,
                dst_ref=slots.at[mine],
                send_sem=sent.at[i],
                recv_sem=got.at[i],
                device_id=device_of(peer),
                device_id_type=MESH,
            )
            for i, peer in enumerate(peers)
        ]
        for copy in copies:
            copy.start()
        for copy in copies:
            copy.wait()
        total = slots[0]
        for i in range(1, count + 1):
            total = fold(total, slots[i])
        o_ref[...] = total

    dma = pltpu.SemaphoreType.DMA
    spec = pl.BlockSpec(memory_space=pltpu.VMEM)
    return pl.pallas_call(
        kernel,
        out_shape=jax.ShapeDtypeStruct(vector.shape, vector.dtype),
        in_specs=[spec],
        out_specs=spec,
        scratch_shapes=[
            pltpu.VMEM((count + 1,) + vector.shape, vector.dtype),
            dma((count,)),
            dma((count,)),
        ],
        compiler_params=pltpu.CompilerParams(collective_id=ident, has_side_effects=True),
    )(vector)


def lanes_of(values):
    row = jnp.concatenate([jnp.stack(values), jnp.zeros((128 - len(values),), jnp.float32)])
    return jnp.broadcast_to(row[None, :], (8, 128))


def full_sum_steps(me, mine, theirs, in_a, in_b, in_c, in_d, in_z, put):
    z_at, y_at, x_at, core = me
    half = mine.shape[3] // 2
    first, second = pl.ds(0, half), pl.ds(half, half)
    by_x, by_y = (turned(me, flip) for flip in ((0, 0, 1, 0), (0, 1, 0, 0)))
    over_x = put(mine.at[1 - x_at, :, :, first], in_a, by_x)
    over_y = put(mine.at[:, 1 - y_at, :, second], in_b, by_y)
    over_x.wait_recv()
    mine[x_at, :, :, first] = mine[x_at, :, :, first] + in_a[...]
    next_y = put(mine.at[x_at, 1 - y_at, :, first], in_c, by_y)
    over_y.wait_recv()
    mine[:, y_at, :, second] = mine[:, y_at, :, second] + in_b[...]
    next_x = put(mine.at[1 - x_at, y_at, :, second], in_d, by_x)
    next_y.wait_recv()
    mine[x_at, y_at, :, first] = mine[x_at, y_at, :, first] + in_c[...]
    next_x.wait_recv()
    mine[x_at, y_at, :, second] = mine[x_at, y_at, :, second] + in_d[...]
    sends = []
    for k in (1, 2, 3):
        peer = turned(me, (k, 0, 0, 0))
        sends.append(put(mine.at[x_at, y_at, peer[0]], in_z.at[k - 1], peer))
    for send in sends:
        send.wait_recv()
    return mine[x_at, y_at, z_at] + in_z[0] + in_z[1] + in_z[2], [
        over_x,
        over_y,
        next_y,
        next_x,
    ] + sends


def putter(sent, got):
    count = [0]

    def put(src, dst, peer):
        at = count[0]
        count[0] += 1
        copy = pltpu.make_async_remote_copy(
            src_ref=src,
            dst_ref=dst,
            send_sem=sent.at[at],
            recv_sem=got.at[at],
            device_id=device_of(peer),
            device_id_type=MESH,
        )
        copy.start()
        return copy

    return put


NEAR_FLIPS = [(0, 0, 0, 1), (0, 0, 1, 0), (0, 1, 0, 0), (1, 0, 0, 0), (2, 0, 0, 0), (3, 0, 0, 0)]


def full_scratch(rows, lanes):
    half = rows // 2
    f32 = jnp.float32
    return [
        pltpu.VMEM((2, 2, 4, rows, lanes), f32),
        pltpu.VMEM((2, 2, 4, rows, lanes), f32),
        pltpu.VMEM((2, 4, half, lanes), f32),
        pltpu.VMEM((2, 4, half, lanes), f32),
        pltpu.VMEM((4, half, lanes), f32),
        pltpu.VMEM((4, half, lanes), f32),
        pltpu.VMEM((3, rows, lanes), f32),
    ]


def full_start(p_ref, me, mine, theirs, own, put):
    core = me[3]
    local = pltpu.make_async_copy(p_ref.at[core], mine, own)
    local.start()
    swap = put(p_ref.at[1 - core], theirs, turned(me, (0, 0, 0, 1)))
    local.wait()
    swap.wait_recv()
    for x in range(2):
        for y in range(2):
            mine[x, y] = mine[x, y] + theirs[x, y]
    return swap


def full_scatter(parts, ident, carry):
    rows, lanes = parts.shape[4:]
    extra = len(carry)

    def kernel(p_ref, *refs):
        carry_in, o_ref, carry_out = refs[:extra], refs[extra], refs[extra + 1 : 2 * extra + 1]
        mine, theirs, in_a, in_b, in_c, in_d, in_z, total, sent, got, own, csent, cgot = refs[
            2 * extra + 1 :
        ]
        me = place()
        greet([turned(me, flip) for flip in NEAR_FLIPS])
        carried = line_start(me, carry_in, carry_out, csent, cgot)
        put = putter(sent, got)
        swap = full_start(p_ref, me, mine, theirs, own.at[0], put)
        value, copies = full_sum_steps(me, mine, theirs, in_a, in_b, in_c, in_d, in_z, put)
        total[...] = value
        done = pltpu.make_async_copy(total, o_ref, own.at[1])
        done.start()
        done.wait()
        for copy in [swap] + copies:
            copy.wait_send()
        for copy in carried:
            copy.wait()

    dma = pltpu.SemaphoreType.DMA
    return comm_call(
        kernel,
        (jax.ShapeDtypeStruct((rows, lanes), jnp.float32),) + line_shapes(carry),
        (parts,) + tuple(carry),
        full_scratch(rows, lanes)
        + [pltpu.VMEM((rows, lanes), jnp.float32), dma((8,)), dma((8,)), dma((2,))]
        + [dma((extra, 3))] * 2,
        ident,
        vmem=True,
        cost_us=40,
    )


def newton_pair(pair):
    wide = 2 * HEAD_DIM
    row = lax.broadcasted_iota(jnp.int32, (wide, wide), 0)
    lane = lax.broadcasted_iota(jnp.int32, (wide, wide), 1)
    same = (row < HEAD_DIM) == (lane < HEAD_DIM)
    gram = jnp.where(same, jnp.concatenate([pair, pair], axis=0), 0.0)
    diagonal = jnp.where(row == lane, gram, 0.0)
    lone = jnp.sum(jnp.where(row < HEAD_DIM, diagonal, 0.0), keepdims=True)
    ltwo = jnp.sum(jnp.where(row < HEAD_DIM, 0.0, diagonal), keepdims=True)
    norm_value = jnp.sqrt(jnp.where(row < HEAD_DIM, lone, ltwo)) + 1e-07
    product = gram / (norm_value * norm_value)
    eye = jnp.where(row == lane, 1.0, 0.0)

    def mul(left, right):
        return jnp.dot(left, right, precision=HIGHEST, preferred_element_type=jnp.float32)

    total = None
    for newton_step in range(5):
        mixer = NS_COEF[0] * eye + NS_COEF[1] * product + NS_COEF[2] * mul(product, product)
        total = mixer if total is None else mul(mixer, total)
        if newton_step < 4:
            product = mul(mul(mixer, product), mixer)
    total = total / norm_value
    return total[:HEAD_DIM] + total[HEAD_DIM:]


def full_newton(parts, ident):
    rows, lanes = parts.shape[4:]
    half = rows // 2

    def kernel(p_ref, o_ref, mine, theirs, in_a, in_b, in_c, in_d, in_z, whole, sent, got, own):
        me = place()
        z_at, y_at, x_at, core = me
        greet([turned(me, flip) for flip in NEAR_FLIPS])
        put = putter(sent, got)
        swap = full_start(p_ref, me, mine, theirs, own.at[0], put)
        value, copies = full_sum_steps(me, mine, theirs, in_a, in_b, in_c, in_d, in_z, put)
        for i in range(rows // HEAD_DIM):
            part = slice(i * HEAD_DIM, (i + 1) * HEAD_DIM)
            whole[core, x_at, y_at, z_at, pl.ds(i * HEAD_DIM, HEAD_DIM)] = newton_pair(value[part])
        first, second = pl.ds(0, half), pl.ds(half, half)
        by_x, by_y = (turned(me, flip) for flip in ((0, 0, 1, 0), (0, 1, 0, 0)))
        slot = whole.at[core, x_at, y_at, z_at]
        over_z = [put(slot, slot, turned(me, (k, 0, 0, 0))) for k in (1, 2, 3)]
        for copy in over_z:
            copy.wait_recv()
        part_a = whole.at[core, x_at, y_at, :, first]
        part_b = whole.at[core, x_at, y_at, :, second]
        over_x = put(part_a, part_a, by_x)
        over_y = put(part_b, part_b, by_y)
        over_x.wait_recv()
        part_a = whole.at[core, :, y_at, :, first]
        next_y = put(part_a, part_a, by_y)
        over_y.wait_recv()
        part_b = whole.at[core, x_at, :, :, second]
        next_x = put(part_b, part_b, by_x)
        next_y.wait_recv()
        next_x.wait_recv()
        last = put(whole.at[core], whole.at[core], turned(me, (0, 0, 0, 1)))
        last.wait_recv()
        done = pltpu.make_async_copy(whole, o_ref, own.at[1])
        done.start()
        done.wait()
        for copy in [swap] + copies + over_z + [over_x, over_y, next_y, next_x, last]:
            copy.wait_send()

    dma = pltpu.SemaphoreType.DMA
    return comm_call(
        kernel,
        jax.ShapeDtypeStruct(parts.shape, jnp.float32),
        (parts,),
        full_scratch(rows, lanes)
        + [pltpu.VMEM((2, 2, 2, 4, rows, lanes), jnp.float32), dma((16,)), dma((16,)), dma((2,))],
        ident,
        vmem=True,
    )


def setup_exchange(slab, small, noisy, meta, ident):
    planes = 4
    flips_f = [flip for flip in LAYER_FLIPS if flip[1] == 0]

    def kernel(
        w_ref, s_ref, n_ref, m_ref, wo, so, no, mo, s_mid, n_mid, sent, got, csent, cgot, own
    ):
        me = place()
        z_at, y_at, x_at, core = me
        mine = rank_of(me)
        f_at = 2 * x_at + core
        layer = [turned(me, flip) for flip in LAYER_FLIPS]
        line = [turned(me, (k, 0, 0, 0)) for k in (1, 2, 3)]
        greet(layer + line)
        put = putter(sent, got)
        locals_ = [
            pltpu.make_async_copy(w_ref.at[mine], wo.at[z_at, mine], own.at[0]),
            pltpu.make_async_copy(s_ref, s_mid.at[z_at], own.at[1]),
            pltpu.make_async_copy(n_ref, n_mid.at[y_at, f_at], own.at[2]),
            pltpu.make_async_copy(m_ref, mo.at[f_at], own.at[3]),
        ]
        for copy in locals_:
            copy.start()
        small_line = [put(s_ref, s_mid.at[z_at], peer) for peer in line]
        slabs = [put(w_ref.at[rank_of(peer)], wo.at[z_at, mine], peer) for peer in layer]
        metas = [put(m_ref, mo.at[f_at], turned(me, flip)) for flip in flips_f]
        noisies = [put(n_ref, n_mid.at[y_at, f_at], peer) for peer in layer]
        for copy in locals_:
            copy.wait()
        for copy in slabs:
            copy.wait_recv()

        def along(which, target, source, step):
            return pltpu.make_async_remote_copy(
                src_ref=wo.at[source],
                dst_ref=wo.at[source],
                send_sem=csent.at[which, step],
                recv_sem=cgot.at[which, step],
                device_id=device_of((target, y_at, x_at, core)),
                device_id_type=MESH,
            )

        def go(step):
            @pl.when((z_at < planes - 1) & (z_at >= step))
            def _():
                along(0, z_at + 1, z_at - step, step).start()

            @pl.when((z_at > 0) & (z_at + step < planes))
            def _():
                along(1, z_at - 1, z_at + step, step).start()

        def come(step):
            @pl.when(z_at >= step + 1)
            def _():
                along(0, z_at - 1, z_at - 1 - step, step).wait_recv()

            @pl.when(z_at + step + 1 < planes)
            def _():
                along(1, z_at + 1, z_at + 1 + step, step).wait_recv()

        go(0)
        for copy in small_line:
            copy.wait_recv()
        smalls = [put(s_mid, so.at[:, mine], peer) for peer in layer]
        small_own = pltpu.make_async_copy(s_mid, so.at[:, mine], own.at[4])
        small_own.start()
        for copy in noisies:
            copy.wait_recv()
        noisy_line = [put(n_mid.at[:, peer[0]], no.at[z_at], peer) for peer in line]
        noisy_own = pltpu.make_async_copy(n_mid.at[:, z_at], no.at[z_at], own.at[5])
        noisy_own.start()
        come(0)
        go(1)
        come(1)
        go(2)
        come(2)
        small_own.wait()
        noisy_own.wait()
        for copy in metas + smalls + noisy_line:
            copy.wait_recv()
        for copy in small_line + slabs + metas + noisies + smalls + noisy_line:
            copy.wait_send()
        for step in range(3):

            @pl.when((z_at < planes - 1) & (z_at >= step))
            def _():
                along(0, z_at + 1, z_at - step, step).wait_send()

            @pl.when((z_at > 0) & (z_at + step < planes))
            def _():
                along(1, z_at - 1, z_at + step, step).wait_send()

    dma = pltpu.SemaphoreType.DMA
    shape = jax.ShapeDtypeStruct
    return comm_call(
        kernel,
        (
            shape((planes,) + slab.shape, slab.dtype),
            shape((planes, RANKS) + small.shape, small.dtype),
            shape((planes, 2) + noisy.shape, noisy.dtype),
            shape((4,) + meta.shape, meta.dtype),
        ),
        (slab, small, noisy, meta),
        [
            pltpu.VMEM((planes,) + small.shape, small.dtype),
            pltpu.VMEM((2, 4) + noisy.shape, noisy.dtype),
            dma((32,)),
            dma((32,)),
            dma((2, 3)),
            dma((2, 3)),
            dma((6,)),
        ],
        ident,
        vmem=True,
        cost_us=60,
    )


def swapped_halves(values):
    half_dim = values.shape[1] // 2
    return jnp.concatenate([values[:, half_dim:], values[:, :half_dim]], axis=1)


def attend_kernel(lengths_ref, qkv_ref, cos_ref, sin_ref, qr_ref, kr_ref, vr_ref, o_ref, low_ref, lse_ref):
    frames = qkv_ref.shape[1]
    length = lengths_ref[pl.program_id(0)]
    cosine, sine_table = cos_ref[...], sin_ref[...]
    chunk = 256
    live = lax.broadcasted_iota(jnp.int32, (chunk, frames), 1) < length
    for head in range(LOCAL_HEADS):
        at = slice(head * HEAD_DIM, (head + 1) * HEAD_DIM)

        def column(which):
            return qkv_ref[0, :, which * COLS + head * HEAD_DIM : which * COLS + (head + 1) * HEAD_DIM]

        query, key = column(0), column(1)
        queries = (query * cosine + swapped_halves(query) * sine_table).astype(LOW)
        keys = (key * cosine + swapped_halves(key) * sine_table).astype(LOW)
        values = column(2).astype(LOW)
        qr_ref[0, head] = queries
        kr_ref[0, head] = keys
        vr_ref[0, head] = values
        for part in range(frames // chunk):
            rows = slice(part * chunk, (part + 1) * chunk)
            scores = lax.dot_general(
                queries[rows], keys, (((1,), (1,)), ((), ())), preferred_element_type=jnp.float32
            ) * (1.0 / math.sqrt(HEAD_DIM))
            scores = jnp.where(live, scores, -1e30)
            top = jnp.max(scores, axis=1, keepdims=True)
            grown = jnp.exp(scores - top)
            total = jnp.sum(grown, axis=1, keepdims=True)
            weights = (grown * (1.0 / total)).astype(LOW)
            mixed = jnp.dot(weights, values, preferred_element_type=jnp.float32)
            o_ref[0, head, rows, :] = mixed
            span = low_ref.shape[2]
            for k in range(chunk // span):
                low_ref[part * (chunk // span) + k, 0, :, at] = mixed[
                    k * span : (k + 1) * span
                ].astype(LOW)
            lse_ref[0, head, rows, :] = top + jnp.log(total)


def attend(qkv, cosine, sine_table, lengths, span):
    count, frames, width = qkv.shape
    heads = pl.BlockSpec((1, LOCAL_HEADS, frames, HEAD_DIM), lambda i: (i, 0, 0, 0))
    table = pl.BlockSpec((frames, HEAD_DIM), lambda i: (0, 0))
    low = jax.ShapeDtypeStruct((count, LOCAL_HEADS, frames, HEAD_DIM), LOW)
    return pl.pallas_call(
        attend_kernel,
        grid=(count,),
        out_shape=(
            low,
            low,
            low,
            jax.ShapeDtypeStruct((count, LOCAL_HEADS, frames, HEAD_DIM), jnp.float32),
            jax.ShapeDtypeStruct((RANKS, count, span, COLS), LOW),
            jax.ShapeDtypeStruct((count, LOCAL_HEADS, frames, 1), jnp.float32),
        ),
        in_specs=[
            pl.BlockSpec(memory_space=pltpu.SMEM),
            pl.BlockSpec((1, frames, width), lambda i: (i, 0, 0)),
            table,
            table,
        ],
        out_specs=(
            heads,
            heads,
            heads,
            heads,
            pl.BlockSpec((RANKS, 1, span, COLS), lambda i: (0, i, 0, 0)),
            pl.BlockSpec((1, LOCAL_HEADS, frames, 1), lambda i: (i, 0, 0, 0)),
        ),
        compiler_params=pltpu.CompilerParams(vmem_limit_bytes=56 << 20),
        cost_estimate=pl.CostEstimate(
            flops=4 * count * frames * frames * COLS,
            bytes_accessed=10 * count * frames * COLS,
            transcendentals=count * LOCAL_HEADS * frames * frames,
        ),
    )(lengths, qkv, cosine, sine_table)


def attend_back_kernel(
    lengths_ref, q_ref, k_ref, v_ref, o_ref, lse_ref, do_ref, cos_ref, sin_ref, d_ref
):
    frames = q_ref.shape[2]
    length = lengths_ref[pl.program_id(0)]
    cosine, sine_table = cos_ref[...], sin_ref[...]
    chunk = 256
    scale = 1.0 / math.sqrt(HEAD_DIM)
    span = do_ref.shape[2]
    live = lax.broadcasted_iota(jnp.int32, (chunk, frames), 1) < length
    for head in range(LOCAL_HEADS):
        at = slice(head * HEAD_DIM, (head + 1) * HEAD_DIM)
        keys = k_ref[0, head]
        values = v_ref[0, head]
        grad_key = jnp.zeros((frames, HEAD_DIM), jnp.float32)
        grad_value = jnp.zeros((frames, HEAD_DIM), jnp.float32)
        for part in range(frames // chunk):
            rows = slice(part * chunk, (part + 1) * chunk)
            queries = q_ref[0, head, rows, :]
            grads = jnp.concatenate(
                [
                    do_ref[part * (chunk // span) + k, 0, :, at]
                    for k in range(chunk // span)
                ],
                axis=0,
            )
            scores = (
                lax.dot_general(
                    queries, keys, (((1,), (1,)), ((), ())), preferred_element_type=jnp.float32
                )
                * scale
            )
            scores = jnp.where(live, scores, -1e30)
            weights = jnp.exp(scores - lse_ref[0, head, rows, :])
            delta = jnp.sum(
                grads.astype(jnp.float32) * o_ref[0, head, rows, :], axis=1, keepdims=True
            )
            pulled = lax.dot_general(
                grads, values, (((1,), (1,)), ((), ())), preferred_element_type=jnp.float32
            )
            pushed = (weights * (pulled - delta)).astype(LOW)
            grad_query = jnp.dot(pushed, keys, preferred_element_type=jnp.float32) * scale
            grad_key = grad_key + rows_product(pushed, queries)
            grad_value = grad_value + rows_product(weights.astype(LOW), grads)
            d_ref[0, rows, head * HEAD_DIM : (head + 1) * HEAD_DIM] = (
                grad_query * cosine[rows] - swapped_halves(grad_query) * sine_table[rows]
            ).astype(LOW)
        grad_key = grad_key * scale
        d_ref[0, :, COLS + head * HEAD_DIM : COLS + (head + 1) * HEAD_DIM] = (
            grad_key * cosine - swapped_halves(grad_key) * sine_table
        ).astype(LOW)
        d_ref[0, :, 2 * COLS + head * HEAD_DIM : 2 * COLS + (head + 1) * HEAD_DIM] = (
            grad_value.astype(LOW)
        )


def attend_back(queries, key_rows, values, mixed, log_total, grads, cosine, sine_table, lengths):
    count, heads_here, frames, width = queries.shape
    span = grads.shape[2]
    heads = pl.BlockSpec((1, heads_here, frames, width), lambda i: (i, 0, 0, 0))
    table = pl.BlockSpec((frames, width), lambda i: (0, 0))
    return pl.pallas_call(
        attend_back_kernel,
        grid=(count,),
        out_shape=jax.ShapeDtypeStruct((count, frames, 3 * COLS), LOW),
        in_specs=[
            pl.BlockSpec(memory_space=pltpu.SMEM),
            heads,
            heads,
            heads,
            heads,
            pl.BlockSpec((1, heads_here, frames, 1), lambda i: (i, 0, 0, 0)),
            pl.BlockSpec((RANKS, 1, span, COLS), lambda i: (0, i, 0, 0)),
            table,
            table,
        ],
        out_specs=pl.BlockSpec((1, frames, 3 * COLS), lambda i: (i, 0, 0)),
        compiler_params=pltpu.CompilerParams(vmem_limit_bytes=56 << 20),
        cost_estimate=pl.CostEstimate(
            flops=10 * count * frames * frames * COLS,
            bytes_accessed=24 * count * frames * COLS,
            transcendentals=count * heads_here * frames * frames,
        ),
    )(lengths, queries, key_rows, values, mixed, log_total, grads, cosine, sine_table)


def cross_forward(cross_query, cross_key, cross_value):
    probs = jax.nn.softmax(scores_of(cross_query, cross_key), axis=-1)
    probs_low = probs.astype(LOW)
    out = jnp.einsum("bhqk,bkhd->bqhd", probs_low, cross_value, preferred_element_type=jnp.float32)
    return probs, probs_low, out


def fast_body(
    latents,
    gaussian_noise,
    timesteps,
    lengths,
    buckets,
    context,
    attention_weights,
    attention_moment,
    cross_weights,
    cross_moment,
    gate_up_weights,
    gate_up_first,
    gate_up_second,
    down_weights,
    down_first,
    down_second,
    latent_weights,
    latent_first,
    latent_second,
    timing_weights,
    timing_first,
    timing_second,
    norm_params,
    norm_first,
    norm_second,
):
    f32 = jnp.float32
    planes = lax.axis_size("z")
    z_at = lax.axis_index("z")
    rank = lax.axis_index("y") * lax.axis_size("f") + lax.axis_index("f")
    item_count, span, latent_dim = latents.shape
    frames = span * RANKS
    tokens = item_count * span
    group_tokens = item_count * frames
    flip = lambda array: jnp.swapaxes(array, 1, 2)

    attention_t = flip(attention_weights)
    cross_t = flip(cross_weights)
    attention_low = attention_t.astype(LOW)
    cross_low_t = cross_t.astype(LOW)
    small_low = jnp.concatenate(
        [
            latent_weights.reshape(-1, latent_weights.shape[2]),
            timing_weights,
            norm_params,
        ],
        axis=0,
    ).T.astype(LOW)
    signal = jnp.cos(0.5 * math.pi * timesteps)[:, None, None]
    noise_level = jnp.sin(0.5 * math.pi * timesteps)[:, None, None]
    noisy_own = (signal * latents + noise_level * gaussian_noise).astype(LOW)
    target_own = signal * gaussian_noise - noise_level * latents
    local_meta = jnp.stack([timesteps, lengths.astype(f32), buckets.astype(f32)])
    slab = jnp.concatenate(
        [
            attention_low[:3].reshape(-1, RANKS, COLS),
            cross_low_t.reshape(-1, RANKS, COLS),
        ],
        axis=0,
    )
    slab_all, small_all, noisy_all, meta_all = setup_exchange(
        jnp.swapaxes(slab, 0, 1),
        small_low,
        noisy_own.reshape(-1, latent_dim),
        jnp.pad(local_meta, ((0, 5), (0, 128 - item_count))),
        16,
    )
    attention_rest, slab_all = lax.optimization_barrier((attention_low[3:], slab_all))
    small_all = small_all.reshape(D, -1)
    latent_in = small_all[:, :LAT].T
    latent_out = small_all[:, LAT : 2 * LAT].T
    timing = small_all[:, 2 * LAT : 2 * LAT + FOUR].T
    norms = small_all[:, 2 * LAT + FOUR :].astype(f32).T
    qkv_rows = 3 * attention_low.shape[1]
    qkv_slab = slab_all[:, :, :qkv_rows].reshape(planes * RANKS, 3, -1, COLS)
    qkv_t = jnp.concatenate([qkv_slab[:, i].reshape(D, COLS) for i in range(3)], axis=1)
    cross_w = jnp.moveaxis(
        slab_all[:, :, qkv_rows:].reshape(planes * RANKS, 2, -1, COLS), 1, 0
    ).reshape(2, E, COLS)
    meta = jnp.swapaxes(meta_all[:, :3, :item_count], 0, 1).reshape(3, -1)
    times_all = meta[0]
    lengths_all = meta[1]
    onehot_all = (meta[2][:, None] == jnp.arange(NBUCK, dtype=f32)[None, :]).astype(f32)
    counts = jnp.dot(lengths_all, onehot_all, precision=HIGHEST)
    present = jnp.sum((counts > 0).astype(f32))
    bucket_scale = 1.0 / (present * LAT * jnp.maximum(counts, 1.0))
    own_at = z_at * item_count
    onehot = lax.dynamic_slice_in_dim(onehot_all, own_at, item_count, 0)
    item_scale = jnp.dot(onehot, bucket_scale, precision=HIGHEST)
    own_lengths = lax.dynamic_slice_in_dim(lengths_all, own_at, item_count, 0).astype(jnp.int32)
    features_all = time_features(times_all).astype(LOW)
    features = lax.dynamic_slice_in_dim(features_all, own_at, item_count, 0)

    noisy_low = jnp.swapaxes(
        noisy_all.reshape(RANKS, item_count, span, latent_dim), 0, 1
    ).reshape(item_count, frames, latent_dim)
    target = lax.ppermute(
        target_own, ALL, [(4 * s + g, RANKS * g + s) for s in range(RANKS) for g in range(planes)]
    ).reshape(tokens, latent_dim)
    context_all = lax.all_gather(context, "f", axis=0, tiled=True)
    context_own = lax.dynamic_slice_in_dim(context_all, own_at, item_count, 0).reshape(-1, E)
    context_len = context.shape[1]

    rest_t = lax.all_gather(attention_rest, ALL, axis=1, tiled=True)
    gate_up = lax.all_gather(gate_up_weights.astype(LOW), "z", axis=0, tiled=True)
    down_pairs = []
    for p in range(planes):
        for r in range(RANKS):
            down_pairs.append((2 * RANKS * (p // 2) + 2 * r + p % 2, RANKS * p + r))
    down = lax.all_gather(
        lax.ppermute(down_weights.astype(LOW), ALL, down_pairs), "z", axis=0, tiled=True
    )

    half_dim = HEAD_DIM // 2
    inverse = 10000.0 ** (-jnp.arange(half_dim, dtype=f32) / half_dim)
    angles = jnp.arange(frames, dtype=f32)[:, None] * inverse[None, :]
    cosine = jnp.concatenate([jnp.cos(angles)] * 2, axis=1)
    sine_table = jnp.concatenate([-jnp.sin(angles), jnp.sin(angles)], axis=1)

    timed = matmul_low(features, timing)
    start_all = (
        matmul_low(noisy_low.reshape(group_tokens, latent_dim), latent_in).reshape(
            item_count, frames, D
        )
        + timed[:, None, :]
    )
    start_own = lax.dynamic_slice_in_dim(start_all, rank * span, span, 1).reshape(tokens, D)
    noisy_mine = lax.dynamic_slice_in_dim(noisy_low, rank * span, span, 1).reshape(
        tokens, latent_dim
    )
    normed_one, back_one = jax.vjp(
        layer_norm, start_all.reshape(group_tokens, D), norms[0], norms[1]
    )
    normed_one = normed_one.astype(LOW)

    queries, key_rows, values, mixed, mixed_heads, log_total = attend(
        matmul_low(normed_one, qkv_t).reshape(item_count, frames, 3 * COLS),
        cosine,
        sine_table,
        own_lengths,
        span,
    )
    mixed_heads = mixed_heads.reshape(RANKS, tokens, COLS)
    mixed_low = jnp.swapaxes(layer_swap([mixed_heads], 1)[0], 0, 1).reshape(tokens, D)
    after_self = start_own + matmul_low(mixed_low, rest_t[0])
    normed_two, back_two = jax.vjp(layer_norm, after_self, norms[2], norms[3])
    normed_two = normed_two.astype(LOW)
    cross_query = (
        matmul_low(normed_two, rest_t[1]).astype(LOW).reshape(item_count, span, HEADS, HEAD_DIM)
    )
    pair_own = jnp.stack(
        [matmul_low(context_own, cross_w[0]), matmul_low(context_own, cross_w[1])]
    ).astype(LOW)
    pair_all = jnp.moveaxis(
        layer_gather(pair_own.reshape(-1, COLS), 3).reshape(RANKS, -1, COLS), 0, 1
    ).reshape(2, item_count, context_len, HEADS, HEAD_DIM)
    cross_key, cross_value = (pair_all[0], pair_all[1])
    probs, probs_low, cross_mixed = cross_forward(cross_query, cross_key, cross_value)
    cross_out = cross_mixed.reshape(tokens, D).astype(LOW)
    after_cross = after_self + matmul_low(cross_out, rest_t[2])
    normed_three, back_three = jax.vjp(layer_norm, after_cross, norms[4], norms[5])
    normed_three = normed_three.astype(LOW)
    normed_group = layer_gather(normed_three, 4).reshape(group_tokens, D)
    gate_both = times_transposed(normed_group, gate_up)
    units = gate_both.shape[1] // 2
    gate_half, up_half = (gate_both[:, :units], gate_both[:, units:])
    inner_act = (jax.nn.silu(gate_half) * up_half).astype(LOW)
    final_state = (
        after_cross
        + layer_sum(matmul_low(inner_act, down).reshape(RANKS, tokens, D), 5)
    ).astype(LOW)
    predicted = times_transposed(final_state, latent_out)

    position = rank * span + jnp.arange(span)
    live_mask = position[None, :] < own_lengths[:, None]
    difference = predicted - target
    errors = jnp.sum(difference * difference, axis=1).reshape(item_count, span)
    per_item = jnp.sum(jnp.where(live_mask, errors, 0.0), axis=1)
    partial_loss = jnp.sum(per_item * item_scale)
    frame_scale = jnp.where(live_mask, item_scale[:, None], 0.0).reshape(tokens, 1)
    grad_pred = (2.0 * difference * frame_scale).astype(LOW)

    grad_out_proj = rows_product(grad_pred, final_state)
    grad_state = matmul_low(grad_pred, latent_out)
    grad_group = layer_gather(grad_state.astype(LOW), 6).reshape(group_tokens, D)
    down_part = rows_product(inner_act, grad_group)
    grad_inner = times_transposed(grad_group, down)
    sigmoid_gate = jax.nn.sigmoid(gate_half)
    grad_gate = grad_inner * up_half * sigmoid_gate * (1.0 + gate_half * (1.0 - sigmoid_gate))
    grad_both = jnp.concatenate([grad_gate, grad_inner * gate_half * sigmoid_gate], axis=1).astype(
        LOW
    )
    gate_up_part = rows_product(grad_both, normed_group)
    down_slab = lax.psum_scatter(down_part, "z", scatter_dimension=0, tiled=True)
    down_grad = lax.ppermute(down_slab, ALL, [(b, a) for a, b in down_pairs])
    gate_up_part = gate_up_part.reshape(planes, -1, D)
    early = gate_up_part.shape[1] * 5 // 8
    early_tops, early_words = line_pack(gate_up_part[:, :early])
    late_tops, late_words = line_pack(gate_up_part[:, early:])
    grad_three, early_tops, early_words = layer_sum(
        matmul_low(grad_both, gate_up).reshape(RANKS, tokens, D),
        8,
        (early_tops, early_words),
    )
    residual_part, gain_three, shift_three = back_three(grad_three)
    grad_state = grad_state + residual_part
    grad_branch = grad_state.astype(LOW)
    grad_cross_out = lax.psum_scatter(
        rows_product(cross_out, grad_branch), ALL, scatter_dimension=0, tiled=True
    )
    grad_mix = (
        times_transposed(grad_branch, rest_t[2])
        .astype(LOW)
        .reshape(item_count, span, HEADS, HEAD_DIM)
    )
    grad_scores = jnp.einsum("bqhd,bkhd->bhqk", grad_mix, cross_value, preferred_element_type=f32)
    grad_cross_value = jnp.einsum(
        "bhqk,bqhd->bkhd", probs_low, grad_mix, preferred_element_type=f32
    )
    pushed = (probs * (grad_scores - jnp.sum(probs * grad_scores, axis=-1, keepdims=True))).astype(
        LOW
    )
    score_scale = math.sqrt(HEAD_DIM)
    grad_cross_query = (
        (jnp.einsum("bhqk,bkhd->bqhd", pushed, cross_key, preferred_element_type=f32) / score_scale)
        .astype(LOW)
        .reshape(tokens, D)
    )
    grad_cross_key = (
        jnp.einsum("bhqk,bqhd->bkhd", pushed, cross_query, preferred_element_type=f32) / score_scale
    )
    grad_pair = jnp.stack([grad_cross_key, grad_cross_value]).reshape(-1, RANKS, COLS)
    grad_pair = layer_sum(jnp.swapaxes(grad_pair, 0, 1), 9).reshape(
        2, item_count * context_len, COLS
    )
    grad_cross_w = jnp.einsum(
        "te,ptc->pec", context_own.astype(f32), grad_pair, precision=HIGHEST
    )
    grad_cross_q = lax.psum_scatter(
        rows_product(normed_two, grad_cross_query), ALL, scatter_dimension=0, tiled=True
    )
    residual_part, gain_two, shift_two = back_two(times_transposed(grad_cross_query, rest_t[1]))
    grad_state = grad_state + residual_part
    grad_branch = grad_state.astype(LOW)
    branch_group, late_tops, late_words = layer_gather(grad_branch, 2, (late_tops, late_words))
    branch_group = branch_group.reshape(group_tokens, D)
    gate_up_grad = jnp.concatenate(
        [
            line_total(gate_up_part[:, :early], early_tops, early_words),
            line_total(gate_up_part[:, early:], late_tops, late_words),
        ],
        axis=0,
    )
    out_rows = lax.dynamic_slice_in_dim(rest_t[0], rank * COLS, COLS, 0)
    grad_self_out = lax.psum_scatter(
        rows_product(mixed_heads.reshape(group_tokens, COLS), branch_group),
        "z",
        scatter_dimension=0,
        tiled=True,
    )
    grad_self_out = lax.ppermute(
        grad_self_out,
        ALL,
        [(RANKS * z + r, planes * r + z) for z in range(planes) for r in range(RANKS)],
    )
    rest_grad = jnp.stack([grad_self_out, grad_cross_q, grad_cross_out])
    grad_mixed = times_transposed(branch_group, out_rows).astype(LOW)
    grad_triple = attend_back(
        queries,
        key_rows,
        values,
        mixed,
        log_total,
        grad_mixed.reshape(RANKS, item_count, span, COLS),
        cosine,
        sine_table,
        own_lengths,
    ).reshape(group_tokens, 3 * COLS)
    qkv_part = rows_product(normed_one, grad_triple).reshape(planes, -1, 3 * COLS)
    cross_part = jnp.moveaxis(grad_cross_w.reshape(2, planes, -1, COLS), 1, 0).reshape(
        planes, -1, COLS
    )
    grad_one = times_transposed(grad_triple, qkv_t)
    residual_part, gain_one, shift_one = back_one(grad_one)
    grad_in_proj = rows_precise(
        noisy_low.reshape(group_tokens, latent_dim).astype(f32), residual_part
    ) + rows_precise(noisy_mine.astype(f32), grad_state)
    grad_timed = jnp.sum(residual_part.reshape(item_count, frames, D), axis=1) + jnp.sum(
        grad_state.reshape(item_count, span, D), axis=1
    )
    timed_slots = lax.dynamic_update_slice(
        jnp.zeros((item_count * planes, D), f32), grad_timed, (own_at, 0)
    )
    small_grad = jnp.concatenate(
        [
            grad_in_proj,
            grad_out_proj,
            jnp.stack([gain_one, shift_one, gain_two, shift_two, gain_three, shift_three]),
            timed_slots,
        ],
        axis=0,
    )
    by_target = small_grad.T.reshape(planes, 2, 2, 2, -1, small_grad.shape[0])
    small_grad, qkv_tops, qkv_words, cross_tops, cross_words = full_scatter(
        jnp.transpose(by_target, (3, 2, 1, 0, 4, 5)),
        17,
        line_pack(qkv_part) + line_pack(cross_part),
    )
    small_grad = small_grad.T
    qkv_grad = line_total(qkv_part, qkv_tops, qkv_words)
    cross_grad = line_total(cross_part, cross_tops, cross_words)
    cross_grad = jnp.swapaxes(cross_grad.reshape(2, RANKS, -1, COLS), 0, 1)
    qkv_grad, cross_grad = layer_swap([qkv_grad.reshape(RANKS, -1, 3 * COLS), cross_grad], 14)
    qkv_grad = jnp.transpose(qkv_grad.reshape(RANKS, -1, 3, COLS), (2, 1, 0, 3)).reshape(3, -1, D)
    cross_grad = jnp.transpose(cross_grad, (1, 2, 0, 3)).reshape(2, -1, D)
    latent_grad = small_grad[: 2 * LAT].reshape(2, LAT, -1)
    norm_grad = small_grad[2 * LAT : 2 * LAT + 6]
    timing_grad = rows_precise(features_all.astype(f32), small_grad[2 * LAT + 6 :])
    attention_grad = jnp.concatenate([qkv_grad, rest_grad], axis=0)

    everything = (
        attention_grad,
        cross_grad,
        latent_grad,
        timing_grad,
        norm_grad,
        gate_up_grad,
        down_grad,
    )
    squares = sum((jnp.sum(grad * grad) for grad in everything))
    totals = all_fold(lanes_of([squares, partial_loss]), 15, jnp.add)
    squares, loss_value = (totals[0, 0], totals[0, 1])
    clip_norm = jnp.sqrt(squares)
    factor = CLIP_AT / jnp.maximum(clip_norm, CLIP_AT)

    moment_t = 0.95 * flip(attention_moment) + attention_grad * factor
    cross_moment_t = 0.95 * flip(cross_moment) + cross_grad * factor
    pair = 2 * HEAD_DIM
    blocks = [
        moment.reshape(moment.shape[0], moment.shape[1], D // pair, pair)
        for moment in (moment_t, cross_moment_t)
    ]
    left_lane = jnp.arange(pair) < HEAD_DIM
    grams = jnp.concatenate(
        [
            jnp.einsum("skbi,skbj->sbij", block, block, precision=HIGHEST).reshape(-1, pair, pair)
            for block in blocks
        ]
    )
    grams = jnp.where(left_lane, grams[:, :HEAD_DIM], grams[:, HEAD_DIM:])
    mixers = full_newton(grams.reshape(2, 2, 2, planes, -1, pair), 18)
    mixers = mixers.reshape(-1, D // pair, HEAD_DIM, pair)
    mixers = jnp.concatenate(
        [jnp.where(left_lane, mixers, 0.0), jnp.where(left_lane, 0.0, mixers)], axis=2
    )
    stacks = attention_t.shape[0]
    orth = [
        jnp.einsum("skbj,sbji->skbi", block, mixer, precision=HIGHEST).reshape(moment.shape)
        for block, mixer, moment in zip(
            blocks, (mixers[:stacks], mixers[stacks:]), (moment_t, cross_moment_t)
        )
    ]
    attention_new = attention_t * (1.0 - MUON_RATE * DECAY_RATE) - MUON_RATE * orth[0]
    cross_new = cross_t * (1.0 - MUON_RATE * DECAY_RATE) - MUON_RATE * orth[1]
    gate_up_new, gate_up_first_new, gate_up_second_new = adam_update(
        gate_up_weights, gate_up_first, gate_up_second, gate_up_grad * factor, ADAM_RATE, DECAY_RATE
    )
    down_new, down_first_new, down_second_new = adam_update(
        down_weights, down_first, down_second, down_grad * factor, ADAM_RATE, DECAY_RATE
    )
    latent_new, latent_first_new, latent_second_new = adam_update(
        latent_weights, latent_first, latent_second, latent_grad * factor, ADAM_RATE, DECAY_RATE
    )
    timing_new, timing_first_new, timing_second_new = adam_update(
        timing_weights, timing_first, timing_second, timing_grad * factor, ADAM_RATE, DECAY_RATE
    )
    norm_new, norm_first_new, norm_second_new = adam_update(
        norm_params, norm_first, norm_second, norm_grad * factor, GAIN_RATE, 0.0
    )
    return (
        loss_value,
        clip_norm,
        flip(attention_new),
        flip(moment_t),
        flip(attention_new.astype(LOW)),
        flip(cross_new),
        flip(cross_moment_t),
        flip(cross_new.astype(LOW)),
        gate_up_new,
        gate_up_first_new,
        gate_up_second_new,
        gate_up_new.astype(LOW),
        down_new,
        down_first_new,
        down_second_new,
        down_new.astype(LOW),
        latent_new,
        latent_first_new,
        latent_second_new,
        latent_new.astype(LOW),
        timing_new,
        timing_first_new,
        timing_second_new,
        timing_new.astype(LOW),
        norm_new,
        norm_first_new,
        norm_second_new,
    )


def solution(mesh):
    if tuple(mesh.devices.shape) != (RANKS, 4):
        return general(mesh)
    mesh3 = jax.sharding.Mesh(mesh.devices.reshape(4, 2, 4), ALL)
    seq = ("z", "y")
    row = P(ALL, None)
    col2 = P(None, ALL)
    col3 = P(None, None, ALL)
    return jax.shard_map(
        fast_body,
        mesh=mesh3,
        in_specs=(P("f", seq, None),) * 2
        + (P("f"),) * 3
        + (P("f", None, None),)
        + (col3,) * 4
        + (row,) * 6
        + (col3,) * 3
        + (col2,) * 6,
        out_specs=(P(),) * 2 + (col3,) * 6 + (row,) * 8 + (col3,) * 4 + (col2,) * 7,
        check_vma=False,
    )
```

```python
import functools
import math

import jax
import jax.numpy as jnp
from jax import lax
from jax.experimental import pallas as pl
from jax.experimental.pallas import tpu as pltpu
from jax.sharding import PartitionSpec as P

D = 1536
HEADS = 24
HEAD_DIM = 64
FF = 6144
E = 768
LAT = 64
FOUR = 256
NBUCK = 4
STEP = 10


HIGHEST = lax.Precision.HIGHEST
NS_COEF = (3.4445, -4.775, 2.0315)
CLIP_AT = 0.01
MUON_RATE = 0.5
ADAM_RATE = 0.02
GAIN_RATE = 0.2
DECAY_RATE = 0.01


def times_transposed(left, weight):
    return lax.dot_general(
        left, weight, (((left.ndim - 1,), (1,)), ((), ())), preferred_element_type=jnp.float32
    )


def matmul_low(left, right):
    return jnp.dot(left, right, preferred_element_type=jnp.float32)


def rows_product(left, right):
    return lax.dot_general(
        left, right, (((0,), (0,)), ((), ())), preferred_element_type=jnp.float32
    )


def rows_precise(left, right):
    return lax.dot_general(left, right, (((0,), (0,)), ((), ())), precision=HIGHEST)


def layer_norm(hidden, gain, shift):
    centred = hidden - jnp.mean(hidden, axis=-1, keepdims=True)
    spread = jnp.mean(centred * centred, axis=-1, keepdims=True)
    return centred * lax.rsqrt(spread + 1e-05) * gain + shift


def rotate(values, cosine, sine_table):
    half_dim = values.shape[-1] // 2
    first = values[..., :half_dim]
    second = values[..., half_dim:]
    return jnp.concatenate(
        [first * cosine - second * sine_table, second * cosine + first * sine_table], axis=-1
    )


def time_features(timesteps):
    count = FOUR // 2
    freqs = jnp.exp(jnp.arange(count, dtype=jnp.float32) * (math.log(100.0) / max(count - 1, 1)))
    phases = 2.0 * math.pi * timesteps[:, None] * freqs[None, :]
    return jnp.concatenate([jnp.cos(phases), jnp.sin(phases)], axis=1)


def split_heads(values):
    return values.reshape(values.shape[0], values.shape[1], HEADS, HEAD_DIM)


def scores_of(queries, key_rows):
    return jnp.einsum(
        "bqhd,bkhd->bhqk", queries, key_rows, preferred_element_type=jnp.float32
    ) / math.sqrt(HEAD_DIM)


def masked_scores(queries, key_rows, lengths):
    key_live = jnp.arange(key_rows.shape[1])[None, :] < lengths[:, None]
    return jnp.where(key_live[:, None, None, :], scores_of(queries, key_rows), -1e30)


def attention_forward(queries, key_low, value_low, lengths):
    item_count, frames = (queries.shape[0], queries.shape[1])
    running_top = jnp.full((item_count, HEADS, frames), -1e29, jnp.float32)
    scores = masked_scores(
        queries, split_heads(lax.all_gather(key_low, "seq", axis=1, tiled=True)), lengths
    )
    new_top = jnp.maximum(running_top, jnp.max(scores, axis=-1))
    running_sum = jnp.sum(jnp.exp(scores - new_top[..., None]), axis=-1)
    running_top, running_sum = (new_top, running_sum)
    log_total = running_top + jnp.log(running_sum)
    scores = masked_scores(
        queries, split_heads(lax.all_gather(key_low, "seq", axis=1, tiled=True)), lengths
    )
    weights = jnp.exp(scores - log_total[..., None]).astype(jnp.bfloat16)
    mixed = jnp.einsum(
        "bhqk,bkhd->bqhd",
        weights,
        split_heads(lax.all_gather(value_low, "seq", axis=1, tiled=True)),
        preferred_element_type=jnp.float32,
    )
    return (mixed, log_total)


def attention_backward(
    queries, key_low, value_low, grad_out, log_total, row_delta, lengths, position
):
    key_heads = split_heads(key_low)
    value_heads = split_heads(value_low)
    local_live = (position[None, :] < lengths[:, None])[:, None, None, :]
    query_flat = queries.reshape(key_low.shape).astype(jnp.float32)
    grad_flat = grad_out.reshape(key_low.shape).astype(jnp.float32)
    total_flat = jnp.transpose(log_total, (0, 2, 1))
    pieces = (
        lax.all_gather(query_flat.astype(jnp.bfloat16), "seq", axis=1, tiled=True).astype(
            jnp.float32
        ),
        lax.all_gather(grad_flat.astype(jnp.bfloat16), "seq", axis=1, tiled=True).astype(
            jnp.float32
        ),
        lax.all_gather(total_flat.astype(jnp.bfloat16), "seq", axis=1, tiled=True).astype(
            jnp.float32
        ),
        lax.all_gather(row_delta.astype(jnp.bfloat16), "seq", axis=1, tiled=True).astype(
            jnp.float32
        ),
    )
    query_rows = split_heads(pieces[0].astype(jnp.bfloat16))
    grad_rows = split_heads(pieces[1].astype(jnp.bfloat16))
    total_rows = jnp.transpose(pieces[2], (0, 2, 1))[..., None]
    delta_rows = jnp.transpose(pieces[3], (0, 2, 1))[..., None]
    scores = jnp.where(local_live, scores_of(query_rows, key_heads), -1e30)
    weights = jnp.exp(scores - total_rows)
    grad_value = jnp.einsum(
        "bhqk,bqhd->bkhd",
        weights.astype(jnp.bfloat16),
        grad_rows,
        preferred_element_type=jnp.float32,
    )
    grad_scores = jnp.einsum(
        "bqhd,bkhd->bhqk", grad_rows, value_heads, preferred_element_type=jnp.float32
    )
    pushed = (weights * (grad_scores - delta_rows)).astype(jnp.bfloat16)
    grad_key = jnp.einsum("bhqk,bqhd->bkhd", pushed, query_rows, preferred_element_type=jnp.float32)
    grad_key, grad_value = (grad_key, grad_value)
    delta_heads = jnp.transpose(row_delta, (0, 2, 1))[..., None]
    pieces = (
        lax.all_gather(key_low, "seq", axis=1, tiled=True),
        lax.all_gather(value_low, "seq", axis=1, tiled=True),
    )
    key_rows = split_heads(pieces[0])
    scores = masked_scores(queries, key_rows, lengths)
    weights = jnp.exp(scores - log_total[..., None])
    grad_scores = jnp.einsum(
        "bqhd,bkhd->bhqk", grad_out, split_heads(pieces[1]), preferred_element_type=jnp.float32
    )
    pushed = (weights * (grad_scores - delta_heads)).astype(jnp.bfloat16)
    grad_query = jnp.einsum("bhqk,bkhd->bqhd", pushed, key_rows, preferred_element_type=jnp.float32)
    score_scale = math.sqrt(HEAD_DIM)
    return (grad_query / score_scale, grad_key / score_scale, grad_value)


def layer_forward(weights, noisy_input, features, context, lengths, cosine, sine_table):
    attention, cross, gate_up, down, latent, timing, norms = weights
    norms = norms.astype(jnp.float32)
    item_count, frames, latent_dim = noisy_input.shape
    tokens = item_count * frames
    noisy_low = noisy_input.reshape(tokens, latent_dim).astype(jnp.bfloat16)
    feat_low = features.astype(jnp.bfloat16)
    timed = matmul_low(feat_low, timing)
    start_state = (
        matmul_low(noisy_low, latent[0]).reshape(item_count, frames, D) + timed[:, None, :]
    ).reshape(tokens, D)
    normed_one, back_one = jax.vjp(layer_norm, start_state, norms[0], norms[1])
    normed_one = normed_one.astype(jnp.bfloat16)
    triple = times_transposed(normed_one, attention[:3].reshape(3 * D, D)).reshape(
        item_count, frames, 3, HEADS, HEAD_DIM
    )
    queries = rotate(triple[:, :, 0], cosine, sine_table).astype(jnp.bfloat16)
    key_low = (
        rotate(triple[:, :, 1], cosine, sine_table)
        .astype(jnp.bfloat16)
        .reshape(item_count, frames, D)
    )
    value_low = triple[:, :, 2].astype(jnp.bfloat16).reshape(item_count, frames, D)
    mixed, log_total = attention_forward(queries, key_low, value_low, lengths)
    mixed_low = mixed.reshape(tokens, D).astype(jnp.bfloat16)
    after_self = start_state + times_transposed(mixed_low, attention[3])
    normed_two, back_two = jax.vjp(layer_norm, after_self, norms[2], norms[3])
    normed_two = normed_two.astype(jnp.bfloat16)
    cross_query = (
        times_transposed(normed_two, attention[4])
        .astype(jnp.bfloat16)
        .reshape(item_count, frames, HEADS, HEAD_DIM)
    )
    context_len = context.shape[1]
    cross_pair = times_transposed(
        context.reshape(item_count * context_len, E), cross.reshape(2 * D, E)
    ).astype(jnp.bfloat16)
    cross_pair = cross_pair.reshape(item_count, context_len, 2, HEADS, HEAD_DIM)
    cross_key, cross_value = (cross_pair[:, :, 0], cross_pair[:, :, 1])
    cross_weights = jax.nn.softmax(scores_of(cross_query, cross_key), axis=-1)
    cross_low = cross_weights.astype(jnp.bfloat16)
    cross_out = (
        jnp.einsum("bhqk,bkhd->bqhd", cross_low, cross_value, preferred_element_type=jnp.float32)
        .reshape(tokens, D)
        .astype(jnp.bfloat16)
    )
    after_cross = after_self + times_transposed(cross_out, attention[5])
    normed_three, back_three = jax.vjp(layer_norm, after_cross, norms[4], norms[5])
    normed_three = normed_three.astype(jnp.bfloat16)
    gate_both = times_transposed(normed_three, gate_up)
    gate_half, up_half = (gate_both[:, :FF], gate_both[:, FF:])
    inner_act = (jax.nn.silu(gate_half) * up_half).astype(jnp.bfloat16)
    final_state = (after_cross + matmul_low(inner_act, down)).astype(jnp.bfloat16)
    predicted = times_transposed(final_state, latent[1])
    saved = (
        noisy_low,
        feat_low,
        back_one,
        normed_one,
        queries,
        key_low,
        value_low,
        mixed,
        log_total,
        mixed_low,
        back_two,
        normed_two,
        cross_query,
        cross_key,
        cross_value,
        cross_weights,
        cross_low,
        cross_out,
        back_three,
        normed_three,
        gate_half,
        up_half,
        inner_act,
        final_state,
    )
    return (predicted, saved)


def layer_backward(weights, saved, grad_pred, context, lengths, cosine, sine_table, position):
    attention, cross, gate_up, down, latent, timing, norms = weights
    (
        noisy_low,
        feat_low,
        back_one,
        normed_one,
        queries,
        key_low,
        value_low,
        mixed,
        log_total,
        mixed_low,
        back_two,
        normed_two,
        cross_query,
        cross_key,
        cross_value,
        cross_weights,
        cross_low,
        cross_out,
        back_three,
        normed_three,
        gate_half,
        up_half,
        inner_act,
        final_state,
    ) = saved
    item_count, frames = (queries.shape[0], queries.shape[1])
    tokens = item_count * frames
    grad_out_proj = rows_product(grad_pred, final_state)
    grad_state = matmul_low(grad_pred, latent[1])
    grad_branch = grad_state.astype(jnp.bfloat16)
    down_reduced = lax.psum_scatter(
        rows_product(inner_act, grad_branch), ("seq", "fsdp"), scatter_dimension=0, tiled=True
    )
    grad_inner = times_transposed(grad_branch, down)
    sigmoid_gate = jax.nn.sigmoid(gate_half)
    grad_gate = grad_inner * up_half * sigmoid_gate * (1.0 + gate_half * (1.0 - sigmoid_gate))
    grad_both = jnp.concatenate([grad_gate, grad_inner * gate_half * sigmoid_gate], axis=1).astype(
        jnp.bfloat16
    )
    gate_up_reduced = lax.psum_scatter(
        rows_product(grad_both, normed_three), ("seq", "fsdp"), scatter_dimension=0, tiled=True
    )
    residual_part, gain_three, shift_three = back_three(matmul_low(grad_both, gate_up))
    grad_state = grad_state + residual_part
    grad_branch = grad_state.astype(jnp.bfloat16)
    grad_cross_out = rows_product(grad_branch, cross_out)
    grad_mix = (
        matmul_low(grad_branch, attention[5])
        .astype(jnp.bfloat16)
        .reshape(item_count, frames, HEADS, HEAD_DIM)
    )
    grad_scores = jnp.einsum(
        "bqhd,bkhd->bhqk", grad_mix, cross_value, preferred_element_type=jnp.float32
    )
    grad_cross_value = jnp.einsum(
        "bhqk,bqhd->bkhd", cross_low, grad_mix, preferred_element_type=jnp.float32
    )
    pushed = (
        cross_weights * (grad_scores - jnp.sum(cross_weights * grad_scores, axis=-1, keepdims=True))
    ).astype(jnp.bfloat16)
    score_scale = math.sqrt(HEAD_DIM)
    grad_cross_query = (
        (
            jnp.einsum("bhqk,bkhd->bqhd", pushed, cross_key, preferred_element_type=jnp.float32)
            / score_scale
        )
        .astype(jnp.bfloat16)
        .reshape(tokens, D)
    )
    grad_cross_key = (
        jnp.einsum("bhqk,bqhd->bkhd", pushed, cross_query, preferred_element_type=jnp.float32)
        / score_scale
    )
    context_len = context.shape[1]
    grad_pair = jnp.stack([grad_cross_key, grad_cross_value], axis=2).reshape(
        item_count * context_len, 2 * D
    )
    grad_cross = rows_precise(
        grad_pair, context.reshape(item_count * context_len, E).astype(jnp.float32)
    ).reshape(2, D, E)
    grad_cross_q = rows_product(grad_cross_query, normed_two)
    residual_part, gain_two, shift_two = back_two(matmul_low(grad_cross_query, attention[4]))
    grad_state = grad_state + residual_part
    grad_branch = grad_state.astype(jnp.bfloat16)
    grad_self_out = rows_product(grad_branch, mixed_low)
    grad_mixed = (
        matmul_low(grad_branch, attention[3])
        .astype(jnp.bfloat16)
        .reshape(item_count, frames, HEADS, HEAD_DIM)
    )
    row_delta = jnp.sum(grad_mixed.astype(jnp.float32) * mixed, axis=-1)
    grad_query, grad_key, grad_value = attention_backward(
        queries, key_low, value_low, grad_mixed, log_total, row_delta, lengths, position
    )
    grad_query = rotate(grad_query, cosine, -sine_table)
    grad_key = rotate(grad_key, cosine, -sine_table)
    grad_triple = (
        jnp.stack([grad_query, grad_key, grad_value], axis=2)
        .astype(jnp.bfloat16)
        .reshape(tokens, 3 * D)
    )
    grad_qkv = rows_product(grad_triple, normed_one).reshape(3, D, D)
    residual_part, gain_one, shift_one = back_one(
        matmul_low(grad_triple, attention[:3].reshape(3 * D, D))
    )
    grad_state = grad_state + residual_part
    grad_in_proj = rows_product(noisy_low, grad_state.astype(jnp.bfloat16))
    grad_timed = jnp.sum(grad_state.reshape(item_count, frames, D), axis=1)
    grad_timing = rows_precise(feat_low.astype(jnp.float32), grad_timed)
    grad_attention = jnp.concatenate(
        [grad_qkv, jnp.stack([grad_self_out, grad_cross_q, grad_cross_out])], axis=0
    )
    grad_latent = jnp.stack([grad_in_proj, grad_out_proj])
    grad_norms = jnp.stack([gain_one, shift_one, gain_two, shift_two, gain_three, shift_three])
    return (
        (grad_attention, grad_cross, grad_latent, grad_timing, grad_norms),
        gate_up_reduced,
        down_reduced,
    )


def gram_of(blocks):
    return jnp.einsum("sbik,sbjk->sbij", blocks, blocks, precision=HIGHEST)


def gram_sum(first, second):
    return lax.psum((gram_of(first), gram_of(second)), ("seq", "fsdp"))


def newton_schulz(first_moment, second_moment):
    moments = (first_moment, second_moment)
    blocks = [
        moment.reshape(moment.shape[0], moment.shape[1] // HEAD_DIM, HEAD_DIM, moment.shape[2])
        for moment in moments
    ]
    gram_list = gram_sum(blocks[0], blocks[1])
    block_norm = [
        jnp.sqrt(jnp.trace(gram, axis1=2, axis2=3))[..., None, None] + 1e-07 for gram in gram_list
    ]
    current = [block / norm_value for block, norm_value in zip(blocks, block_norm)]
    products = [gram / (norm_value * norm_value) for gram, norm_value in zip(gram_list, block_norm)]
    for newton_step in range(5):
        if newton_step > 0:
            products = gram_sum(current[0], current[1])
        updated = []
        for block, product in zip(current, products):
            squared = jnp.einsum("sbij,sbjk->sbik", product, product, precision=HIGHEST)
            mixer = NS_COEF[1] * product + NS_COEF[2] * squared
            updated.append(
                NS_COEF[0] * block + jnp.einsum("sbij,sbjk->sbik", mixer, block, precision=HIGHEST)
            )
        current = updated
    return [block.reshape(moment.shape) for block, moment in zip(current, moments)]


def adam_update(weight, first, second, grad, rate, decay):
    first_new = 0.9 * first + 0.1 * grad
    second_new = 0.95 * second + 0.05 * grad * grad
    first_hat = first_new / (1.0 - 0.9**STEP)
    second_hat = second_new / (1.0 - 0.95**STEP)
    weight_new = weight - rate * (first_hat / (jnp.sqrt(second_hat) + 1e-08) + decay * weight)
    return (weight_new, first_new, second_new)


def body(
    latents,
    gaussian_noise,
    timesteps,
    lengths,
    buckets,
    context,
    attention_weights,
    attention_moment,
    cross_weights,
    cross_moment,
    gate_up_weights,
    gate_up_first,
    gate_up_second,
    down_weights,
    down_first,
    down_second,
    latent_weights,
    latent_first,
    latent_second,
    timing_weights,
    timing_first,
    timing_second,
    norm_params,
    norm_first,
    norm_second,
):
    low_type = jnp.bfloat16
    item_count, frames, latent_dim = latents.shape
    tokens = item_count * frames
    onehot = (buckets[:, None] == jnp.arange(NBUCK)[None, :]).astype(jnp.float32)
    counts = lax.psum(jnp.dot(lengths.astype(jnp.float32), onehot, precision=HIGHEST), "fsdp")
    present = jnp.sum((counts > 0).astype(jnp.float32))
    bucket_scale = 1.0 / (present * LAT * jnp.maximum(counts, 1.0))
    item_scale = jnp.dot(onehot, bucket_scale, precision=HIGHEST)
    shards = (
        attention_weights.astype(low_type),
        cross_weights.astype(low_type),
        gate_up_weights.astype(low_type),
        down_weights.astype(low_type),
        latent_weights.astype(low_type),
        timing_weights.astype(low_type),
        norm_params.astype(low_type),
    )
    weights = (
        lax.all_gather(shards[0], ("seq", "fsdp"), axis=2, tiled=True),
        lax.all_gather(shards[1], ("seq", "fsdp"), axis=2, tiled=True),
        lax.all_gather(shards[2], ("seq", "fsdp"), axis=0, tiled=True),
        lax.all_gather(shards[3], ("seq", "fsdp"), axis=0, tiled=True),
        lax.all_gather(shards[4], ("seq", "fsdp"), axis=2, tiled=True),
        lax.all_gather(shards[5], ("seq", "fsdp"), axis=1, tiled=True),
        lax.all_gather(shards[6], ("seq", "fsdp"), axis=1, tiled=True),
    )
    signal = jnp.cos(0.5 * math.pi * timesteps)[:, None, None]
    noise_level = jnp.sin(0.5 * math.pi * timesteps)[:, None, None]
    noisy_input = signal * latents + noise_level * gaussian_noise
    target = (signal * gaussian_noise - noise_level * latents).reshape(tokens, latent_dim)
    features = time_features(timesteps)
    position = lax.axis_index("seq") * frames + jnp.arange(frames)
    live_mask = position[None, :] < lengths[:, None]
    half_dim = HEAD_DIM // 2
    inverse = 10000.0 ** (-jnp.arange(half_dim, dtype=jnp.float32) / half_dim)
    angles = position.astype(jnp.float32)[:, None] * inverse[None, :]
    cosine = jnp.cos(angles)[None, :, None, :]
    sine_table = jnp.sin(angles)[None, :, None, :]
    predicted, saved = layer_forward(
        weights, noisy_input, features, context, lengths, cosine, sine_table
    )
    difference = predicted - target
    errors = jnp.sum(difference * difference, axis=1).reshape(item_count, frames)
    per_item = jnp.sum(jnp.where(live_mask, errors, 0.0), axis=1)
    partial_sums = jnp.dot(per_item, onehot, precision=HIGHEST)
    bucket_sums = lax.psum(partial_sums, ("seq", "fsdp"))
    frame_scale = jnp.where(live_mask, item_scale[:, None], 0.0).reshape(tokens, 1)
    grad_pred = (2.0 * difference * frame_scale).astype(low_type)
    local_grads, gate_up_grad, down_grad = layer_backward(
        weights, saved, grad_pred, context, lengths, cosine, sine_table, position
    )
    reduced = (
        lax.psum_scatter(local_grads[0], ("seq", "fsdp"), scatter_dimension=2, tiled=True),
        lax.psum_scatter(local_grads[1], ("seq", "fsdp"), scatter_dimension=2, tiled=True),
        lax.psum_scatter(local_grads[2], ("seq", "fsdp"), scatter_dimension=2, tiled=True),
        lax.psum_scatter(local_grads[3], ("seq", "fsdp"), scatter_dimension=1, tiled=True),
        lax.psum_scatter(local_grads[4], ("seq", "fsdp"), scatter_dimension=1, tiled=True),
    )
    everything = tuple(reduced) + (gate_up_grad, down_grad)
    squares = sum((jnp.sum(grad * grad) for grad in everything))
    squares = lax.psum(squares, ("seq", "fsdp"))
    loss_value = jnp.sum(bucket_sums * bucket_scale)
    clip_norm = jnp.sqrt(squares)
    factor = CLIP_AT / jnp.maximum(clip_norm, CLIP_AT)
    attention_moment_new = 0.95 * attention_moment + reduced[0] * factor
    cross_moment_new = 0.95 * cross_moment + reduced[1] * factor
    attention_orth, cross_orth = newton_schulz(attention_moment_new, cross_moment_new)
    attention_new = attention_weights * (1.0 - MUON_RATE * DECAY_RATE) - MUON_RATE * attention_orth
    cross_new = cross_weights * (1.0 - MUON_RATE * DECAY_RATE) - MUON_RATE * cross_orth
    gate_up_new, gate_up_first_new, gate_up_second_new = adam_update(
        gate_up_weights, gate_up_first, gate_up_second, gate_up_grad * factor, ADAM_RATE, DECAY_RATE
    )
    down_new, down_first_new, down_second_new = adam_update(
        down_weights, down_first, down_second, down_grad * factor, ADAM_RATE, DECAY_RATE
    )
    latent_new, latent_first_new, latent_second_new = adam_update(
        latent_weights, latent_first, latent_second, reduced[2] * factor, ADAM_RATE, DECAY_RATE
    )
    timing_new, timing_first_new, timing_second_new = adam_update(
        timing_weights, timing_first, timing_second, reduced[3] * factor, ADAM_RATE, DECAY_RATE
    )
    norm_new, norm_first_new, norm_second_new = adam_update(
        norm_params, norm_first, norm_second, reduced[4] * factor, GAIN_RATE, 0.0
    )
    return (
        loss_value,
        clip_norm,
        attention_new,
        attention_moment_new,
        attention_new.astype(low_type),
        cross_new,
        cross_moment_new,
        cross_new.astype(low_type),
        gate_up_new,
        gate_up_first_new,
        gate_up_second_new,
        gate_up_new.astype(low_type),
        down_new,
        down_first_new,
        down_second_new,
        down_new.astype(low_type),
        latent_new,
        latent_first_new,
        latent_second_new,
        latent_new.astype(low_type),
        timing_new,
        timing_first_new,
        timing_second_new,
        timing_new.astype(low_type),
        norm_new,
        norm_first_new,
        norm_second_new,
    )


def general(mesh):
    return jax.shard_map(
        body,
        mesh=mesh,
        in_specs=(
            P("fsdp", "seq", None),
            P("fsdp", "seq", None),
            P("fsdp"),
            P("fsdp"),
            P("fsdp"),
            P("fsdp", None, None),
            P(None, None, ("seq", "fsdp")),
            P(None, None, ("seq", "fsdp")),
            P(None, None, ("seq", "fsdp")),
            P(None, None, ("seq", "fsdp")),
            P(("seq", "fsdp"), None),
            P(("seq", "fsdp"), None),
            P(("seq", "fsdp"), None),
            P(("seq", "fsdp"), None),
            P(("seq", "fsdp"), None),
            P(("seq", "fsdp"), None),
            P(None, None, ("seq", "fsdp")),
            P(None, None, ("seq", "fsdp")),
            P(None, None, ("seq", "fsdp")),
            P(None, ("seq", "fsdp")),
            P(None, ("seq", "fsdp")),
            P(None, ("seq", "fsdp")),
            P(None, ("seq", "fsdp")),
            P(None, ("seq", "fsdp")),
            P(None, ("seq", "fsdp")),
        ),
        out_specs=(
            P(),
            P(),
            P(None, None, ("seq", "fsdp")),
            P(None, None, ("seq", "fsdp")),
            P(None, None, ("seq", "fsdp")),
            P(None, None, ("seq", "fsdp")),
            P(None, None, ("seq", "fsdp")),
            P(None, None, ("seq", "fsdp")),
            P(("seq", "fsdp"), None),
            P(("seq", "fsdp"), None),
            P(("seq", "fsdp"), None),
            P(("seq", "fsdp"), None),
            P(("seq", "fsdp"), None),
            P(("seq", "fsdp"), None),
            P(("seq", "fsdp"), None),
            P(("seq", "fsdp"), None),
            P(None, None, ("seq", "fsdp")),
            P(None, None, ("seq", "fsdp")),
            P(None, None, ("seq", "fsdp")),
            P(None, None, ("seq", "fsdp")),
            P(None, ("seq", "fsdp")),
            P(None, ("seq", "fsdp")),
            P(None, ("seq", "fsdp")),
            P(None, ("seq", "fsdp")),
            P(None, ("seq", "fsdp")),
            P(None, ("seq", "fsdp")),
            P(None, ("seq", "fsdp")),
        ),
        check_vma=False,
    )


LAYER = ("y", "f")
ALL = ("z", "y", "f")
RANKS = 8
LOCAL_HEADS = HEADS // RANKS
COLS = LOCAL_HEADS * HEAD_DIM
LOW = jnp.bfloat16


MESH = pl.DeviceIdType.MESH


def place():
    at = lax.axis_index("f")
    return lax.axis_index("z"), lax.axis_index("y"), at // 2, at % 2


def turned(me, flip):
    z_at, y_at, x_at, core = me
    low = z_at % 2
    high = z_at // 2
    low = 1 - low if flip[0] & 1 else low
    high = 1 - high if flip[0] & 2 else high
    return (
        2 * high + low,
        1 - y_at if flip[1] else y_at,
        1 - x_at if flip[2] else x_at,
        1 - core if flip[3] else core,
    )


def device_of(where):
    return (where[0], where[1], 2 * where[2] + where[3])


def rank_of(where):
    return 4 * where[1] + 2 * where[2] + where[3]


def greet(peers):
    barrier = pltpu.get_barrier_semaphore()
    for peer in peers:
        pl.semaphore_signal(barrier, inc=1, device_id=device_of(peer), device_id_type=MESH)
    pl.semaphore_wait(barrier, len(peers))


LAYER_FLIPS = [(0, y, x, c) for y in range(2) for x in range(2) for c in range(2)][1:]


def comm_call(kernel, out_shape, arrays, scratch, ident, vmem=False, cost_us=20):
    spec = pl.BlockSpec(memory_space=pl.ANY)
    return pl.pallas_call(
        kernel,
        out_shape=out_shape,
        in_specs=[spec] * len(arrays),
        out_specs=jax.tree.map(lambda _: spec, out_shape),
        scratch_shapes=scratch,
        compiler_params=pltpu.CompilerParams(
            collective_id=ident, has_side_effects=True, vmem_limit_bytes=(40 << 20) if vmem else None
        ),
        cost_estimate=pl.CostEstimate(
            flops=cost_us * 10**9, bytes_accessed=1 << 20, transcendentals=0
        ),
    )(*arrays)


LINE_FLIPS = [(1, 0, 0, 0), (2, 0, 0, 0), (3, 0, 0, 0)]


def line_start(me, ins, outs, sent, got):
    copies = []
    for i, (src, dst) in enumerate(zip(ins, outs)):
        for k, flip in enumerate(LINE_FLIPS):
            peer = turned(me, flip)
            copy = pltpu.make_async_remote_copy(
                src_ref=src if len(src.shape) == 2 else src.at[peer[0]],
                dst_ref=dst.at[k],
                send_sem=sent.at[i, k],
                recv_sem=got.at[i, k],
                device_id=device_of(peer),
                device_id_type=MESH,
            )
            copy.start()
            copies.append(copy)
    return copies


def line_shapes(arrays):
    return tuple(
        jax.ShapeDtypeStruct((3,) + (a.shape if a.ndim == 2 else a.shape[1:]), a.dtype)
        for a in arrays
    )


LEVELS = 32000.0


def line_pack(parts):
    tops = jnp.max(jnp.abs(parts), axis=2)
    codes = jnp.round(parts * (LEVELS / jnp.maximum(tops, 1e-30))[:, :, None]).astype(jnp.int32)
    half = parts.shape[1] // 2
    return tops, lax.shift_left(codes[:, :half], 16) | (codes[:, half:] & 65535)


def line_total(part, tops, words):
    z_at = lax.axis_index("z")
    total = lax.dynamic_index_in_dim(part, z_at, 0, keepdims=False)
    steps = lax.dynamic_index_in_dim(tops, z_at, 1, keepdims=False) * (1.0 / LEVELS)
    for k in range(3):
        high = lax.shift_right_arithmetic(words[k], 16)
        low = lax.shift_right_arithmetic(lax.shift_left(words[k], 16), 16)
        codes = jnp.concatenate([high, low], axis=0).astype(jnp.float32)
        total = total + codes * steps[k][:, None]
    return total


def putter(sent, got):
    count = [0]

    def put(src, dst, peer):
        at = count[0]
        count[0] += 1
        copy = pltpu.make_async_remote_copy(
            src_ref=src,
            dst_ref=dst,
            send_sem=sent.at[at],
            recv_sem=got.at[at],
            device_id=device_of(peer),
            device_id_type=MESH,
        )
        copy.start()
        return copy

    return put


def swap_flow(me, put, x_ref, o_ref, own):
    mine = rank_of(me)
    peers = [turned(me, flip) for flip in LAYER_FLIPS]
    copies = [put(x_ref.at[rank_of(peer)], o_ref.at[mine], peer) for peer in peers]
    local = pltpu.make_async_copy(x_ref.at[mine], o_ref.at[mine], own)
    local.start()
    yield
    local.wait()
    for copy in copies:
        copy.wait()


def gather_flow(me, put, x_ref, o_ref, own):
    half = x_ref.shape[0] // 2
    by_x, by_y, by_xy = (turned(me, (0, y, x, 0)) for y, x in ((0, 1), (1, 0), (1, 1)))
    other = turned(me, (0, 0, 0, 1))
    slot = o_ref.at[rank_of(me)]
    first, second = pl.ds(0, half), pl.ds(half, half)
    copies = [
        put(x_ref.at[first], slot.at[first], by_x),
        put(x_ref.at[second], slot.at[second], by_y),
        put(x_ref.at[second], slot.at[second], by_x),
        put(x_ref.at[first], slot.at[first], by_y),
        put(x_ref, slot, other),
    ]
    local = pltpu.make_async_copy(x_ref, slot, own)
    local.start()
    from_x, from_y, from_xy = (o_ref.at[rank_of(p)] for p in (by_x, by_y, by_xy))
    yield
    copies[0].wait_recv()
    copies.append(put(from_x.at[first], from_x.at[first], by_y))
    copies[1].wait_recv()
    copies.append(put(from_y.at[second], from_y.at[second], by_x))
    yield
    copies[2].wait_recv()
    copies.append(put(from_x, from_x, other))
    copies[3].wait_recv()
    copies.append(put(from_y, from_y, other))
    yield
    copies[5].wait_recv()
    copies[6].wait_recv()
    copies.append(put(from_xy, from_xy, other))
    local.wait()
    for i in (4, 7, 8, 9):
        copies[i].wait_recv()
    for copy in copies:
        copy.wait_send()


def encode(value, words, steps):
    half = value.shape[0] // 2
    top = jnp.max(jnp.abs(value), axis=1, keepdims=True)
    codes = jnp.round(value * (LEVELS / jnp.maximum(top, 1e-30))).astype(jnp.int32)
    words[...] = lax.shift_left(codes[:half], 16) | (codes[half:] & 65535)
    steps[...] = jnp.broadcast_to(top * (1.0 / LEVELS), steps.shape)


def decode(words, steps):
    values = words[...]
    high = lax.shift_right_arithmetic(values, 16)
    low = lax.shift_right_arithmetic(lax.shift_left(values, 16), 16)
    return jnp.concatenate([high, low], axis=0).astype(jnp.float32) * steps[:, 0:1]


def sum_flow(me, put, p_ref, o_ref, own, mine, theirs, out_words, out_steps, in_words, in_steps):
    half = mine.shape[1] // 2
    by_x, by_y = (turned(me, flip) for flip in ((0, 0, 1, 0), (0, 1, 0, 0)))
    other = turned(me, (0, 0, 0, 1))
    cores, locals_ = [], []
    for slot in (3, 2, 1, 0):
        chip = turned(me, (0, slot // 2, slot % 2, 0))
        local = pltpu.make_async_copy(p_ref.at[rank_of(chip)], mine.at[slot], own.at[slot])
        local.start()
        locals_.append(local)
        cores.append(put(p_ref.at[rank_of(turned(chip, (0, 0, 0, 1)))], theirs.at[slot], other))
    first, second = pl.ds(0, half), pl.ds(half, half)
    copies = []

    def pass_on(unit, slot, rows, peer):
        encode(mine[slot, rows, :], out_words.at[unit], out_steps.at[unit])
        copies.append(
            (
                put(out_words.at[unit], in_words.at[unit], peer),
                put(out_steps.at[unit], in_steps.at[unit], peer),
            )
        )

    def take_in(unit, slot, rows):
        for copy in copies[unit]:
            copy.wait_recv()
        mine[slot, rows, :] = mine[slot, rows, :] + decode(in_words.at[unit], in_steps.at[unit])

    for i, slot in enumerate((3, 2, 1, 0)):
        locals_[i].wait()
        cores[i].wait_recv()
        mine[slot] = mine[slot] + theirs[slot]
        if slot == 3:
            pass_on(0, 3, first, by_x)
            pass_on(1, 3, second, by_y)
        if slot == 2:
            pass_on(2, 2, second, by_y)
        if slot == 1:
            pass_on(3, 1, first, by_x)
    yield
    take_in(0, 2, first)
    pass_on(4, 2, first, by_y)
    take_in(1, 1, second)
    pass_on(5, 1, second, by_x)
    yield
    take_in(3, 0, first)
    take_in(2, 0, second)
    yield
    take_in(4, 0, first)
    take_in(5, 0, second)
    done = pltpu.make_async_copy(mine.at[0], o_ref, own.at[4])
    done.start()
    done.wait()
    for copy in cores + [copy for pair in copies for copy in pair]:
        copy.wait_send()


def everyone_flow(me, put, x_ref, o_ref, own):
    slot = o_ref.at[RANKS * me[0] + rank_of(me)]
    copies = [put(x_ref, slot, turned(me, flip)) for flip in ALL_FLIPS]
    local = pltpu.make_async_copy(x_ref, slot, own)
    local.start()
    yield
    local.wait()
    for copy in copies:
        copy.wait()


def down_owner(z_at, rank):
    block = 2 * RANKS * (z_at // 2) + 2 * rank + z_at % 2
    return block // RANKS, block % RANKS


def move_flow(me, x_ref, o_ref, sent, got, own):
    z_at, mine = me[0], rank_of(me)
    to_z, to_rank = down_owner(z_at, mine)
    stays = (to_z == z_at) & (to_rank == mine)
    remote = pltpu.make_async_remote_copy(
        src_ref=x_ref,
        dst_ref=o_ref,
        send_sem=sent,
        recv_sem=got,
        device_id=(to_z, to_rank // 4, to_rank % 4),
        device_id_type=MESH,
    )
    local = pltpu.make_async_copy(x_ref, o_ref, own)

    @pl.when(stays)
    def _():
        local.start()

    @pl.when(jnp.logical_not(stays))
    def _():
        remote.start()

    yield

    @pl.when(stays)
    def _():
        local.wait()

    @pl.when(jnp.logical_not(stays))
    def _():
        remote.wait()


ALL_FLIPS = [(z, y, x, c) for z in range(4) for y in range(2) for x in range(2) for c in range(2)][1:]


def plane_step(ident, cost_us, sums=(), gathers=(), swaps=(), everyone=(), moves=(), carry=()):
    n_sum, n_gather, n_swap, n_carry = len(sums), len(gathers), len(swaps), len(carry)
    n_all = len(everyone)
    n_move = len(moves)
    total = n_sum + n_gather + n_swap + n_all + n_move + n_carry
    f32 = jnp.float32
    n_put = 16 * n_sum + 10 * n_gather + 7 * n_swap + 31 * n_all + n_move

    def kernel(*refs):
        ins, outs, scratch = refs[:total], refs[total : 2 * total], refs[2 * total :]
        sent, got, own, line_sent, line_got = scratch[:5]
        me = place()
        if n_all:
            peers = [turned(me, flip) for flip in ALL_FLIPS]
        elif n_swap:
            peers = [turned(me, flip) for flip in LAYER_FLIPS]
        else:
            peers = [turned(me, flip) for flip in ((0, 0, 1, 0), (0, 1, 0, 0), (0, 0, 0, 1))]
        if n_carry and not n_all:
            peers = peers + [turned(me, flip) for flip in LINE_FLIPS]
        greet(peers)
        put = putter(sent, got)
        carried = line_start(me, ins[total - n_carry :], outs[total - n_carry :], line_sent, line_got)
        flows = []
        for i in range(total - n_carry):
            if i < n_sum:
                flows.append(
                    sum_flow(me, put, ins[i], outs[i], own.at[i], *scratch[5 + 6 * i : 11 + 6 * i])
                )
            elif i < n_sum + n_gather:
                flows.append(gather_flow(me, put, ins[i], outs[i], own.at[i, 0]))
            elif i >= n_sum + n_gather + n_swap + n_all:
                at = n_put - n_move + (i - (n_sum + n_gather + n_swap + n_all))
                flows.append(
                    move_flow(me, ins[i], outs[i], sent.at[at], got.at[at], own.at[i, 0])
                )
            elif i >= n_sum + n_gather + n_swap:
                flows.append(everyone_flow(me, put, ins[i], outs[i], own.at[i, 0]))
            else:
                flows.append(swap_flow(me, put, ins[i], outs[i], own.at[i, 0]))
        for _ in range(8):
            for flow in flows:
                next(flow, None)
        for copy in carried:
            copy.wait()

    dma = pltpu.SemaphoreType.DMA
    shape = jax.ShapeDtypeStruct
    outs = [shape(a.shape[1:], f32) for a in sums]
    outs += [shape((RANKS,) + a.shape, a.dtype) for a in gathers]
    outs += [shape(a.shape, a.dtype) for a in swaps]
    outs += [shape((len(ALL_FLIPS) + 1,) + a.shape, a.dtype) for a in everyone]
    outs += [shape(a.shape, a.dtype) for a in moves]
    scratch = [
        dma((n_put,)),
        dma((n_put,)),
        dma((total, 5)),
        dma((max(n_carry, 1), 3)),
        dma((max(n_carry, 1), 3)),
    ]
    for a in sums:
        rows, lanes = a.shape[1:]
        scratch += [
            pltpu.VMEM((4, rows, lanes), f32),
            pltpu.VMEM((4, rows, lanes), f32),
            pltpu.VMEM((6, rows // 4, lanes), jnp.int32),
            pltpu.VMEM((6, rows // 2, 128), f32),
            pltpu.VMEM((6, rows // 4, lanes), jnp.int32),
            pltpu.VMEM((6, rows // 2, 128), f32),
        ]
    return comm_call(
        kernel,
        tuple(outs) + line_shapes(carry),
        tuple(sums) + tuple(gathers) + tuple(swaps) + tuple(everyone) + tuple(moves) + tuple(carry),
        scratch,
        ident,
        vmem=bool(sums),
        cost_us=cost_us,
    )


def lanes_of(values):
    row = jnp.concatenate([jnp.stack(values), jnp.zeros((128 - len(values),), jnp.float32)])
    return jnp.broadcast_to(row[None, :], (8, 128))


def full_sum_steps(me, mine, theirs, in_a, in_b, in_c, in_d, in_z, put):
    z_at, y_at, x_at, core = me
    half = mine.shape[3] // 2
    first, second = pl.ds(0, half), pl.ds(half, half)
    by_x, by_y = (turned(me, flip) for flip in ((0, 0, 1, 0), (0, 1, 0, 0)))
    over_x = put(mine.at[1 - x_at, :, :, first], in_a, by_x)
    over_y = put(mine.at[:, 1 - y_at, :, second], in_b, by_y)
    over_x.wait_recv()
    mine[x_at, :, :, first] = mine[x_at, :, :, first] + in_a[...]
    next_y = put(mine.at[x_at, 1 - y_at, :, first], in_c, by_y)
    over_y.wait_recv()
    mine[:, y_at, :, second] = mine[:, y_at, :, second] + in_b[...]
    next_x = put(mine.at[1 - x_at, y_at, :, second], in_d, by_x)
    next_y.wait_recv()
    mine[x_at, y_at, :, first] = mine[x_at, y_at, :, first] + in_c[...]
    next_x.wait_recv()
    mine[x_at, y_at, :, second] = mine[x_at, y_at, :, second] + in_d[...]
    sends = []
    for k in (1, 2, 3):
        peer = turned(me, (k, 0, 0, 0))
        sends.append(put(mine.at[x_at, y_at, peer[0]], in_z.at[k - 1], peer))
    for send in sends:
        send.wait_recv()
    return mine[x_at, y_at, z_at] + in_z[0] + in_z[1] + in_z[2], [
        over_x,
        over_y,
        next_y,
        next_x,
    ] + sends


NEAR_FLIPS = [(0, 0, 0, 1), (0, 0, 1, 0), (0, 1, 0, 0), (1, 0, 0, 0), (2, 0, 0, 0), (3, 0, 0, 0)]


def full_scratch(rows, lanes):
    half = rows // 2
    f32 = jnp.float32
    return [
        pltpu.VMEM((2, 2, 4, rows, lanes), f32),
        pltpu.VMEM((2, 2, 4, rows, lanes), f32),
        pltpu.VMEM((2, 4, half, lanes), f32),
        pltpu.VMEM((2, 4, half, lanes), f32),
        pltpu.VMEM((4, half, lanes), f32),
        pltpu.VMEM((4, half, lanes), f32),
        pltpu.VMEM((3, rows, lanes), f32),
    ]


def full_start(p_ref, me, mine, theirs, own, put):
    core = me[3]
    local = pltpu.make_async_copy(p_ref.at[core], mine, own)
    local.start()
    swap = put(p_ref.at[1 - core], theirs, turned(me, (0, 0, 0, 1)))
    local.wait()
    swap.wait_recv()
    for x in range(2):
        for y in range(2):
            mine[x, y] = mine[x, y] + theirs[x, y]
    return swap


def full_scatter(parts, ident, carry):
    rows, lanes = parts.shape[4:]
    extra = len(carry)

    def kernel(p_ref, *refs):
        carry_in, o_ref, carry_out = refs[:extra], refs[extra], refs[extra + 1 : 2 * extra + 1]
        mine, theirs, in_a, in_b, in_c, in_d, in_z, total, sent, got, own, csent, cgot = refs[
            2 * extra + 1 :
        ]
        me = place()
        greet([turned(me, flip) for flip in NEAR_FLIPS])
        carried = line_start(me, carry_in, carry_out, csent, cgot)
        put = putter(sent, got)
        swap = full_start(p_ref, me, mine, theirs, own.at[0], put)
        value, copies = full_sum_steps(me, mine, theirs, in_a, in_b, in_c, in_d, in_z, put)
        total[...] = value
        done = pltpu.make_async_copy(total, o_ref, own.at[1])
        done.start()
        done.wait()
        for copy in [swap] + copies:
            copy.wait_send()
        for copy in carried:
            copy.wait()

    dma = pltpu.SemaphoreType.DMA
    return comm_call(
        kernel,
        (jax.ShapeDtypeStruct((rows, lanes), jnp.float32),) + line_shapes(carry),
        (parts,) + tuple(carry),
        full_scratch(rows, lanes)
        + [pltpu.VMEM((rows, lanes), jnp.float32), dma((8,)), dma((8,)), dma((2,))]
        + [dma((extra, 3))] * 2,
        ident,
        vmem=True,
        cost_us=40,
    )


def newton_pair(pair):
    wide = 2 * HEAD_DIM
    row = lax.broadcasted_iota(jnp.int32, (wide, wide), 0)
    lane = lax.broadcasted_iota(jnp.int32, (wide, wide), 1)
    same = (row < HEAD_DIM) == (lane < HEAD_DIM)
    gram = jnp.where(same, jnp.concatenate([pair, pair], axis=0), 0.0)
    diagonal = jnp.where(row == lane, gram, 0.0)
    lone = jnp.sum(jnp.where(row < HEAD_DIM, diagonal, 0.0), keepdims=True)
    ltwo = jnp.sum(jnp.where(row < HEAD_DIM, 0.0, diagonal), keepdims=True)
    norm_value = jnp.sqrt(jnp.where(row < HEAD_DIM, lone, ltwo)) + 1e-07
    product = gram / (norm_value * norm_value)
    eye = jnp.where(row == lane, 1.0, 0.0)

    def mul(left, right):
        return jnp.dot(left, right, precision=HIGHEST, preferred_element_type=jnp.float32)

    total = None
    for newton_step in range(5):
        mixer = NS_COEF[0] * eye + NS_COEF[1] * product + NS_COEF[2] * mul(product, product)
        total = mixer if total is None else mul(mixer, total)
        if newton_step < 4:
            product = mul(mul(mixer, product), mixer)
    total = total / norm_value
    return total[:HEAD_DIM] + total[HEAD_DIM:]


def full_newton(parts, ident):
    rows, lanes = parts.shape[4:]
    half = rows // 2

    def kernel(p_ref, o_ref, mine, theirs, in_a, in_b, in_c, in_d, in_z, whole, sent, got, own):
        me = place()
        z_at, y_at, x_at, core = me
        greet([turned(me, flip) for flip in NEAR_FLIPS])
        put = putter(sent, got)
        swap = full_start(p_ref, me, mine, theirs, own.at[0], put)
        value, copies = full_sum_steps(me, mine, theirs, in_a, in_b, in_c, in_d, in_z, put)
        for i in range(rows // HEAD_DIM):
            part = slice(i * HEAD_DIM, (i + 1) * HEAD_DIM)
            whole[core, x_at, y_at, z_at, pl.ds(i * HEAD_DIM, HEAD_DIM)] = newton_pair(value[part])
        first, second = pl.ds(0, half), pl.ds(half, half)
        by_x, by_y = (turned(me, flip) for flip in ((0, 0, 1, 0), (0, 1, 0, 0)))
        slot = whole.at[core, x_at, y_at, z_at]
        over_z = [put(slot, slot, turned(me, (k, 0, 0, 0))) for k in (1, 2, 3)]
        for copy in over_z:
            copy.wait_recv()
        part_a = whole.at[core, x_at, y_at, :, first]
        part_b = whole.at[core, x_at, y_at, :, second]
        over_x = put(part_a, part_a, by_x)
        over_y = put(part_b, part_b, by_y)
        over_x.wait_recv()
        part_a = whole.at[core, :, y_at, :, first]
        next_y = put(part_a, part_a, by_y)
        over_y.wait_recv()
        part_b = whole.at[core, x_at, :, :, second]
        next_x = put(part_b, part_b, by_x)
        next_y.wait_recv()
        next_x.wait_recv()
        last = put(whole.at[core], whole.at[core], turned(me, (0, 0, 0, 1)))
        last.wait_recv()
        done = pltpu.make_async_copy(whole, o_ref, own.at[1])
        done.start()
        done.wait()
        for copy in [swap] + copies + over_z + [over_x, over_y, next_y, next_x, last]:
            copy.wait_send()

    dma = pltpu.SemaphoreType.DMA
    return comm_call(
        kernel,
        jax.ShapeDtypeStruct(parts.shape, jnp.float32),
        (parts,),
        full_scratch(rows, lanes)
        + [pltpu.VMEM((2, 2, 2, 4, rows, lanes), jnp.float32), dma((16,)), dma((16,)), dma((2,))],
        ident,
        vmem=True,
    )


def setup_exchange(slab, swap, small, noisy, meta, ident):
    planes = 4
    flips_f = [flip for flip in LAYER_FLIPS if flip[1] == 0]

    def kernel(
        w_ref, c_ref, s_ref, n_ref, m_ref, wo, co, so, no, mo, s_mid, n_mid, sent, got, csent, cgot, own
    ):
        me = place()
        z_at, y_at, x_at, core = me
        mine = rank_of(me)
        f_at = 2 * x_at + core
        layer = [turned(me, flip) for flip in LAYER_FLIPS]
        line = [turned(me, (k, 0, 0, 0)) for k in (1, 2, 3)]
        greet(layer + line)
        put = putter(sent, got)
        locals_ = [
            pltpu.make_async_copy(w_ref.at[mine], wo.at[z_at, mine], own.at[0]),
            pltpu.make_async_copy(s_ref, s_mid.at[z_at], own.at[1]),
            pltpu.make_async_copy(n_ref, n_mid.at[y_at, f_at], own.at[2]),
            pltpu.make_async_copy(m_ref, mo.at[f_at], own.at[3]),
            pltpu.make_async_copy(c_ref.at[mine], co.at[mine], own.at[6]),
        ]
        for copy in locals_:
            copy.start()
        slabs = [put(w_ref.at[rank_of(peer)], wo.at[z_at, mine], peer) for peer in layer]
        small_line = [put(s_ref, s_mid.at[z_at], peer) for peer in line]
        metas = [put(m_ref, mo.at[f_at], turned(me, flip)) for flip in flips_f]
        noisies = [put(n_ref, n_mid.at[y_at, f_at], peer) for peer in layer]
        for copy in locals_:
            copy.wait()
        for copy in slabs:
            copy.wait_recv()

        def along(which, target, source, step):
            return pltpu.make_async_remote_copy(
                src_ref=wo.at[source],
                dst_ref=wo.at[source],
                send_sem=csent.at[which, step],
                recv_sem=cgot.at[which, step],
                device_id=device_of((target, y_at, x_at, core)),
                device_id_type=MESH,
            )

        def go(step):
            @pl.when((z_at < planes - 1) & (z_at >= step))
            def _():
                along(0, z_at + 1, z_at - step, step).start()

            @pl.when((z_at > 0) & (z_at + step < planes))
            def _():
                along(1, z_at - 1, z_at + step, step).start()

        def come(step):
            @pl.when(z_at >= step + 1)
            def _():
                along(0, z_at - 1, z_at - 1 - step, step).wait_recv()

            @pl.when(z_at + step + 1 < planes)
            def _():
                along(1, z_at + 1, z_at + 1 + step, step).wait_recv()

        go(0)
        for copy in small_line:
            copy.wait_recv()
        smalls = [put(s_mid, so.at[:, mine], peer) for peer in layer]
        small_own = pltpu.make_async_copy(s_mid, so.at[:, mine], own.at[4])
        small_own.start()
        for copy in noisies:
            copy.wait_recv()
        noisy_line = [put(n_mid.at[:, peer[0]], no.at[z_at], peer) for peer in line]
        noisy_own = pltpu.make_async_copy(n_mid.at[:, z_at], no.at[z_at], own.at[5])
        noisy_own.start()
        swaps = [put(c_ref.at[rank_of(peer)], co.at[mine], peer) for peer in layer]
        come(0)
        go(1)
        come(1)
        go(2)
        come(2)
        small_own.wait()
        noisy_own.wait()
        for copy in metas + smalls + noisy_line + swaps:
            copy.wait_recv()
        for copy in small_line + slabs + metas + noisies + smalls + noisy_line + swaps:
            copy.wait_send()
        for step in range(3):

            @pl.when((z_at < planes - 1) & (z_at >= step))
            def _():
                along(0, z_at + 1, z_at - step, step).wait_send()

            @pl.when((z_at > 0) & (z_at + step < planes))
            def _():
                along(1, z_at - 1, z_at + step, step).wait_send()

    dma = pltpu.SemaphoreType.DMA
    shape = jax.ShapeDtypeStruct
    return comm_call(
        kernel,
        (
            shape((planes,) + slab.shape, slab.dtype),
            shape(swap.shape, swap.dtype),
            shape((planes, RANKS) + small.shape, small.dtype),
            shape((planes, 2) + noisy.shape, noisy.dtype),
            shape((4,) + meta.shape, meta.dtype),
        ),
        (slab, swap, small, noisy, meta),
        [
            pltpu.VMEM((planes,) + small.shape, small.dtype),
            pltpu.VMEM((2, 4) + noisy.shape, noisy.dtype),
            dma((40,)),
            dma((40,)),
            dma((2, 3)),
            dma((2, 3)),
            dma((7,)),
        ],
        ident,
        vmem=True,
        cost_us=60,
    )


def swapped_halves(values):
    half_dim = values.shape[1] // 2
    return jnp.concatenate([values[:, half_dim:], values[:, :half_dim]], axis=1)


def attend_kernel(lengths_ref, qkv_ref, cos_ref, sin_ref, qr_ref, kr_ref, vr_ref, o_ref, low_ref, lse_ref):
    frames = qkv_ref.shape[1]
    length = lengths_ref[pl.program_id(0)]
    cosine, sine_table = cos_ref[...], sin_ref[...]
    chunk = 256
    live = lax.broadcasted_iota(jnp.int32, (chunk, frames), 1) < length
    for head in range(LOCAL_HEADS):
        at = slice(head * HEAD_DIM, (head + 1) * HEAD_DIM)

        def column(which):
            return qkv_ref[0, :, which * COLS + head * HEAD_DIM : which * COLS + (head + 1) * HEAD_DIM]

        query, key = column(0), column(1)
        queries = (query * cosine + swapped_halves(query) * sine_table).astype(LOW)
        keys = (key * cosine + swapped_halves(key) * sine_table).astype(LOW)
        values = column(2).astype(LOW)
        qr_ref[0, head] = queries
        kr_ref[0, head] = keys
        vr_ref[0, head] = values
        for part in range(frames // chunk):
            rows = slice(part * chunk, (part + 1) * chunk)
            scores = lax.dot_general(
                queries[rows], keys, (((1,), (1,)), ((), ())), preferred_element_type=jnp.float32
            ) * (1.0 / math.sqrt(HEAD_DIM))
            scores = jnp.where(live, scores, -1e30)
            top = jnp.max(scores, axis=1, keepdims=True)
            grown = jnp.exp(scores - top)
            total = jnp.sum(grown, axis=1, keepdims=True)
            weights = (grown * (1.0 / total)).astype(LOW)
            mixed = jnp.dot(weights, values, preferred_element_type=jnp.float32)
            o_ref[0, head, rows, :] = mixed
            span = low_ref.shape[2]
            for k in range(chunk // span):
                low_ref[part * (chunk // span) + k, 0, :, at] = mixed[
                    k * span : (k + 1) * span
                ].astype(LOW)
            lse_ref[0, head, rows, :] = top + jnp.log(total)


def attend(qkv, cosine, sine_table, lengths, span):
    count, frames, width = qkv.shape
    heads = pl.BlockSpec((1, LOCAL_HEADS, frames, HEAD_DIM), lambda i: (i, 0, 0, 0))
    table = pl.BlockSpec((frames, HEAD_DIM), lambda i: (0, 0))
    low = jax.ShapeDtypeStruct((count, LOCAL_HEADS, frames, HEAD_DIM), LOW)
    return pl.pallas_call(
        attend_kernel,
        grid=(count,),
        out_shape=(
            low,
            low,
            low,
            jax.ShapeDtypeStruct((count, LOCAL_HEADS, frames, HEAD_DIM), jnp.float32),
            jax.ShapeDtypeStruct((RANKS, count, span, COLS), LOW),
            jax.ShapeDtypeStruct((count, LOCAL_HEADS, frames, 1), jnp.float32),
        ),
        in_specs=[
            pl.BlockSpec(memory_space=pltpu.SMEM),
            pl.BlockSpec((1, frames, width), lambda i: (i, 0, 0)),
            table,
            table,
        ],
        out_specs=(
            heads,
            heads,
            heads,
            heads,
            pl.BlockSpec((RANKS, 1, span, COLS), lambda i: (0, i, 0, 0)),
            pl.BlockSpec((1, LOCAL_HEADS, frames, 1), lambda i: (i, 0, 0, 0)),
        ),
        compiler_params=pltpu.CompilerParams(vmem_limit_bytes=56 << 20),
        cost_estimate=pl.CostEstimate(
            flops=4 * count * frames * frames * COLS,
            bytes_accessed=10 * count * frames * COLS,
            transcendentals=count * LOCAL_HEADS * frames * frames,
        ),
    )(lengths, qkv, cosine, sine_table)


def attend_back_kernel(
    lengths_ref, q_ref, k_ref, v_ref, o_ref, lse_ref, do_ref, cos_ref, sin_ref, d_ref
):
    frames = q_ref.shape[2]
    length = lengths_ref[pl.program_id(0)]
    cosine, sine_table = cos_ref[...], sin_ref[...]
    chunk = 256
    scale = 1.0 / math.sqrt(HEAD_DIM)
    span = do_ref.shape[2]
    live = lax.broadcasted_iota(jnp.int32, (chunk, frames), 1) < length
    for head in range(LOCAL_HEADS):
        at = slice(head * HEAD_DIM, (head + 1) * HEAD_DIM)
        keys = k_ref[0, head]
        values = v_ref[0, head]
        grad_key = jnp.zeros((frames, HEAD_DIM), jnp.float32)
        grad_value = jnp.zeros((frames, HEAD_DIM), jnp.float32)
        for part in range(frames // chunk):
            rows = slice(part * chunk, (part + 1) * chunk)
            queries = q_ref[0, head, rows, :]
            grads = jnp.concatenate(
                [
                    do_ref[part * (chunk // span) + k, 0, :, at]
                    for k in range(chunk // span)
                ],
                axis=0,
            )
            scores = (
                lax.dot_general(
                    queries, keys, (((1,), (1,)), ((), ())), preferred_element_type=jnp.float32
                )
                * scale
            )
            scores = jnp.where(live, scores, -1e30)
            weights = jnp.exp(scores - lse_ref[0, head, rows, :])
            delta = jnp.sum(
                grads.astype(jnp.float32) * o_ref[0, head, rows, :], axis=1, keepdims=True
            )
            pulled = lax.dot_general(
                grads, values, (((1,), (1,)), ((), ())), preferred_element_type=jnp.float32
            )
            pushed = (weights * (pulled - delta)).astype(LOW)
            grad_query = jnp.dot(pushed, keys, preferred_element_type=jnp.float32) * scale
            grad_key = grad_key + rows_product(pushed, queries)
            grad_value = grad_value + rows_product(weights.astype(LOW), grads)
            d_ref[0, rows, head * HEAD_DIM : (head + 1) * HEAD_DIM] = (
                grad_query * cosine[rows] - swapped_halves(grad_query) * sine_table[rows]
            ).astype(LOW)
        grad_key = grad_key * scale
        d_ref[0, :, COLS + head * HEAD_DIM : COLS + (head + 1) * HEAD_DIM] = (
            grad_key * cosine - swapped_halves(grad_key) * sine_table
        ).astype(LOW)
        d_ref[0, :, 2 * COLS + head * HEAD_DIM : 2 * COLS + (head + 1) * HEAD_DIM] = (
            grad_value.astype(LOW)
        )


def attend_back(queries, key_rows, values, mixed, log_total, grads, cosine, sine_table, lengths):
    count, heads_here, frames, width = queries.shape
    span = grads.shape[2]
    heads = pl.BlockSpec((1, heads_here, frames, width), lambda i: (i, 0, 0, 0))
    table = pl.BlockSpec((frames, width), lambda i: (0, 0))
    return pl.pallas_call(
        attend_back_kernel,
        grid=(count,),
        out_shape=jax.ShapeDtypeStruct((count, frames, 3 * COLS), LOW),
        in_specs=[
            pl.BlockSpec(memory_space=pltpu.SMEM),
            heads,
            heads,
            heads,
            heads,
            pl.BlockSpec((1, heads_here, frames, 1), lambda i: (i, 0, 0, 0)),
            pl.BlockSpec((RANKS, 1, span, COLS), lambda i: (0, i, 0, 0)),
            table,
            table,
        ],
        out_specs=pl.BlockSpec((1, frames, 3 * COLS), lambda i: (i, 0, 0)),
        compiler_params=pltpu.CompilerParams(vmem_limit_bytes=56 << 20),
        cost_estimate=pl.CostEstimate(
            flops=10 * count * frames * frames * COLS,
            bytes_accessed=24 * count * frames * COLS,
            transcendentals=count * heads_here * frames * frames,
        ),
    )(lengths, queries, key_rows, values, mixed, log_total, grads, cosine, sine_table)


def first_state(noisy_ref, win_ref, timed_ref):
    hidden = jnp.dot(noisy_ref[...], win_ref[...], preferred_element_type=jnp.float32) + timed_ref[0]
    centred = hidden - jnp.mean(hidden, axis=1, keepdims=True)
    spread = lax.rsqrt(jnp.mean(centred * centred, axis=1, keepdims=True) + 1e-05)
    return centred * spread, spread


def first_kernel(noisy_ref, win_ref, timed_ref, norm_ref, w_ref, qkv_ref):
    unit, _ = first_state(noisy_ref, win_ref, timed_ref)
    normed = (unit * norm_ref[0:1] + norm_ref[1:2]).astype(LOW)
    qkv_ref[...] = jnp.dot(normed, w_ref[...], preferred_element_type=jnp.float32)


def first_back_kernel(
    items, noisy_ref, win_ref, timed_ref, norm_ref, w_ref, d_ref, dw_ref, in_ref, rows_ref
):
    step = pl.program_id(0)

    @pl.when(step == 0)
    def _():
        dw_ref[...] = jnp.zeros_like(dw_ref)
        in_ref[...] = jnp.zeros_like(in_ref)
        rows_ref[...] = jnp.zeros_like(rows_ref)

    unit, spread = first_state(noisy_ref, win_ref, timed_ref)
    gain = norm_ref[0:1]
    grads = d_ref[...]
    dw_ref[...] += rows_product((unit * gain + norm_ref[1:2]).astype(LOW), grads)
    grad_normed = times_transposed(grads, w_ref[...])
    scaled = grad_normed * gain
    grad_hidden = spread * (
        scaled
        - jnp.mean(scaled, axis=1, keepdims=True)
        - unit * jnp.mean(scaled * unit, axis=1, keepdims=True)
    )
    high = grad_hidden.astype(LOW)
    low = (grad_hidden - high.astype(jnp.float32)).astype(LOW)
    in_ref[...] += rows_product(noisy_ref[...], high) + rows_product(noisy_ref[...], low)
    item = step // (pl.num_programs(0) // items)
    at = lax.broadcasted_iota(jnp.int32, rows_ref.shape, 0)
    rows_ref[...] += (
        jnp.where(at == 0, jnp.sum(grad_normed * unit, axis=0, keepdims=True), 0.0)
        + jnp.where(at == 1, jnp.sum(grad_normed, axis=0, keepdims=True), 0.0)
        + jnp.where(at == 2 + item, jnp.sum(grad_hidden, axis=0, keepdims=True), 0.0)
    )


def first_specs(noisy, timed, weight):
    tokens, latent_dim = noisy.shape
    items = timed.shape[0]
    block = 256
    each = tokens // items // block
    rows = lambda lanes: pl.BlockSpec((block, lanes), lambda i: (i, 0))
    whole = lambda shape: pl.BlockSpec(shape, lambda i: (0, 0))
    specs = [
        rows(latent_dim),
        whole((latent_dim, D)),
        pl.BlockSpec((1, 1, D), lambda i: (i // each, 0, 0)),
        whole((2, D)),
        whole(weight.shape),
    ]
    return tokens // block, rows, whole, specs


def first_forward(noisy, win, timed, norm, weight):
    steps, rows, _, specs = first_specs(noisy, timed, weight)
    width = weight.shape[1]
    return pl.pallas_call(
        first_kernel,
        grid=(steps,),
        out_shape=jax.ShapeDtypeStruct((noisy.shape[0], width), jnp.float32),
        in_specs=specs,
        out_specs=rows(width),
        compiler_params=pltpu.CompilerParams(vmem_limit_bytes=40 << 20),
        cost_estimate=pl.CostEstimate(
            flops=2 * noisy.shape[0] * D * width, bytes_accessed=8 << 20, transcendentals=0
        ),
    )(noisy, win, timed, norm, weight)


def first_backward(noisy, win, timed, norm, weight, grads):
    steps, rows, whole, specs = first_specs(noisy, timed, weight)
    width = weight.shape[1]
    f32 = jnp.float32
    return pl.pallas_call(
        functools.partial(first_back_kernel, timed.shape[0]),
        grid=(steps,),
        out_shape=(
            jax.ShapeDtypeStruct((D, width), f32),
            jax.ShapeDtypeStruct((noisy.shape[1], D), f32),
            jax.ShapeDtypeStruct((8, D), f32),
        ),
        in_specs=specs + [rows(width)],
        out_specs=(whole((D, width)), whole((noisy.shape[1], D)), whole((8, D))),
        compiler_params=pltpu.CompilerParams(vmem_limit_bytes=40 << 20),
        cost_estimate=pl.CostEstimate(
            flops=8 * noisy.shape[0] * D * width, bytes_accessed=8 << 20, transcendentals=0
        ),
    )(noisy, win, timed, norm, weight, grads)


def cross_probs(query, key):
    scores = lax.dot_general(
        query, key, (((1,), (1,)), ((), ())), preferred_element_type=jnp.float32
    ) * (1.0 / math.sqrt(HEAD_DIM))
    grown = jnp.exp(scores - jnp.max(scores, axis=1, keepdims=True))
    return grown / jnp.sum(grown, axis=1, keepdims=True)


def cross_kernel(q_ref, pair_ref, two_ref, self_ref, o_ref, *by_owner):
    for head in range(HEADS):
        rank, local = head // LOCAL_HEADS, head % LOCAL_HEADS
        at = slice(head * HEAD_DIM, (head + 1) * HEAD_DIM)
        own = slice(local * HEAD_DIM, (local + 1) * HEAD_DIM)
        probs = cross_probs(q_ref[0, :, at], pair_ref[rank, 0, 0, :, own]).astype(LOW)
        o_ref[0, :, at] = jnp.dot(
            probs, pair_ref[rank, 1, 0, :, own], preferred_element_type=jnp.float32
        ).astype(LOW)
    planes = 4
    share = D // (planes * RANKS)
    for x_ref, out_ref in zip((self_ref, two_ref, o_ref), by_owner):
        for rank in range(RANKS):
            out_ref[rank, 0] = jnp.concatenate(
                [
                    x_ref[0, :, (plane * RANKS + rank) * share : (plane * RANKS + rank + 1) * share]
                    for plane in range(planes)
                ],
                axis=1,
            )


def cross_back_kernel(q_ref, pair_ref, do_ref, dq_ref, dpair_ref):
    scale = 1.0 / math.sqrt(HEAD_DIM)
    for head in range(HEADS):
        rank, local = head // LOCAL_HEADS, head % LOCAL_HEADS
        at = slice(head * HEAD_DIM, (head + 1) * HEAD_DIM)
        own = slice(local * HEAD_DIM, (local + 1) * HEAD_DIM)
        query, grads = q_ref[0, :, at], do_ref[0, :, at]
        key = pair_ref[rank, 0, 0, :, own]
        probs = cross_probs(query, key)
        pulled = lax.dot_general(
            grads,
            pair_ref[rank, 1, 0, :, own],
            (((1,), (1,)), ((), ())),
            preferred_element_type=jnp.float32,
        )
        delta = jnp.sum(probs * pulled, axis=1, keepdims=True)
        pushed = (probs * (pulled - delta)).astype(LOW)
        dq_ref[0, :, at] = (
            jnp.dot(pushed, key, preferred_element_type=jnp.float32) * scale
        ).astype(LOW)
        dpair_ref[rank, 0, 0, :, own] = rows_product(pushed, query) * scale
        dpair_ref[rank, 1, 0, :, own] = rows_product(probs.astype(LOW), grads)


def cross_specs(count, span, context_len):
    rows = pl.BlockSpec((1, span, D), lambda i: (i, 0, 0))
    pair = pl.BlockSpec((RANKS, 2, 1, context_len, COLS), lambda i: (0, 0, i, 0, 0))
    cost = pl.CostEstimate(
        flops=10 * count * span * context_len * D,
        bytes_accessed=8 * count * span * D,
        transcendentals=count * HEADS * span * context_len,
    )
    return rows, pair, cost


def cross_forward(queries, pair, two, own):
    count, span, _ = queries.shape
    rows, pair_spec, cost = cross_specs(count, span, pair.shape[3])
    owned = jax.ShapeDtypeStruct((RANKS, count, span, COLS), LOW)
    return pl.pallas_call(
        cross_kernel,
        grid=(count,),
        out_shape=(jax.ShapeDtypeStruct(queries.shape, LOW),) + (owned,) * 3,
        in_specs=[rows, pair_spec, rows, rows],
        out_specs=(rows,) + (pl.BlockSpec((RANKS, 1, span, COLS), lambda i: (0, i, 0, 0)),) * 3,
        compiler_params=pltpu.CompilerParams(vmem_limit_bytes=40 << 20),
        cost_estimate=cost,
    )(queries, pair, two, own)


def cross_backward(queries, pair, grads):
    count, span, _ = queries.shape
    rows, pair_spec, cost = cross_specs(count, span, pair.shape[3])
    return pl.pallas_call(
        cross_back_kernel,
        grid=(count,),
        out_shape=(
            jax.ShapeDtypeStruct(queries.shape, LOW),
            jax.ShapeDtypeStruct(pair.shape, jnp.float32),
        ),
        in_specs=[rows, pair_spec, rows],
        out_specs=(rows, pair_spec),
        compiler_params=pltpu.CompilerParams(vmem_limit_bytes=40 << 20),
        cost_estimate=cost,
    )(queries, pair, grads)


def fast_body(
    latents,
    gaussian_noise,
    timesteps,
    lengths,
    buckets,
    context,
    attention_weights,
    attention_moment,
    cross_weights,
    cross_moment,
    gate_up_weights,
    gate_up_first,
    gate_up_second,
    down_weights,
    down_first,
    down_second,
    latent_weights,
    latent_first,
    latent_second,
    timing_weights,
    timing_first,
    timing_second,
    norm_params,
    norm_first,
    norm_second,
):
    f32 = jnp.float32
    planes = lax.axis_size("z")
    z_at = lax.axis_index("z")
    rank = lax.axis_index("y") * lax.axis_size("f") + lax.axis_index("f")
    item_count, span, latent_dim = latents.shape
    frames = span * RANKS
    tokens = item_count * span
    group_tokens = item_count * frames
    flip = lambda array: jnp.swapaxes(array, 1, 2)

    attention_t = flip(attention_weights)
    cross_t = flip(cross_weights)
    attention_low = attention_t.astype(LOW)
    cross_low_t = cross_t.astype(LOW)
    small_low = jnp.concatenate(
        [
            latent_weights.reshape(-1, latent_weights.shape[2]),
            timing_weights,
            norm_params,
        ],
        axis=0,
    ).T.astype(LOW)
    signal = jnp.cos(0.5 * math.pi * timesteps)[:, None, None]
    noise_level = jnp.sin(0.5 * math.pi * timesteps)[:, None, None]
    noisy_own = (signal * latents + noise_level * gaussian_noise).astype(LOW)
    target_own = signal * gaussian_noise - noise_level * latents
    local_meta = jnp.stack([timesteps, lengths.astype(f32), buckets.astype(f32)])
    slab_of = lambda array: jnp.swapaxes(array.reshape(-1, RANKS, COLS), 0, 1)
    slab_all, cross_slab, small_all, noisy_all, meta_all = setup_exchange(
        slab_of(attention_low[:3]),
        slab_of(cross_low_t),
        small_low,
        noisy_own.reshape(-1, latent_dim),
        jnp.pad(local_meta, ((0, 5), (0, 128 - item_count))),
        16,
    )
    attention_rest, slab_all = lax.optimization_barrier((attention_low[3:], slab_all))
    small_all = small_all.reshape(D, -1)
    latent_in = small_all[:, :LAT].T
    latent_out = small_all[:, LAT : 2 * LAT].T
    timing = small_all[:, 2 * LAT : 2 * LAT + FOUR].T
    norms = small_all[:, 2 * LAT + FOUR :].astype(f32).T
    qkv_slab = slab_all.reshape(planes * RANKS, 3, -1, COLS)
    qkv_t = jnp.concatenate([qkv_slab[:, i].reshape(D, COLS) for i in range(3)], axis=1)
    meta = jnp.swapaxes(meta_all[:, :3, :item_count], 0, 1).reshape(3, -1)
    times_all = meta[0]
    lengths_all = meta[1]
    onehot_all = (meta[2][:, None] == jnp.arange(NBUCK, dtype=f32)[None, :]).astype(f32)
    counts = jnp.dot(lengths_all, onehot_all, precision=HIGHEST)
    present = jnp.sum((counts > 0).astype(f32))
    bucket_scale = 1.0 / (present * LAT * jnp.maximum(counts, 1.0))
    own_at = z_at * item_count
    onehot = lax.dynamic_slice_in_dim(onehot_all, own_at, item_count, 0)
    item_scale = jnp.dot(onehot, bucket_scale, precision=HIGHEST)
    own_lengths = lax.dynamic_slice_in_dim(lengths_all, own_at, item_count, 0).astype(jnp.int32)
    features_all = time_features(times_all).astype(LOW)
    features = lax.dynamic_slice_in_dim(features_all, own_at, item_count, 0)

    noisy_low = jnp.swapaxes(
        noisy_all.reshape(RANKS, item_count, span, latent_dim), 0, 1
    ).reshape(item_count, frames, latent_dim)
    target = lax.ppermute(
        target_own, ALL, [(4 * s + g, RANKS * g + s) for s in range(RANKS) for g in range(planes)]
    ).reshape(tokens, latent_dim)
    context_all = lax.all_gather(context, "f", axis=0, tiled=True)
    context_own = lax.dynamic_slice_in_dim(context_all, own_at, item_count, 0).reshape(-1, E)
    context_len = context.shape[1]

    rest_t = lax.all_gather(attention_rest, ALL, axis=1, tiled=True)
    gate_up = lax.all_gather(gate_up_weights.astype(LOW), "z", axis=0, tiled=True)
    down_pairs = []
    for p in range(planes):
        for r in range(RANKS):
            down_pairs.append((2 * RANKS * (p // 2) + 2 * r + p % 2, RANKS * p + r))
    down = lax.all_gather(
        lax.ppermute(down_weights.astype(LOW), ALL, down_pairs), "z", axis=0, tiled=True
    )

    half_dim = HEAD_DIM // 2
    inverse = 10000.0 ** (-jnp.arange(half_dim, dtype=f32) / half_dim)
    angles = jnp.arange(frames, dtype=f32)[:, None] * inverse[None, :]
    cosine = jnp.concatenate([jnp.cos(angles)] * 2, axis=1)
    sine_table = jnp.concatenate([-jnp.sin(angles), jnp.sin(angles)], axis=1)

    timed = matmul_low(features, timing)
    noisy_mine = lax.dynamic_slice_in_dim(noisy_low, rank * span, span, 1)
    start_own = (
        matmul_low(noisy_mine.reshape(tokens, latent_dim), latent_in).reshape(item_count, span, D)
        + timed[:, None, :]
    ).reshape(tokens, D)
    noisy_mine = noisy_mine.reshape(tokens, latent_dim)
    first = (
        noisy_low.reshape(group_tokens, latent_dim),
        latent_in,
        timed[:, None, :],
        norms[:2],
        qkv_t,
    )
    queries, key_rows, values, mixed, mixed_heads, log_total = attend(
        first_forward(*first).reshape(item_count, frames, 3 * COLS),
        cosine,
        sine_table,
        own_lengths,
        span,
    )
    mixed_heads = mixed_heads.reshape(RANKS, tokens, COLS)
    cross_slab = cross_slab.reshape(-1, COLS)
    mixed_low, cross_slabs = plane_step(1, 25, swaps=[mixed_heads], carry=[cross_slab])
    mixed_low = jnp.swapaxes(mixed_low, 0, 1).reshape(tokens, D)
    cross_slabs = jnp.concatenate([cross_slab[None], cross_slabs], axis=0)
    cross_slabs = jnp.take(cross_slabs, jnp.arange(planes) ^ z_at, axis=0, mode="clip")
    cross_slabs = cross_slabs.reshape(planes * RANKS, 2, -1, COLS)
    cross_w = [cross_slabs[:, i].reshape(E, COLS) for i in range(2)]
    after_self = start_own + matmul_low(mixed_low, rest_t[0])
    normed_two, back_two = jax.vjp(layer_norm, after_self, norms[2], norms[3])
    normed_two = normed_two.astype(LOW)
    cross_query = matmul_low(normed_two, rest_t[1]).astype(LOW).reshape(item_count, span, D)
    pair_own = jnp.stack(
        [matmul_low(context_own, cross_w[0]), matmul_low(context_own, cross_w[1])]
    ).astype(LOW)
    (pair_all,) = plane_step(3, 12, gathers=[pair_own.reshape(-1, COLS)])
    pair_all = pair_all.reshape(RANKS, 2, item_count, context_len, COLS)
    cross_out, *owned = cross_forward(
        cross_query,
        pair_all,
        normed_two.reshape(item_count, span, D),
        mixed_low.reshape(item_count, span, D),
    )
    cross_out = cross_out.reshape(tokens, D)
    owned = [array.reshape(RANKS, tokens, COLS) for array in owned]
    after_cross = after_self + matmul_low(cross_out, rest_t[2])
    normed_three, back_three = jax.vjp(layer_norm, after_cross, norms[4], norms[5])
    normed_three = normed_three.astype(LOW)
    normed_group, self_heads, two_heads, out_heads = plane_step(
        4, 70, gathers=[normed_three], swaps=owned
    )
    normed_group = normed_group.reshape(group_tokens, D)
    gate_both = times_transposed(normed_group, gate_up)
    units = gate_both.shape[1] // 2
    gate_half, up_half = (gate_both[:, :units], gate_both[:, units:])
    inner_act = (jax.nn.silu(gate_half) * up_half).astype(LOW)
    final_state = (
        after_cross
        + plane_step(5, 65, sums=[matmul_low(inner_act, down).reshape(RANKS, tokens, D)])[0]
    ).astype(LOW)
    predicted = times_transposed(final_state, latent_out)

    position = rank * span + jnp.arange(span)
    live_mask = position[None, :] < own_lengths[:, None]
    difference = predicted - target
    errors = jnp.sum(difference * difference, axis=1).reshape(item_count, span)
    per_item = jnp.sum(jnp.where(live_mask, errors, 0.0), axis=1)
    partial_loss = jnp.sum(per_item * item_scale)
    frame_scale = jnp.where(live_mask, item_scale[:, None], 0.0).reshape(tokens, 1)
    grad_pred = (2.0 * difference * frame_scale).astype(LOW)

    grad_out_proj = rows_product(grad_pred, final_state)
    grad_state = matmul_low(grad_pred, latent_out)
    (grad_group,) = plane_step(6, 30, gathers=[grad_state.astype(LOW)])
    grad_group = grad_group.reshape(group_tokens, D)
    down_part = rows_product(inner_act, grad_group)
    grad_inner = times_transposed(grad_group, down)
    sigmoid_gate = jax.nn.sigmoid(gate_half)
    grad_gate = grad_inner * up_half * sigmoid_gate * (1.0 + gate_half * (1.0 - sigmoid_gate))
    grad_both = jnp.concatenate([grad_gate, grad_inner * gate_half * sigmoid_gate], axis=1).astype(
        LOW
    )
    gate_up_part = rows_product(grad_both, normed_group)
    gate_up_part = gate_up_part.reshape(planes, -1, D)
    early = gate_up_part.shape[1] // 3
    early_tops, early_words = line_pack(gate_up_part[:, :early])
    late_tops, late_words = line_pack(gate_up_part[:, early:])
    grad_three, early_tops, early_words = plane_step(
        8,
        65,
        sums=[matmul_low(grad_both, gate_up).reshape(RANKS, tokens, D)],
        carry=[early_tops, early_words],
    )
    residual_part, gain_three, shift_three = back_three(grad_three)
    grad_state = grad_state + residual_part
    grad_branch = grad_state.astype(LOW)
    cross_branch = grad_branch
    grad_mix = times_transposed(grad_branch, rest_t[2]).astype(LOW).reshape(item_count, span, D)
    grad_cross_query, grad_pair = cross_backward(cross_query, pair_all, grad_mix)
    grad_cross_query = grad_cross_query.reshape(tokens, D)
    (
        grad_pair,
        cross_branch,
        query_branch,
        late_tops,
        late_words,
    ) = plane_step(
        9,
        90,
        sums=[grad_pair.reshape(RANKS, -1, COLS)],
        gathers=[cross_branch, grad_cross_query],
        carry=[late_tops, late_words],
    )
    down_part, grad_pair = lax.optimization_barrier((down_part, grad_pair))
    down_sum = lax.psum_scatter(down_part, "z", scatter_dimension=0, tiled=True)
    gate_up_grad = jnp.concatenate(
        [
            line_total(gate_up_part[:, :early], early_tops, early_words),
            line_total(gate_up_part[:, early:], late_tops, late_words),
        ],
        axis=0,
    )
    grad_pair = grad_pair.reshape(2, item_count * context_len, COLS)
    cross_part = rows_precise(
        context_own.astype(f32), jnp.concatenate([grad_pair[0], grad_pair[1]], axis=1)
    ).reshape(planes, -1, 2 * COLS)
    by_plane = lambda parts: parts.reshape(planes, -1, D)
    cross_out_part = by_plane(
        rows_product(out_heads.reshape(group_tokens, COLS), cross_branch.reshape(group_tokens, D))
    )
    cross_q_part = by_plane(
        rows_product(two_heads.reshape(group_tokens, COLS), query_branch.reshape(group_tokens, D))
    )
    residual_part, gain_two, shift_two = back_two(times_transposed(grad_cross_query, rest_t[1]))
    grad_state = grad_state + residual_part
    grad_branch = grad_state.astype(LOW)
    (
        branch_group,
        cq_tops,
        cq_words,
        co_tops,
        co_words,
        cross_tops,
        cross_words,
    ) = plane_step(
        2,
        35,
        gathers=[grad_branch],
        carry=line_pack(cross_q_part) + line_pack(cross_out_part) + line_pack(cross_part),
    )
    branch_group = branch_group.reshape(group_tokens, D)
    cross_sums = jnp.stack(
        [
            line_total(cross_q_part, cq_tops, cq_words),
            line_total(cross_out_part, co_tops, co_words),
        ]
    )
    out_rows = lax.dynamic_slice_in_dim(rest_t[0], rank * COLS, COLS, 0)
    self_out_sum = lax.psum_scatter(
        rows_product(self_heads.reshape(group_tokens, COLS), branch_group),
        "z",
        scatter_dimension=0,
        tiled=True,
    )
    grad_mixed = times_transposed(branch_group, out_rows).astype(LOW)
    grad_triple = attend_back(
        queries,
        key_rows,
        values,
        mixed,
        log_total,
        grad_mixed.reshape(RANKS, item_count, span, COLS),
        cosine,
        sine_table,
        own_lengths,
    ).reshape(group_tokens, 3 * COLS)
    qkv_part, grad_in_proj, first_rows = first_backward(*first, grad_triple)
    qkv_part = qkv_part.reshape(planes, -1, 3 * COLS)
    gain_one, shift_one = (first_rows[0], first_rows[1])
    grad_in_proj = grad_in_proj + rows_precise(noisy_mine.astype(f32), grad_state)
    grad_timed = first_rows[2 : 2 + item_count] + jnp.sum(
        grad_state.reshape(item_count, span, D), axis=1
    )
    timed_slots = lax.dynamic_update_slice(
        jnp.zeros((item_count * planes, D), f32), grad_timed, (own_at, 0)
    )
    small_grad = jnp.concatenate(
        [
            grad_in_proj,
            grad_out_proj,
            timed_slots,
            jnp.stack([gain_one, shift_one, gain_two, shift_two, gain_three, shift_three]),
            jnp.zeros((2, D), f32),
        ],
        axis=0,
    )
    small_grad, down_sum, self_out_sum = lax.optimization_barrier(
        (small_grad, down_sum, self_out_sum)
    )
    by_target = small_grad.T.reshape(planes, 2, 2, 2, -1, small_grad.shape[0])
    small_grad, qkv_tops, qkv_words = full_scatter(
        jnp.transpose(by_target, (3, 2, 1, 0, 4, 5)),
        17,
        line_pack(qkv_part),
    )
    small_grad = small_grad.T
    rest_grad = jnp.concatenate([self_out_sum[None], cross_sums], axis=0)
    qkv_grad = line_total(qkv_part, qkv_tops, qkv_words)
    cross_grad = line_total(cross_part, cross_tops, cross_words)
    latent_grad = small_grad[: 2 * LAT].reshape(2, LAT, -1)
    timed_end = 2 * LAT + timed_slots.shape[0]
    norm_grad = small_grad[timed_end : timed_end + 6]
    timing_grad = rows_precise(features_all.astype(f32), small_grad[2 * LAT : timed_end])
    everything = (
        qkv_grad,
        self_out_sum,
        cross_sums,
        cross_grad,
        latent_grad,
        timing_grad,
        norm_grad,
        gate_up_grad,
        down_sum,
    )
    squares = sum((jnp.sum(grad * grad) for grad in everything))
    down_tops, down_words = line_pack(down_sum[None])
    qkv_grad, cross_grad, totals, down_tops, down_words = plane_step(
        14,
        30,
        swaps=[
            qkv_grad.reshape(RANKS, -1, 3 * COLS),
            cross_grad.reshape(RANKS, -1, 2 * COLS),
        ],
        everyone=[lanes_of([squares, partial_loss])],
        moves=[down_tops, down_words[0]],
    )
    down_grad = jnp.concatenate(
        [
            lax.shift_right_arithmetic(down_words, 16),
            lax.shift_right_arithmetic(lax.shift_left(down_words, 16), 16),
        ],
        axis=0,
    ).astype(f32) * (down_tops[0] * (1.0 / LEVELS))[:, None]
    totals = jnp.sum(totals, axis=0)
    squares, loss_value = (totals[0, 0], totals[0, 1])
    qkv_grad = jnp.transpose(qkv_grad.reshape(RANKS, -1, 3, COLS), (2, 1, 0, 3)).reshape(3, -1, D)
    cross_grad = jnp.transpose(cross_grad.reshape(RANKS, -1, 2, COLS), (2, 1, 0, 3)).reshape(
        2, -1, D
    )
    attention_grad = jnp.concatenate([qkv_grad, rest_grad], axis=0)

    clip_norm = jnp.sqrt(squares)
    factor = CLIP_AT / jnp.maximum(clip_norm, CLIP_AT)

    moment_t = 0.95 * flip(attention_moment) + attention_grad * factor
    cross_moment_t = 0.95 * flip(cross_moment) + cross_grad * factor
    pair = 2 * HEAD_DIM
    blocks = [
        moment.reshape(moment.shape[0], moment.shape[1], D // pair, pair)
        for moment in (moment_t, cross_moment_t)
    ]
    left_lane = jnp.arange(pair) < HEAD_DIM
    grams = jnp.concatenate(
        [
            jnp.einsum("skbi,skbj->sbij", block, block, precision=HIGHEST).reshape(-1, pair, pair)
            for block in blocks
        ]
    )
    grams = jnp.where(left_lane, grams[:, :HEAD_DIM], grams[:, HEAD_DIM:])
    mixers = full_newton(grams.reshape(2, 2, 2, planes, -1, pair), 18)
    mixers = mixers.reshape(-1, D // pair, HEAD_DIM, pair)
    mixers = jnp.concatenate(
        [jnp.where(left_lane, mixers, 0.0), jnp.where(left_lane, 0.0, mixers)], axis=2
    )
    stacks = attention_t.shape[0]
    orth = [
        jnp.einsum("skbj,sbji->skbi", block, mixer, precision=HIGHEST).reshape(moment.shape)
        for block, mixer, moment in zip(
            blocks, (mixers[:stacks], mixers[stacks:]), (moment_t, cross_moment_t)
        )
    ]
    attention_new = attention_t * (1.0 - MUON_RATE * DECAY_RATE) - MUON_RATE * orth[0]
    cross_new = cross_t * (1.0 - MUON_RATE * DECAY_RATE) - MUON_RATE * orth[1]
    gate_up_new, gate_up_first_new, gate_up_second_new = adam_update(
        gate_up_weights, gate_up_first, gate_up_second, gate_up_grad * factor, ADAM_RATE, DECAY_RATE
    )
    down_new, down_first_new, down_second_new = adam_update(
        down_weights, down_first, down_second, down_grad * factor, ADAM_RATE, DECAY_RATE
    )
    latent_new, latent_first_new, latent_second_new = adam_update(
        latent_weights, latent_first, latent_second, latent_grad * factor, ADAM_RATE, DECAY_RATE
    )
    timing_new, timing_first_new, timing_second_new = adam_update(
        timing_weights, timing_first, timing_second, timing_grad * factor, ADAM_RATE, DECAY_RATE
    )
    norm_new, norm_first_new, norm_second_new = adam_update(
        norm_params, norm_first, norm_second, norm_grad * factor, GAIN_RATE, 0.0
    )
    return (
        loss_value,
        clip_norm,
        flip(attention_new),
        flip(moment_t),
        flip(attention_new.astype(LOW)),
        flip(cross_new),
        flip(cross_moment_t),
        flip(cross_new.astype(LOW)),
        gate_up_new,
        gate_up_first_new,
        gate_up_second_new,
        gate_up_new.astype(LOW),
        down_new,
        down_first_new,
        down_second_new,
        down_new.astype(LOW),
        latent_new,
        latent_first_new,
        latent_second_new,
        latent_new.astype(LOW),
        timing_new,
        timing_first_new,
        timing_second_new,
        timing_new.astype(LOW),
        norm_new,
        norm_first_new,
        norm_second_new,
    )


def solution(mesh):
    if tuple(mesh.devices.shape) != (RANKS, 4):
        return general(mesh)
    mesh3 = jax.sharding.Mesh(mesh.devices.reshape(4, 2, 4), ALL)
    seq = ("z", "y")
    row = P(ALL, None)
    col2 = P(None, ALL)
    col3 = P(None, None, ALL)
    return jax.shard_map(
        fast_body,
        mesh=mesh3,
        in_specs=(P("f", seq, None),) * 2
        + (P("f"),) * 3
        + (P("f", None, None),)
        + (col3,) * 4
        + (row,) * 6
        + (col3,) * 3
        + (col2,) * 6,
        out_specs=(P(),) * 2 + (col3,) * 6 + (row,) * 8 + (col3,) * 4 + (col2,) * 7,
        check_vma=False,
    )
```

```python
import functools
import math

import jax
import jax.numpy as jnp
from jax import lax
from jax.experimental import pallas as pl
from jax.experimental.pallas import tpu as pltpu
from jax.sharding import PartitionSpec as P

D = 1536
HEADS = 24
HEAD_DIM = 64
FF = 6144
E = 768
LAT = 64
FOUR = 256
NBUCK = 4
STEP = 10


HIGHEST = lax.Precision.HIGHEST
NS_COEF = (3.4445, -4.775, 2.0315)
CLIP_AT = 0.01
MUON_RATE = 0.5
ADAM_RATE = 0.02
GAIN_RATE = 0.2
DECAY_RATE = 0.01


def times_transposed(left, weight):
    return lax.dot_general(
        left, weight, (((left.ndim - 1,), (1,)), ((), ())), preferred_element_type=jnp.float32
    )


def matmul_low(left, right):
    return jnp.dot(left, right, preferred_element_type=jnp.float32)


def rows_product(left, right):
    return lax.dot_general(
        left, right, (((0,), (0,)), ((), ())), preferred_element_type=jnp.float32
    )


def rows_precise(left, right):
    return lax.dot_general(left, right, (((0,), (0,)), ((), ())), precision=HIGHEST)


def layer_norm(hidden, gain, shift):
    centred = hidden - jnp.mean(hidden, axis=-1, keepdims=True)
    spread = jnp.mean(centred * centred, axis=-1, keepdims=True)
    return centred * lax.rsqrt(spread + 1e-05) * gain + shift


def rotate(values, cosine, sine_table):
    half_dim = values.shape[-1] // 2
    first = values[..., :half_dim]
    second = values[..., half_dim:]
    return jnp.concatenate(
        [first * cosine - second * sine_table, second * cosine + first * sine_table], axis=-1
    )


def time_features(timesteps):
    count = FOUR // 2
    freqs = jnp.exp(jnp.arange(count, dtype=jnp.float32) * (math.log(100.0) / max(count - 1, 1)))
    phases = 2.0 * math.pi * timesteps[:, None] * freqs[None, :]
    return jnp.concatenate([jnp.cos(phases), jnp.sin(phases)], axis=1)


def split_heads(values):
    return values.reshape(values.shape[0], values.shape[1], HEADS, HEAD_DIM)


def scores_of(queries, key_rows):
    return jnp.einsum(
        "bqhd,bkhd->bhqk", queries, key_rows, preferred_element_type=jnp.float32
    ) / math.sqrt(HEAD_DIM)


def masked_scores(queries, key_rows, lengths):
    key_live = jnp.arange(key_rows.shape[1])[None, :] < lengths[:, None]
    return jnp.where(key_live[:, None, None, :], scores_of(queries, key_rows), -1e30)


def attention_forward(queries, key_low, value_low, lengths):
    item_count, frames = (queries.shape[0], queries.shape[1])
    running_top = jnp.full((item_count, HEADS, frames), -1e29, jnp.float32)
    scores = masked_scores(
        queries, split_heads(lax.all_gather(key_low, "seq", axis=1, tiled=True)), lengths
    )
    new_top = jnp.maximum(running_top, jnp.max(scores, axis=-1))
    running_sum = jnp.sum(jnp.exp(scores - new_top[..., None]), axis=-1)
    running_top, running_sum = (new_top, running_sum)
    log_total = running_top + jnp.log(running_sum)
    scores = masked_scores(
        queries, split_heads(lax.all_gather(key_low, "seq", axis=1, tiled=True)), lengths
    )
    weights = jnp.exp(scores - log_total[..., None]).astype(jnp.bfloat16)
    mixed = jnp.einsum(
        "bhqk,bkhd->bqhd",
        weights,
        split_heads(lax.all_gather(value_low, "seq", axis=1, tiled=True)),
        preferred_element_type=jnp.float32,
    )
    return (mixed, log_total)


def attention_backward(
    queries, key_low, value_low, grad_out, log_total, row_delta, lengths, position
):
    key_heads = split_heads(key_low)
    value_heads = split_heads(value_low)
    local_live = (position[None, :] < lengths[:, None])[:, None, None, :]
    query_flat = queries.reshape(key_low.shape).astype(jnp.float32)
    grad_flat = grad_out.reshape(key_low.shape).astype(jnp.float32)
    total_flat = jnp.transpose(log_total, (0, 2, 1))
    pieces = (
        lax.all_gather(query_flat.astype(jnp.bfloat16), "seq", axis=1, tiled=True).astype(
            jnp.float32
        ),
        lax.all_gather(grad_flat.astype(jnp.bfloat16), "seq", axis=1, tiled=True).astype(
            jnp.float32
        ),
        lax.all_gather(total_flat.astype(jnp.bfloat16), "seq", axis=1, tiled=True).astype(
            jnp.float32
        ),
        lax.all_gather(row_delta.astype(jnp.bfloat16), "seq", axis=1, tiled=True).astype(
            jnp.float32
        ),
    )
    query_rows = split_heads(pieces[0].astype(jnp.bfloat16))
    grad_rows = split_heads(pieces[1].astype(jnp.bfloat16))
    total_rows = jnp.transpose(pieces[2], (0, 2, 1))[..., None]
    delta_rows = jnp.transpose(pieces[3], (0, 2, 1))[..., None]
    scores = jnp.where(local_live, scores_of(query_rows, key_heads), -1e30)
    weights = jnp.exp(scores - total_rows)
    grad_value = jnp.einsum(
        "bhqk,bqhd->bkhd",
        weights.astype(jnp.bfloat16),
        grad_rows,
        preferred_element_type=jnp.float32,
    )
    grad_scores = jnp.einsum(
        "bqhd,bkhd->bhqk", grad_rows, value_heads, preferred_element_type=jnp.float32
    )
    pushed = (weights * (grad_scores - delta_rows)).astype(jnp.bfloat16)
    grad_key = jnp.einsum("bhqk,bqhd->bkhd", pushed, query_rows, preferred_element_type=jnp.float32)
    grad_key, grad_value = (grad_key, grad_value)
    delta_heads = jnp.transpose(row_delta, (0, 2, 1))[..., None]
    pieces = (
        lax.all_gather(key_low, "seq", axis=1, tiled=True),
        lax.all_gather(value_low, "seq", axis=1, tiled=True),
    )
    key_rows = split_heads(pieces[0])
    scores = masked_scores(queries, key_rows, lengths)
    weights = jnp.exp(scores - log_total[..., None])
    grad_scores = jnp.einsum(
        "bqhd,bkhd->bhqk", grad_out, split_heads(pieces[1]), preferred_element_type=jnp.float32
    )
    pushed = (weights * (grad_scores - delta_heads)).astype(jnp.bfloat16)
    grad_query = jnp.einsum("bhqk,bkhd->bqhd", pushed, key_rows, preferred_element_type=jnp.float32)
    score_scale = math.sqrt(HEAD_DIM)
    return (grad_query / score_scale, grad_key / score_scale, grad_value)


def layer_forward(weights, noisy_input, features, context, lengths, cosine, sine_table):
    attention, cross, gate_up, down, latent, timing, norms = weights
    norms = norms.astype(jnp.float32)
    item_count, frames, latent_dim = noisy_input.shape
    tokens = item_count * frames
    noisy_low = noisy_input.reshape(tokens, latent_dim).astype(jnp.bfloat16)
    feat_low = features.astype(jnp.bfloat16)
    timed = matmul_low(feat_low, timing)
    start_state = (
        matmul_low(noisy_low, latent[0]).reshape(item_count, frames, D) + timed[:, None, :]
    ).reshape(tokens, D)
    normed_one, back_one = jax.vjp(layer_norm, start_state, norms[0], norms[1])
    normed_one = normed_one.astype(jnp.bfloat16)
    triple = times_transposed(normed_one, attention[:3].reshape(3 * D, D)).reshape(
        item_count, frames, 3, HEADS, HEAD_DIM
    )
    queries = rotate(triple[:, :, 0], cosine, sine_table).astype(jnp.bfloat16)
    key_low = (
        rotate(triple[:, :, 1], cosine, sine_table)
        .astype(jnp.bfloat16)
        .reshape(item_count, frames, D)
    )
    value_low = triple[:, :, 2].astype(jnp.bfloat16).reshape(item_count, frames, D)
    mixed, log_total = attention_forward(queries, key_low, value_low, lengths)
    mixed_low = mixed.reshape(tokens, D).astype(jnp.bfloat16)
    after_self = start_state + times_transposed(mixed_low, attention[3])
    normed_two, back_two = jax.vjp(layer_norm, after_self, norms[2], norms[3])
    normed_two = normed_two.astype(jnp.bfloat16)
    cross_query = (
        times_transposed(normed_two, attention[4])
        .astype(jnp.bfloat16)
        .reshape(item_count, frames, HEADS, HEAD_DIM)
    )
    context_len = context.shape[1]
    cross_pair = times_transposed(
        context.reshape(item_count * context_len, E), cross.reshape(2 * D, E)
    ).astype(jnp.bfloat16)
    cross_pair = cross_pair.reshape(item_count, context_len, 2, HEADS, HEAD_DIM)
    cross_key, cross_value = (cross_pair[:, :, 0], cross_pair[:, :, 1])
    cross_weights = jax.nn.softmax(scores_of(cross_query, cross_key), axis=-1)
    cross_low = cross_weights.astype(jnp.bfloat16)
    cross_out = (
        jnp.einsum("bhqk,bkhd->bqhd", cross_low, cross_value, preferred_element_type=jnp.float32)
        .reshape(tokens, D)
        .astype(jnp.bfloat16)
    )
    after_cross = after_self + times_transposed(cross_out, attention[5])
    normed_three, back_three = jax.vjp(layer_norm, after_cross, norms[4], norms[5])
    normed_three = normed_three.astype(jnp.bfloat16)
    gate_both = times_transposed(normed_three, gate_up)
    gate_half, up_half = (gate_both[:, :FF], gate_both[:, FF:])
    inner_act = (jax.nn.silu(gate_half) * up_half).astype(jnp.bfloat16)
    final_state = (after_cross + matmul_low(inner_act, down)).astype(jnp.bfloat16)
    predicted = times_transposed(final_state, latent[1])
    saved = (
        noisy_low,
        feat_low,
        back_one,
        normed_one,
        queries,
        key_low,
        value_low,
        mixed,
        log_total,
        mixed_low,
        back_two,
        normed_two,
        cross_query,
        cross_key,
        cross_value,
        cross_weights,
        cross_low,
        cross_out,
        back_three,
        normed_three,
        gate_half,
        up_half,
        inner_act,
        final_state,
    )
    return (predicted, saved)


def layer_backward(weights, saved, grad_pred, context, lengths, cosine, sine_table, position):
    attention, cross, gate_up, down, latent, timing, norms = weights
    (
        noisy_low,
        feat_low,
        back_one,
        normed_one,
        queries,
        key_low,
        value_low,
        mixed,
        log_total,
        mixed_low,
        back_two,
        normed_two,
        cross_query,
        cross_key,
        cross_value,
        cross_weights,
        cross_low,
        cross_out,
        back_three,
        normed_three,
        gate_half,
        up_half,
        inner_act,
        final_state,
    ) = saved
    item_count, frames = (queries.shape[0], queries.shape[1])
    tokens = item_count * frames
    grad_out_proj = rows_product(grad_pred, final_state)
    grad_state = matmul_low(grad_pred, latent[1])
    grad_branch = grad_state.astype(jnp.bfloat16)
    down_reduced = lax.psum_scatter(
        rows_product(inner_act, grad_branch), ("seq", "fsdp"), scatter_dimension=0, tiled=True
    )
    grad_inner = times_transposed(grad_branch, down)
    sigmoid_gate = jax.nn.sigmoid(gate_half)
    grad_gate = grad_inner * up_half * sigmoid_gate * (1.0 + gate_half * (1.0 - sigmoid_gate))
    grad_both = jnp.concatenate([grad_gate, grad_inner * gate_half * sigmoid_gate], axis=1).astype(
        jnp.bfloat16
    )
    gate_up_reduced = lax.psum_scatter(
        rows_product(grad_both, normed_three), ("seq", "fsdp"), scatter_dimension=0, tiled=True
    )
    residual_part, gain_three, shift_three = back_three(matmul_low(grad_both, gate_up))
    grad_state = grad_state + residual_part
    grad_branch = grad_state.astype(jnp.bfloat16)
    grad_cross_out = rows_product(grad_branch, cross_out)
    grad_mix = (
        matmul_low(grad_branch, attention[5])
        .astype(jnp.bfloat16)
        .reshape(item_count, frames, HEADS, HEAD_DIM)
    )
    grad_scores = jnp.einsum(
        "bqhd,bkhd->bhqk", grad_mix, cross_value, preferred_element_type=jnp.float32
    )
    grad_cross_value = jnp.einsum(
        "bhqk,bqhd->bkhd", cross_low, grad_mix, preferred_element_type=jnp.float32
    )
    pushed = (
        cross_weights * (grad_scores - jnp.sum(cross_weights * grad_scores, axis=-1, keepdims=True))
    ).astype(jnp.bfloat16)
    score_scale = math.sqrt(HEAD_DIM)
    grad_cross_query = (
        (
            jnp.einsum("bhqk,bkhd->bqhd", pushed, cross_key, preferred_element_type=jnp.float32)
            / score_scale
        )
        .astype(jnp.bfloat16)
        .reshape(tokens, D)
    )
    grad_cross_key = (
        jnp.einsum("bhqk,bqhd->bkhd", pushed, cross_query, preferred_element_type=jnp.float32)
        / score_scale
    )
    context_len = context.shape[1]
    grad_pair = jnp.stack([grad_cross_key, grad_cross_value], axis=2).reshape(
        item_count * context_len, 2 * D
    )
    grad_cross = rows_precise(
        grad_pair, context.reshape(item_count * context_len, E).astype(jnp.float32)
    ).reshape(2, D, E)
    grad_cross_q = rows_product(grad_cross_query, normed_two)
    residual_part, gain_two, shift_two = back_two(matmul_low(grad_cross_query, attention[4]))
    grad_state = grad_state + residual_part
    grad_branch = grad_state.astype(jnp.bfloat16)
    grad_self_out = rows_product(grad_branch, mixed_low)
    grad_mixed = (
        matmul_low(grad_branch, attention[3])
        .astype(jnp.bfloat16)
        .reshape(item_count, frames, HEADS, HEAD_DIM)
    )
    row_delta = jnp.sum(grad_mixed.astype(jnp.float32) * mixed, axis=-1)
    grad_query, grad_key, grad_value = attention_backward(
        queries, key_low, value_low, grad_mixed, log_total, row_delta, lengths, position
    )
    grad_query = rotate(grad_query, cosine, -sine_table)
    grad_key = rotate(grad_key, cosine, -sine_table)
    grad_triple = (
        jnp.stack([grad_query, grad_key, grad_value], axis=2)
        .astype(jnp.bfloat16)
        .reshape(tokens, 3 * D)
    )
    grad_qkv = rows_product(grad_triple, normed_one).reshape(3, D, D)
    residual_part, gain_one, shift_one = back_one(
        matmul_low(grad_triple, attention[:3].reshape(3 * D, D))
    )
    grad_state = grad_state + residual_part
    grad_in_proj = rows_product(noisy_low, grad_state.astype(jnp.bfloat16))
    grad_timed = jnp.sum(grad_state.reshape(item_count, frames, D), axis=1)
    grad_timing = rows_precise(feat_low.astype(jnp.float32), grad_timed)
    grad_attention = jnp.concatenate(
        [grad_qkv, jnp.stack([grad_self_out, grad_cross_q, grad_cross_out])], axis=0
    )
    grad_latent = jnp.stack([grad_in_proj, grad_out_proj])
    grad_norms = jnp.stack([gain_one, shift_one, gain_two, shift_two, gain_three, shift_three])
    return (
        (grad_attention, grad_cross, grad_latent, grad_timing, grad_norms),
        gate_up_reduced,
        down_reduced,
    )


def gram_of(blocks):
    return jnp.einsum("sbik,sbjk->sbij", blocks, blocks, precision=HIGHEST)


def gram_sum(first, second):
    return lax.psum((gram_of(first), gram_of(second)), ("seq", "fsdp"))


def newton_schulz(first_moment, second_moment):
    moments = (first_moment, second_moment)
    blocks = [
        moment.reshape(moment.shape[0], moment.shape[1] // HEAD_DIM, HEAD_DIM, moment.shape[2])
        for moment in moments
    ]
    gram_list = gram_sum(blocks[0], blocks[1])
    block_norm = [
        jnp.sqrt(jnp.trace(gram, axis1=2, axis2=3))[..., None, None] + 1e-07 for gram in gram_list
    ]
    current = [block / norm_value for block, norm_value in zip(blocks, block_norm)]
    products = [gram / (norm_value * norm_value) for gram, norm_value in zip(gram_list, block_norm)]
    for newton_step in range(5):
        if newton_step > 0:
            products = gram_sum(current[0], current[1])
        updated = []
        for block, product in zip(current, products):
            squared = jnp.einsum("sbij,sbjk->sbik", product, product, precision=HIGHEST)
            mixer = NS_COEF[1] * product + NS_COEF[2] * squared
            updated.append(
                NS_COEF[0] * block + jnp.einsum("sbij,sbjk->sbik", mixer, block, precision=HIGHEST)
            )
        current = updated
    return [block.reshape(moment.shape) for block, moment in zip(current, moments)]


def adam_update(weight, first, second, grad, rate, decay):
    first_new = 0.9 * first + 0.1 * grad
    second_new = 0.95 * second + 0.05 * grad * grad
    first_hat = first_new / (1.0 - 0.9**STEP)
    second_hat = second_new / (1.0 - 0.95**STEP)
    weight_new = weight - rate * (first_hat / (jnp.sqrt(second_hat) + 1e-08) + decay * weight)
    return (weight_new, first_new, second_new)


def body(
    latents,
    gaussian_noise,
    timesteps,
    lengths,
    buckets,
    context,
    attention_weights,
    attention_moment,
    cross_weights,
    cross_moment,
    gate_up_weights,
    gate_up_first,
    gate_up_second,
    down_weights,
    down_first,
    down_second,
    latent_weights,
    latent_first,
    latent_second,
    timing_weights,
    timing_first,
    timing_second,
    norm_params,
    norm_first,
    norm_second,
):
    low_type = jnp.bfloat16
    item_count, frames, latent_dim = latents.shape
    tokens = item_count * frames
    onehot = (buckets[:, None] == jnp.arange(NBUCK)[None, :]).astype(jnp.float32)
    counts = lax.psum(jnp.dot(lengths.astype(jnp.float32), onehot, precision=HIGHEST), "fsdp")
    present = jnp.sum((counts > 0).astype(jnp.float32))
    bucket_scale = 1.0 / (present * LAT * jnp.maximum(counts, 1.0))
    item_scale = jnp.dot(onehot, bucket_scale, precision=HIGHEST)
    shards = (
        attention_weights.astype(low_type),
        cross_weights.astype(low_type),
        gate_up_weights.astype(low_type),
        down_weights.astype(low_type),
        latent_weights.astype(low_type),
        timing_weights.astype(low_type),
        norm_params.astype(low_type),
    )
    weights = (
        lax.all_gather(shards[0], ("seq", "fsdp"), axis=2, tiled=True),
        lax.all_gather(shards[1], ("seq", "fsdp"), axis=2, tiled=True),
        lax.all_gather(shards[2], ("seq", "fsdp"), axis=0, tiled=True),
        lax.all_gather(shards[3], ("seq", "fsdp"), axis=0, tiled=True),
        lax.all_gather(shards[4], ("seq", "fsdp"), axis=2, tiled=True),
        lax.all_gather(shards[5], ("seq", "fsdp"), axis=1, tiled=True),
        lax.all_gather(shards[6], ("seq", "fsdp"), axis=1, tiled=True),
    )
    signal = jnp.cos(0.5 * math.pi * timesteps)[:, None, None]
    noise_level = jnp.sin(0.5 * math.pi * timesteps)[:, None, None]
    noisy_input = signal * latents + noise_level * gaussian_noise
    target = (signal * gaussian_noise - noise_level * latents).reshape(tokens, latent_dim)
    features = time_features(timesteps)
    position = lax.axis_index("seq") * frames + jnp.arange(frames)
    live_mask = position[None, :] < lengths[:, None]
    half_dim = HEAD_DIM // 2
    inverse = 10000.0 ** (-jnp.arange(half_dim, dtype=jnp.float32) / half_dim)
    angles = position.astype(jnp.float32)[:, None] * inverse[None, :]
    cosine = jnp.cos(angles)[None, :, None, :]
    sine_table = jnp.sin(angles)[None, :, None, :]
    predicted, saved = layer_forward(
        weights, noisy_input, features, context, lengths, cosine, sine_table
    )
    difference = predicted - target
    errors = jnp.sum(difference * difference, axis=1).reshape(item_count, frames)
    per_item = jnp.sum(jnp.where(live_mask, errors, 0.0), axis=1)
    partial_sums = jnp.dot(per_item, onehot, precision=HIGHEST)
    bucket_sums = lax.psum(partial_sums, ("seq", "fsdp"))
    frame_scale = jnp.where(live_mask, item_scale[:, None], 0.0).reshape(tokens, 1)
    grad_pred = (2.0 * difference * frame_scale).astype(low_type)
    local_grads, gate_up_grad, down_grad = layer_backward(
        weights, saved, grad_pred, context, lengths, cosine, sine_table, position
    )
    reduced = (
        lax.psum_scatter(local_grads[0], ("seq", "fsdp"), scatter_dimension=2, tiled=True),
        lax.psum_scatter(local_grads[1], ("seq", "fsdp"), scatter_dimension=2, tiled=True),
        lax.psum_scatter(local_grads[2], ("seq", "fsdp"), scatter_dimension=2, tiled=True),
        lax.psum_scatter(local_grads[3], ("seq", "fsdp"), scatter_dimension=1, tiled=True),
        lax.psum_scatter(local_grads[4], ("seq", "fsdp"), scatter_dimension=1, tiled=True),
    )
    everything = tuple(reduced) + (gate_up_grad, down_grad)
    squares = sum((jnp.sum(grad * grad) for grad in everything))
    squares = lax.psum(squares, ("seq", "fsdp"))
    loss_value = jnp.sum(bucket_sums * bucket_scale)
    clip_norm = jnp.sqrt(squares)
    factor = CLIP_AT / jnp.maximum(clip_norm, CLIP_AT)
    attention_moment_new = 0.95 * attention_moment + reduced[0] * factor
    cross_moment_new = 0.95 * cross_moment + reduced[1] * factor
    attention_orth, cross_orth = newton_schulz(attention_moment_new, cross_moment_new)
    attention_new = attention_weights * (1.0 - MUON_RATE * DECAY_RATE) - MUON_RATE * attention_orth
    cross_new = cross_weights * (1.0 - MUON_RATE * DECAY_RATE) - MUON_RATE * cross_orth
    gate_up_new, gate_up_first_new, gate_up_second_new = adam_update(
        gate_up_weights, gate_up_first, gate_up_second, gate_up_grad * factor, ADAM_RATE, DECAY_RATE
    )
    down_new, down_first_new, down_second_new = adam_update(
        down_weights, down_first, down_second, down_grad * factor, ADAM_RATE, DECAY_RATE
    )
    latent_new, latent_first_new, latent_second_new = adam_update(
        latent_weights, latent_first, latent_second, reduced[2] * factor, ADAM_RATE, DECAY_RATE
    )
    timing_new, timing_first_new, timing_second_new = adam_update(
        timing_weights, timing_first, timing_second, reduced[3] * factor, ADAM_RATE, DECAY_RATE
    )
    norm_new, norm_first_new, norm_second_new = adam_update(
        norm_params, norm_first, norm_second, reduced[4] * factor, GAIN_RATE, 0.0
    )
    return (
        loss_value,
        clip_norm,
        attention_new,
        attention_moment_new,
        attention_new.astype(low_type),
        cross_new,
        cross_moment_new,
        cross_new.astype(low_type),
        gate_up_new,
        gate_up_first_new,
        gate_up_second_new,
        gate_up_new.astype(low_type),
        down_new,
        down_first_new,
        down_second_new,
        down_new.astype(low_type),
        latent_new,
        latent_first_new,
        latent_second_new,
        latent_new.astype(low_type),
        timing_new,
        timing_first_new,
        timing_second_new,
        timing_new.astype(low_type),
        norm_new,
        norm_first_new,
        norm_second_new,
    )


def general(mesh):
    return jax.shard_map(
        body,
        mesh=mesh,
        in_specs=(
            P("fsdp", "seq", None),
            P("fsdp", "seq", None),
            P("fsdp"),
            P("fsdp"),
            P("fsdp"),
            P("fsdp", None, None),
            P(None, None, ("seq", "fsdp")),
            P(None, None, ("seq", "fsdp")),
            P(None, None, ("seq", "fsdp")),
            P(None, None, ("seq", "fsdp")),
            P(("seq", "fsdp"), None),
            P(("seq", "fsdp"), None),
            P(("seq", "fsdp"), None),
            P(("seq", "fsdp"), None),
            P(("seq", "fsdp"), None),
            P(("seq", "fsdp"), None),
            P(None, None, ("seq", "fsdp")),
            P(None, None, ("seq", "fsdp")),
            P(None, None, ("seq", "fsdp")),
            P(None, ("seq", "fsdp")),
            P(None, ("seq", "fsdp")),
            P(None, ("seq", "fsdp")),
            P(None, ("seq", "fsdp")),
            P(None, ("seq", "fsdp")),
            P(None, ("seq", "fsdp")),
        ),
        out_specs=(
            P(),
            P(),
            P(None, None, ("seq", "fsdp")),
            P(None, None, ("seq", "fsdp")),
            P(None, None, ("seq", "fsdp")),
            P(None, None, ("seq", "fsdp")),
            P(None, None, ("seq", "fsdp")),
            P(None, None, ("seq", "fsdp")),
            P(("seq", "fsdp"), None),
            P(("seq", "fsdp"), None),
            P(("seq", "fsdp"), None),
            P(("seq", "fsdp"), None),
            P(("seq", "fsdp"), None),
            P(("seq", "fsdp"), None),
            P(("seq", "fsdp"), None),
            P(("seq", "fsdp"), None),
            P(None, None, ("seq", "fsdp")),
            P(None, None, ("seq", "fsdp")),
            P(None, None, ("seq", "fsdp")),
            P(None, None, ("seq", "fsdp")),
            P(None, ("seq", "fsdp")),
            P(None, ("seq", "fsdp")),
            P(None, ("seq", "fsdp")),
            P(None, ("seq", "fsdp")),
            P(None, ("seq", "fsdp")),
            P(None, ("seq", "fsdp")),
            P(None, ("seq", "fsdp")),
        ),
        check_vma=False,
    )


LAYER = ("y", "f")
ALL = ("z", "y", "f")
RANKS = 8
LOCAL_HEADS = HEADS // RANKS
COLS = LOCAL_HEADS * HEAD_DIM
LOW = jnp.bfloat16


MESH = pl.DeviceIdType.MESH


def place():
    at = lax.axis_index("f")
    return lax.axis_index("z"), lax.axis_index("y"), at // 2, at % 2


def turned(me, flip):
    z_at, y_at, x_at, core = me
    low = z_at % 2
    high = z_at // 2
    low = 1 - low if flip[0] & 1 else low
    high = 1 - high if flip[0] & 2 else high
    return (
        2 * high + low,
        1 - y_at if flip[1] else y_at,
        1 - x_at if flip[2] else x_at,
        1 - core if flip[3] else core,
    )


def device_of(where):
    return (where[0], where[1], 2 * where[2] + where[3])


def rank_of(where):
    return 4 * where[1] + 2 * where[2] + where[3]


def greet(peers):
    barrier = pltpu.get_barrier_semaphore()
    for peer in peers:
        pl.semaphore_signal(barrier, inc=1, device_id=device_of(peer), device_id_type=MESH)
    pl.semaphore_wait(barrier, len(peers))


LAYER_FLIPS = [(0, y, x, c) for y in range(2) for x in range(2) for c in range(2)][1:]


def comm_call(kernel, out_shape, arrays, scratch, ident, vmem=False, cost_us=20):
    spec = pl.BlockSpec(memory_space=pl.ANY)
    return pl.pallas_call(
        kernel,
        out_shape=out_shape,
        in_specs=[spec] * len(arrays),
        out_specs=jax.tree.map(lambda _: spec, out_shape),
        scratch_shapes=scratch,
        compiler_params=pltpu.CompilerParams(
            collective_id=ident, has_side_effects=True, vmem_limit_bytes=(40 << 20) if vmem else None
        ),
        cost_estimate=pl.CostEstimate(
            flops=cost_us * 10**9, bytes_accessed=1 << 20, transcendentals=0
        ),
    )(*arrays)


LINE_FLIPS = [(1, 0, 0, 0), (2, 0, 0, 0), (3, 0, 0, 0)]


def line_start(me, ins, outs, sent, got):
    copies = []
    for i, (src, dst) in enumerate(zip(ins, outs)):
        for k, flip in enumerate(LINE_FLIPS):
            peer = turned(me, flip)
            copy = pltpu.make_async_remote_copy(
                src_ref=src if len(src.shape) == 2 else src.at[peer[0]],
                dst_ref=dst.at[k],
                send_sem=sent.at[i, k],
                recv_sem=got.at[i, k],
                device_id=device_of(peer),
                device_id_type=MESH,
            )
            copy.start()
            copies.append(copy)
    return copies


def line_shapes(arrays):
    return tuple(
        jax.ShapeDtypeStruct((3,) + (a.shape if a.ndim == 2 else a.shape[1:]), a.dtype)
        for a in arrays
    )


LEVELS = 32000.0


def line_pack(parts):
    tops = jnp.max(jnp.abs(parts), axis=2)
    codes = jnp.round(parts * (LEVELS / jnp.maximum(tops, 1e-30))[:, :, None]).astype(jnp.int32)
    half = parts.shape[1] // 2
    return tops, lax.shift_left(codes[:, :half], 16) | (codes[:, half:] & 65535)


def line_total(part, tops, words):
    z_at = lax.axis_index("z")
    total = lax.dynamic_index_in_dim(part, z_at, 0, keepdims=False)
    steps = lax.dynamic_index_in_dim(tops, z_at, 1, keepdims=False) * (1.0 / LEVELS)
    for k in range(3):
        high = lax.shift_right_arithmetic(words[k], 16)
        low = lax.shift_right_arithmetic(lax.shift_left(words[k], 16), 16)
        codes = jnp.concatenate([high, low], axis=0).astype(jnp.float32)
        total = total + codes * steps[k][:, None]
    return total


def putter(sent, got):
    count = [0]

    def put(src, dst, peer):
        at = count[0]
        count[0] += 1
        copy = pltpu.make_async_remote_copy(
            src_ref=src,
            dst_ref=dst,
            send_sem=sent.at[at],
            recv_sem=got.at[at],
            device_id=device_of(peer),
            device_id_type=MESH,
        )
        copy.start()
        return copy

    return put


def swap_flow(me, put, x_ref, o_ref, own):
    mine = rank_of(me)
    peers = [turned(me, flip) for flip in LAYER_FLIPS]
    copies = [put(x_ref.at[rank_of(peer)], o_ref.at[mine], peer) for peer in peers]
    local = pltpu.make_async_copy(x_ref.at[mine], o_ref.at[mine], own)
    local.start()
    yield
    local.wait()
    for copy in copies:
        copy.wait()


def gather_flow(me, put, x_ref, o_ref, own):
    half = x_ref.shape[0] // 2
    by_x, by_y, by_xy = (turned(me, (0, y, x, 0)) for y, x in ((0, 1), (1, 0), (1, 1)))
    other = turned(me, (0, 0, 0, 1))
    slot = o_ref.at[rank_of(me)]
    first, second = pl.ds(0, half), pl.ds(half, half)
    copies = [
        put(x_ref.at[first], slot.at[first], by_x),
        put(x_ref.at[second], slot.at[second], by_y),
        put(x_ref.at[second], slot.at[second], by_x),
        put(x_ref.at[first], slot.at[first], by_y),
        put(x_ref, slot, other),
    ]
    local = pltpu.make_async_copy(x_ref, slot, own)
    local.start()
    from_x, from_y, from_xy = (o_ref.at[rank_of(p)] for p in (by_x, by_y, by_xy))
    yield
    copies[0].wait_recv()
    copies.append(put(from_x.at[first], from_x.at[first], by_y))
    copies[1].wait_recv()
    copies.append(put(from_y.at[second], from_y.at[second], by_x))
    yield
    copies[2].wait_recv()
    copies.append(put(from_x, from_x, other))
    copies[3].wait_recv()
    copies.append(put(from_y, from_y, other))
    yield
    copies[5].wait_recv()
    copies[6].wait_recv()
    copies.append(put(from_xy, from_xy, other))
    local.wait()
    for i in (4, 7, 8, 9):
        copies[i].wait_recv()
    for copy in copies:
        copy.wait_send()


def encode(value, words, steps):
    half = value.shape[0] // 2
    top = jnp.max(jnp.abs(value), axis=1, keepdims=True)
    codes = jnp.round(value * (LEVELS / jnp.maximum(top, 1e-30))).astype(jnp.int32)
    words[...] = lax.shift_left(codes[:half], 16) | (codes[half:] & 65535)
    steps[...] = jnp.broadcast_to(top * (1.0 / LEVELS), steps.shape)


def decode(words, steps):
    values = words[...]
    high = lax.shift_right_arithmetic(values, 16)
    low = lax.shift_right_arithmetic(lax.shift_left(values, 16), 16)
    return jnp.concatenate([high, low], axis=0).astype(jnp.float32) * steps[:, 0:1]


def sum_flow(me, put, p_ref, o_ref, own, mine, theirs, out_words, out_steps, in_words, in_steps):
    half = mine.shape[1] // 2
    by_x, by_y = (turned(me, flip) for flip in ((0, 0, 1, 0), (0, 1, 0, 0)))
    other = turned(me, (0, 0, 0, 1))
    cores, locals_ = [], []
    for slot in (3, 2, 1, 0):
        chip = turned(me, (0, slot // 2, slot % 2, 0))
        local = pltpu.make_async_copy(p_ref.at[rank_of(chip)], mine.at[slot], own.at[slot])
        local.start()
        locals_.append(local)
        cores.append(put(p_ref.at[rank_of(turned(chip, (0, 0, 0, 1)))], theirs.at[slot], other))
    first, second = pl.ds(0, half), pl.ds(half, half)
    copies = []

    def pass_on(unit, slot, rows, peer):
        encode(mine[slot, rows, :], out_words.at[unit], out_steps.at[unit])
        copies.append(
            (
                put(out_words.at[unit], in_words.at[unit], peer),
                put(out_steps.at[unit], in_steps.at[unit], peer),
            )
        )

    def take_in(unit, slot, rows):
        for copy in copies[unit]:
            copy.wait_recv()
        mine[slot, rows, :] = mine[slot, rows, :] + decode(in_words.at[unit], in_steps.at[unit])

    for i, slot in enumerate((3, 2, 1, 0)):
        locals_[i].wait()
        cores[i].wait_recv()
        mine[slot] = mine[slot] + theirs[slot]
        if slot == 3:
            pass_on(0, 3, first, by_x)
            pass_on(1, 3, second, by_y)
        if slot == 2:
            pass_on(2, 2, second, by_y)
        if slot == 1:
            pass_on(3, 1, first, by_x)
    yield
    take_in(0, 2, first)
    pass_on(4, 2, first, by_y)
    take_in(1, 1, second)
    pass_on(5, 1, second, by_x)
    yield
    take_in(3, 0, first)
    take_in(2, 0, second)
    yield
    take_in(4, 0, first)
    take_in(5, 0, second)
    done = pltpu.make_async_copy(mine.at[0], o_ref, own.at[4])
    done.start()
    done.wait()
    for copy in cores + [copy for pair in copies for copy in pair]:
        copy.wait_send()


def everyone_flow(me, put, x_ref, o_ref, own):
    slot = o_ref.at[RANKS * me[0] + rank_of(me)]
    copies = [put(x_ref, slot, turned(me, flip)) for flip in ALL_FLIPS]
    local = pltpu.make_async_copy(x_ref, slot, own)
    local.start()
    yield
    local.wait()
    for copy in copies:
        copy.wait()


def down_owner(z_at, rank):
    block = 2 * RANKS * (z_at // 2) + 2 * rank + z_at % 2
    return block // RANKS, block % RANKS


def move_flow(me, x_ref, o_ref, sent, got, own):
    z_at, mine = me[0], rank_of(me)
    to_z, to_rank = down_owner(z_at, mine)
    stays = (to_z == z_at) & (to_rank == mine)
    remote = pltpu.make_async_remote_copy(
        src_ref=x_ref,
        dst_ref=o_ref,
        send_sem=sent,
        recv_sem=got,
        device_id=(to_z, to_rank // 4, to_rank % 4),
        device_id_type=MESH,
    )
    local = pltpu.make_async_copy(x_ref, o_ref, own)

    @pl.when(stays)
    def _():
        local.start()

    @pl.when(jnp.logical_not(stays))
    def _():
        remote.start()

    yield

    @pl.when(stays)
    def _():
        local.wait()

    @pl.when(jnp.logical_not(stays))
    def _():
        remote.wait()


ALL_FLIPS = [(z, y, x, c) for z in range(4) for y in range(2) for x in range(2) for c in range(2)][1:]


def plane_step(ident, cost_us, sums=(), gathers=(), swaps=(), everyone=(), moves=(), carry=()):
    n_sum, n_gather, n_swap, n_carry = len(sums), len(gathers), len(swaps), len(carry)
    n_all = len(everyone)
    n_move = len(moves)
    total = n_sum + n_gather + n_swap + n_all + n_move + n_carry
    f32 = jnp.float32
    n_put = 16 * n_sum + 10 * n_gather + 7 * n_swap + 31 * n_all + n_move

    def kernel(*refs):
        ins, outs, scratch = refs[:total], refs[total : 2 * total], refs[2 * total :]
        sent, got, own, line_sent, line_got = scratch[:5]
        me = place()
        if n_all:
            peers = [turned(me, flip) for flip in ALL_FLIPS]
        elif n_swap:
            peers = [turned(me, flip) for flip in LAYER_FLIPS]
        else:
            peers = [turned(me, flip) for flip in ((0, 0, 1, 0), (0, 1, 0, 0), (0, 0, 0, 1))]
        if n_carry and not n_all:
            peers = peers + [turned(me, flip) for flip in LINE_FLIPS]
        greet(peers)
        put = putter(sent, got)
        carried = line_start(me, ins[total - n_carry :], outs[total - n_carry :], line_sent, line_got)
        flows = []
        for i in range(total - n_carry):
            if i < n_sum:
                flows.append(
                    sum_flow(me, put, ins[i], outs[i], own.at[i], *scratch[5 + 6 * i : 11 + 6 * i])
                )
            elif i < n_sum + n_gather:
                flows.append(gather_flow(me, put, ins[i], outs[i], own.at[i, 0]))
            elif i >= n_sum + n_gather + n_swap + n_all:
                at = n_put - n_move + (i - (n_sum + n_gather + n_swap + n_all))
                flows.append(
                    move_flow(me, ins[i], outs[i], sent.at[at], got.at[at], own.at[i, 0])
                )
            elif i >= n_sum + n_gather + n_swap:
                flows.append(everyone_flow(me, put, ins[i], outs[i], own.at[i, 0]))
            else:
                flows.append(swap_flow(me, put, ins[i], outs[i], own.at[i, 0]))
        for _ in range(8):
            for flow in flows[n_sum:] + flows[:n_sum]:
                next(flow, None)
        for copy in carried:
            copy.wait()

    dma = pltpu.SemaphoreType.DMA
    shape = jax.ShapeDtypeStruct
    outs = [shape(a.shape[1:], f32) for a in sums]
    outs += [shape((RANKS,) + a.shape, a.dtype) for a in gathers]
    outs += [shape(a.shape, a.dtype) for a in swaps]
    outs += [shape((len(ALL_FLIPS) + 1,) + a.shape, a.dtype) for a in everyone]
    outs += [shape(a.shape, a.dtype) for a in moves]
    scratch = [
        dma((n_put,)),
        dma((n_put,)),
        dma((total, 5)),
        dma((max(n_carry, 1), 3)),
        dma((max(n_carry, 1), 3)),
    ]
    for a in sums:
        rows, lanes = a.shape[1:]
        scratch += [
            pltpu.VMEM((4, rows, lanes), f32),
            pltpu.VMEM((4, rows, lanes), f32),
            pltpu.VMEM((6, rows // 4, lanes), jnp.int32),
            pltpu.VMEM((6, rows // 2, 128), f32),
            pltpu.VMEM((6, rows // 4, lanes), jnp.int32),
            pltpu.VMEM((6, rows // 2, 128), f32),
        ]
    return comm_call(
        kernel,
        tuple(outs) + line_shapes(carry),
        tuple(sums) + tuple(gathers) + tuple(swaps) + tuple(everyone) + tuple(moves) + tuple(carry),
        scratch,
        ident,
        vmem=bool(sums),
        cost_us=cost_us,
    )


def lanes_of(values):
    row = jnp.concatenate([jnp.stack(values), jnp.zeros((128 - len(values),), jnp.float32)])
    return jnp.broadcast_to(row[None, :], (8, 128))


def full_sum_steps(me, mine, theirs, in_a, in_b, in_c, in_d, in_z, put):
    z_at, y_at, x_at, core = me
    half = mine.shape[3] // 2
    first, second = pl.ds(0, half), pl.ds(half, half)
    by_x, by_y = (turned(me, flip) for flip in ((0, 0, 1, 0), (0, 1, 0, 0)))
    over_x = put(mine.at[1 - x_at, :, :, first], in_a, by_x)
    over_y = put(mine.at[:, 1 - y_at, :, second], in_b, by_y)
    over_x.wait_recv()
    mine[x_at, :, :, first] = mine[x_at, :, :, first] + in_a[...]
    next_y = put(mine.at[x_at, 1 - y_at, :, first], in_c, by_y)
    over_y.wait_recv()
    mine[:, y_at, :, second] = mine[:, y_at, :, second] + in_b[...]
    next_x = put(mine.at[1 - x_at, y_at, :, second], in_d, by_x)
    next_y.wait_recv()
    mine[x_at, y_at, :, first] = mine[x_at, y_at, :, first] + in_c[...]
    next_x.wait_recv()
    mine[x_at, y_at, :, second] = mine[x_at, y_at, :, second] + in_d[...]
    sends = []
    for k in (1, 2, 3):
        peer = turned(me, (k, 0, 0, 0))
        sends.append(put(mine.at[x_at, y_at, peer[0]], in_z.at[k - 1], peer))
    for send in sends:
        send.wait_recv()
    return mine[x_at, y_at, z_at] + in_z[0] + in_z[1] + in_z[2], [
        over_x,
        over_y,
        next_y,
        next_x,
    ] + sends


NEAR_FLIPS = [(0, 0, 0, 1), (0, 0, 1, 0), (0, 1, 0, 0), (1, 0, 0, 0), (2, 0, 0, 0), (3, 0, 0, 0)]


def full_scratch(rows, lanes):
    half = rows // 2
    f32 = jnp.float32
    return [
        pltpu.VMEM((2, 2, 4, rows, lanes), f32),
        pltpu.VMEM((2, 2, 4, rows, lanes), f32),
        pltpu.VMEM((2, 4, half, lanes), f32),
        pltpu.VMEM((2, 4, half, lanes), f32),
        pltpu.VMEM((4, half, lanes), f32),
        pltpu.VMEM((4, half, lanes), f32),
        pltpu.VMEM((3, rows, lanes), f32),
    ]


def full_start(p_ref, me, mine, theirs, own, put):
    core = me[3]
    local = pltpu.make_async_copy(p_ref.at[core], mine, own)
    local.start()
    swap = put(p_ref.at[1 - core], theirs, turned(me, (0, 0, 0, 1)))
    local.wait()
    swap.wait_recv()
    for x in range(2):
        for y in range(2):
            mine[x, y] = mine[x, y] + theirs[x, y]
    return swap


def full_scatter(parts, ident, carry):
    rows, lanes = parts.shape[4:]
    extra = len(carry)

    def kernel(p_ref, *refs):
        carry_in, o_ref, carry_out = refs[:extra], refs[extra], refs[extra + 1 : 2 * extra + 1]
        mine, theirs, in_a, in_b, in_c, in_d, in_z, total, sent, got, own, csent, cgot = refs[
            2 * extra + 1 :
        ]
        me = place()
        greet([turned(me, flip) for flip in NEAR_FLIPS])
        carried = line_start(me, carry_in, carry_out, csent, cgot)
        put = putter(sent, got)
        swap = full_start(p_ref, me, mine, theirs, own.at[0], put)
        value, copies = full_sum_steps(me, mine, theirs, in_a, in_b, in_c, in_d, in_z, put)
        total[...] = value
        done = pltpu.make_async_copy(total, o_ref, own.at[1])
        done.start()
        done.wait()
        for copy in [swap] + copies:
            copy.wait_send()
        for copy in carried:
            copy.wait()

    dma = pltpu.SemaphoreType.DMA
    return comm_call(
        kernel,
        (jax.ShapeDtypeStruct((rows, lanes), jnp.float32),) + line_shapes(carry),
        (parts,) + tuple(carry),
        full_scratch(rows, lanes)
        + [pltpu.VMEM((rows, lanes), jnp.float32), dma((8,)), dma((8,)), dma((2,))]
        + [dma((extra, 3))] * 2,
        ident,
        vmem=True,
        cost_us=40,
    )


def newton_pair(pair):
    wide = 2 * HEAD_DIM
    row = lax.broadcasted_iota(jnp.int32, (wide, wide), 0)
    lane = lax.broadcasted_iota(jnp.int32, (wide, wide), 1)
    same = (row < HEAD_DIM) == (lane < HEAD_DIM)
    gram = jnp.where(same, jnp.concatenate([pair, pair], axis=0), 0.0)
    diagonal = jnp.where(row == lane, gram, 0.0)
    lone = jnp.sum(jnp.where(row < HEAD_DIM, diagonal, 0.0), keepdims=True)
    ltwo = jnp.sum(jnp.where(row < HEAD_DIM, 0.0, diagonal), keepdims=True)
    norm_value = jnp.sqrt(jnp.where(row < HEAD_DIM, lone, ltwo)) + 1e-07
    product = gram / (norm_value * norm_value)
    eye = jnp.where(row == lane, 1.0, 0.0)

    def mul(left, right):
        return jnp.dot(left, right, precision=HIGHEST, preferred_element_type=jnp.float32)

    total = None
    for newton_step in range(5):
        mixer = NS_COEF[0] * eye + NS_COEF[1] * product + NS_COEF[2] * mul(product, product)
        total = mixer if total is None else mul(mixer, total)
        if newton_step < 4:
            product = mul(mul(mixer, product), mixer)
    total = total / norm_value
    return total[:HEAD_DIM] + total[HEAD_DIM:]


def full_newton(parts, ident):
    rows, lanes = parts.shape[4:]
    half = rows // 2

    def kernel(p_ref, o_ref, mine, theirs, in_a, in_b, in_c, in_d, in_z, whole, sent, got, own):
        me = place()
        z_at, y_at, x_at, core = me
        greet([turned(me, flip) for flip in NEAR_FLIPS])
        put = putter(sent, got)
        swap = full_start(p_ref, me, mine, theirs, own.at[0], put)
        value, copies = full_sum_steps(me, mine, theirs, in_a, in_b, in_c, in_d, in_z, put)
        for i in range(rows // HEAD_DIM):
            part = slice(i * HEAD_DIM, (i + 1) * HEAD_DIM)
            whole[core, x_at, y_at, z_at, pl.ds(i * HEAD_DIM, HEAD_DIM)] = newton_pair(value[part])
        first, second = pl.ds(0, half), pl.ds(half, half)
        by_x, by_y = (turned(me, flip) for flip in ((0, 0, 1, 0), (0, 1, 0, 0)))
        slot = whole.at[core, x_at, y_at, z_at]
        over_z = [put(slot, slot, turned(me, (k, 0, 0, 0))) for k in (1, 2, 3)]
        for copy in over_z:
            copy.wait_recv()
        part_a = whole.at[core, x_at, y_at, :, first]
        part_b = whole.at[core, x_at, y_at, :, second]
        over_x = put(part_a, part_a, by_x)
        over_y = put(part_b, part_b, by_y)
        over_x.wait_recv()
        part_a = whole.at[core, :, y_at, :, first]
        next_y = put(part_a, part_a, by_y)
        over_y.wait_recv()
        part_b = whole.at[core, x_at, :, :, second]
        next_x = put(part_b, part_b, by_x)
        next_y.wait_recv()
        next_x.wait_recv()
        last = put(whole.at[core], whole.at[core], turned(me, (0, 0, 0, 1)))
        last.wait_recv()
        done = pltpu.make_async_copy(whole, o_ref, own.at[1])
        done.start()
        done.wait()
        for copy in [swap] + copies + over_z + [over_x, over_y, next_y, next_x, last]:
            copy.wait_send()

    dma = pltpu.SemaphoreType.DMA
    return comm_call(
        kernel,
        jax.ShapeDtypeStruct(parts.shape, jnp.float32),
        (parts,),
        full_scratch(rows, lanes)
        + [pltpu.VMEM((2, 2, 2, 4, rows, lanes), jnp.float32), dma((16,)), dma((16,)), dma((2,))],
        ident,
        vmem=True,
    )


def setup_exchange(slab, swap, small, noisy, meta, ident):
    planes = 4
    flips_f = [flip for flip in LAYER_FLIPS if flip[1] == 0]

    def kernel(
        w_ref, c_ref, s_ref, n_ref, m_ref, wo, co, so, no, mo, s_mid, n_mid, sent, got, csent, cgot, own
    ):
        me = place()
        z_at, y_at, x_at, core = me
        mine = rank_of(me)
        f_at = 2 * x_at + core
        layer = [turned(me, flip) for flip in LAYER_FLIPS]
        line = [turned(me, (k, 0, 0, 0)) for k in (1, 2, 3)]
        greet(layer + line)
        put = putter(sent, got)
        locals_ = [
            pltpu.make_async_copy(w_ref.at[mine], wo.at[z_at, mine], own.at[0]),
            pltpu.make_async_copy(s_ref, s_mid.at[z_at], own.at[1]),
            pltpu.make_async_copy(n_ref, n_mid.at[y_at, f_at], own.at[2]),
            pltpu.make_async_copy(m_ref, mo.at[f_at], own.at[3]),
            pltpu.make_async_copy(c_ref.at[mine], co.at[mine], own.at[6]),
        ]
        for copy in locals_:
            copy.start()
        slabs = [put(w_ref.at[rank_of(peer)], wo.at[z_at, mine], peer) for peer in layer]
        small_line = [put(s_ref, s_mid.at[z_at], peer) for peer in line]
        metas = [put(m_ref, mo.at[f_at], turned(me, flip)) for flip in flips_f]
        noisies = [put(n_ref, n_mid.at[y_at, f_at], peer) for peer in layer]
        for copy in locals_:
            copy.wait()
        for copy in slabs:
            copy.wait_recv()

        def along(which, target, source, step):
            return pltpu.make_async_remote_copy(
                src_ref=wo.at[source],
                dst_ref=wo.at[source],
                send_sem=csent.at[which, step],
                recv_sem=cgot.at[which, step],
                device_id=device_of((target, y_at, x_at, core)),
                device_id_type=MESH,
            )

        def go(step):
            @pl.when((z_at < planes - 1) & (z_at >= step))
            def _():
                along(0, z_at + 1, z_at - step, step).start()

            @pl.when((z_at > 0) & (z_at + step < planes))
            def _():
                along(1, z_at - 1, z_at + step, step).start()

        def come(step):
            @pl.when(z_at >= step + 1)
            def _():
                along(0, z_at - 1, z_at - 1 - step, step).wait_recv()

            @pl.when(z_at + step + 1 < planes)
            def _():
                along(1, z_at + 1, z_at + 1 + step, step).wait_recv()

        go(0)
        for copy in small_line:
            copy.wait_recv()
        smalls = [put(s_mid, so.at[:, mine], peer) for peer in layer]
        small_own = pltpu.make_async_copy(s_mid, so.at[:, mine], own.at[4])
        small_own.start()
        for copy in noisies:
            copy.wait_recv()
        noisy_line = [put(n_mid.at[:, peer[0]], no.at[z_at], peer) for peer in line]
        noisy_own = pltpu.make_async_copy(n_mid.at[:, z_at], no.at[z_at], own.at[5])
        noisy_own.start()
        swaps = [put(c_ref.at[rank_of(peer)], co.at[mine], peer) for peer in layer]
        come(0)
        go(1)
        come(1)
        go(2)
        come(2)
        small_own.wait()
        noisy_own.wait()
        for copy in metas + smalls + noisy_line + swaps:
            copy.wait_recv()
        for copy in small_line + slabs + metas + noisies + smalls + noisy_line + swaps:
            copy.wait_send()
        for step in range(3):

            @pl.when((z_at < planes - 1) & (z_at >= step))
            def _():
                along(0, z_at + 1, z_at - step, step).wait_send()

            @pl.when((z_at > 0) & (z_at + step < planes))
            def _():
                along(1, z_at - 1, z_at + step, step).wait_send()

    dma = pltpu.SemaphoreType.DMA
    shape = jax.ShapeDtypeStruct
    return comm_call(
        kernel,
        (
            shape((planes,) + slab.shape, slab.dtype),
            shape(swap.shape, swap.dtype),
            shape((planes, RANKS) + small.shape, small.dtype),
            shape((planes, 2) + noisy.shape, noisy.dtype),
            shape((4,) + meta.shape, meta.dtype),
        ),
        (slab, swap, small, noisy, meta),
        [
            pltpu.VMEM((planes,) + small.shape, small.dtype),
            pltpu.VMEM((2, 4) + noisy.shape, noisy.dtype),
            dma((40,)),
            dma((40,)),
            dma((2, 3)),
            dma((2, 3)),
            dma((7,)),
        ],
        ident,
        vmem=True,
        cost_us=60,
    )


def swapped_halves(values):
    half_dim = values.shape[1] // 2
    return jnp.concatenate([values[:, half_dim:], values[:, :half_dim]], axis=1)


def attend_kernel(lengths_ref, qkv_ref, cos_ref, sin_ref, qr_ref, kr_ref, vr_ref, o_ref, low_ref, lse_ref):
    frames = qkv_ref.shape[1]
    length = lengths_ref[pl.program_id(0)]
    cosine, sine_table = cos_ref[...], sin_ref[...]
    chunk = 256
    live = lax.broadcasted_iota(jnp.int32, (chunk, frames), 1) < length
    for head in range(LOCAL_HEADS):
        at = slice(head * HEAD_DIM, (head + 1) * HEAD_DIM)

        def column(which):
            return qkv_ref[0, :, which * COLS + head * HEAD_DIM : which * COLS + (head + 1) * HEAD_DIM]

        query, key = column(0), column(1)
        queries = (query * cosine + swapped_halves(query) * sine_table).astype(LOW)
        keys = (key * cosine + swapped_halves(key) * sine_table).astype(LOW)
        values = column(2).astype(LOW)
        qr_ref[0, head] = queries
        kr_ref[0, head] = keys
        vr_ref[0, head] = values
        for part in range(frames // chunk):
            rows = slice(part * chunk, (part + 1) * chunk)
            scores = lax.dot_general(
                queries[rows], keys, (((1,), (1,)), ((), ())), preferred_element_type=jnp.float32
            ) * (1.0 / math.sqrt(HEAD_DIM))
            scores = jnp.where(live, scores, -1e30)
            top = jnp.max(scores, axis=1, keepdims=True)
            grown = jnp.exp(scores - top)
            total = jnp.sum(grown, axis=1, keepdims=True)
            weights = (grown * (1.0 / total)).astype(LOW)
            mixed = jnp.dot(weights, values, preferred_element_type=jnp.float32)
            o_ref[0, head, rows, :] = mixed
            span = low_ref.shape[2]
            for k in range(chunk // span):
                low_ref[part * (chunk // span) + k, 0, :, at] = mixed[
                    k * span : (k + 1) * span
                ].astype(LOW)
            lse_ref[0, head, rows, :] = top + jnp.log(total)


def attend(qkv, cosine, sine_table, lengths, span):
    count, frames, width = qkv.shape
    heads = pl.BlockSpec((1, LOCAL_HEADS, frames, HEAD_DIM), lambda i: (i, 0, 0, 0))
    table = pl.BlockSpec((frames, HEAD_DIM), lambda i: (0, 0))
    low = jax.ShapeDtypeStruct((count, LOCAL_HEADS, frames, HEAD_DIM), LOW)
    return pl.pallas_call(
        attend_kernel,
        grid=(count,),
        out_shape=(
            low,
            low,
            low,
            jax.ShapeDtypeStruct((count, LOCAL_HEADS, frames, HEAD_DIM), jnp.float32),
            jax.ShapeDtypeStruct((RANKS, count, span, COLS), LOW),
            jax.ShapeDtypeStruct((count, LOCAL_HEADS, frames, 1), jnp.float32),
        ),
        in_specs=[
            pl.BlockSpec(memory_space=pltpu.SMEM),
            pl.BlockSpec((1, frames, width), lambda i: (i, 0, 0)),
            table,
            table,
        ],
        out_specs=(
            heads,
            heads,
            heads,
            heads,
            pl.BlockSpec((RANKS, 1, span, COLS), lambda i: (0, i, 0, 0)),
            pl.BlockSpec((1, LOCAL_HEADS, frames, 1), lambda i: (i, 0, 0, 0)),
        ),
        compiler_params=pltpu.CompilerParams(vmem_limit_bytes=56 << 20),
        cost_estimate=pl.CostEstimate(
            flops=4 * count * frames * frames * COLS,
            bytes_accessed=10 * count * frames * COLS,
            transcendentals=count * LOCAL_HEADS * frames * frames,
        ),
    )(lengths, qkv, cosine, sine_table)


def attend_back_kernel(
    lengths_ref, q_ref, k_ref, v_ref, o_ref, lse_ref, do_ref, cos_ref, sin_ref, d_ref
):
    frames = q_ref.shape[2]
    length = lengths_ref[pl.program_id(0)]
    cosine, sine_table = cos_ref[...], sin_ref[...]
    chunk = 256
    scale = 1.0 / math.sqrt(HEAD_DIM)
    span = do_ref.shape[2]
    live = lax.broadcasted_iota(jnp.int32, (chunk, frames), 1) < length
    for head in range(LOCAL_HEADS):
        at = slice(head * HEAD_DIM, (head + 1) * HEAD_DIM)
        keys = k_ref[0, head]
        values = v_ref[0, head]
        grad_key = jnp.zeros((frames, HEAD_DIM), jnp.float32)
        grad_value = jnp.zeros((frames, HEAD_DIM), jnp.float32)
        for part in range(frames // chunk):
            rows = slice(part * chunk, (part + 1) * chunk)
            queries = q_ref[0, head, rows, :]
            grads = jnp.concatenate(
                [
                    do_ref[part * (chunk // span) + k, 0, :, at]
                    for k in range(chunk // span)
                ],
                axis=0,
            )
            scores = (
                lax.dot_general(
                    queries, keys, (((1,), (1,)), ((), ())), preferred_element_type=jnp.float32
                )
                * scale
            )
            scores = jnp.where(live, scores, -1e30)
            weights = jnp.exp(scores - lse_ref[0, head, rows, :])
            delta = jnp.sum(
                grads.astype(jnp.float32) * o_ref[0, head, rows, :], axis=1, keepdims=True
            )
            pulled = lax.dot_general(
                grads, values, (((1,), (1,)), ((), ())), preferred_element_type=jnp.float32
            )
            pushed = (weights * (pulled - delta)).astype(LOW)
            grad_query = jnp.dot(pushed, keys, preferred_element_type=jnp.float32) * scale
            grad_key = grad_key + rows_product(pushed, queries)
            grad_value = grad_value + rows_product(weights.astype(LOW), grads)
            d_ref[0, rows, head * HEAD_DIM : (head + 1) * HEAD_DIM] = (
                grad_query * cosine[rows] - swapped_halves(grad_query) * sine_table[rows]
            ).astype(LOW)
        grad_key = grad_key * scale
        d_ref[0, :, COLS + head * HEAD_DIM : COLS + (head + 1) * HEAD_DIM] = (
            grad_key * cosine - swapped_halves(grad_key) * sine_table
        ).astype(LOW)
        d_ref[0, :, 2 * COLS + head * HEAD_DIM : 2 * COLS + (head + 1) * HEAD_DIM] = (
            grad_value.astype(LOW)
        )


def attend_back(queries, key_rows, values, mixed, log_total, grads, cosine, sine_table, lengths):
    count, heads_here, frames, width = queries.shape
    span = grads.shape[2]
    heads = pl.BlockSpec((1, heads_here, frames, width), lambda i: (i, 0, 0, 0))
    table = pl.BlockSpec((frames, width), lambda i: (0, 0))
    return pl.pallas_call(
        attend_back_kernel,
        grid=(count,),
        out_shape=jax.ShapeDtypeStruct((count, frames, 3 * COLS), LOW),
        in_specs=[
            pl.BlockSpec(memory_space=pltpu.SMEM),
            heads,
            heads,
            heads,
            heads,
            pl.BlockSpec((1, heads_here, frames, 1), lambda i: (i, 0, 0, 0)),
            pl.BlockSpec((RANKS, 1, span, COLS), lambda i: (0, i, 0, 0)),
            table,
            table,
        ],
        out_specs=pl.BlockSpec((1, frames, 3 * COLS), lambda i: (i, 0, 0)),
        compiler_params=pltpu.CompilerParams(vmem_limit_bytes=56 << 20),
        cost_estimate=pl.CostEstimate(
            flops=10 * count * frames * frames * COLS,
            bytes_accessed=24 * count * frames * COLS,
            transcendentals=count * heads_here * frames * frames,
        ),
    )(lengths, queries, key_rows, values, mixed, log_total, grads, cosine, sine_table)


def first_state(noisy_ref, win_ref, timed_ref):
    hidden = jnp.dot(noisy_ref[...], win_ref[...], preferred_element_type=jnp.float32) + timed_ref[0]
    centred = hidden - jnp.mean(hidden, axis=1, keepdims=True)
    spread = lax.rsqrt(jnp.mean(centred * centred, axis=1, keepdims=True) + 1e-05)
    return centred * spread, spread


def first_kernel(noisy_ref, win_ref, timed_ref, norm_ref, w_ref, qkv_ref):
    unit, _ = first_state(noisy_ref, win_ref, timed_ref)
    normed = (unit * norm_ref[0:1] + norm_ref[1:2]).astype(LOW)
    qkv_ref[...] = jnp.dot(normed, w_ref[...], preferred_element_type=jnp.float32)


def first_back_kernel(
    items, noisy_ref, win_ref, timed_ref, norm_ref, w_ref, d_ref, dw_ref, in_ref, rows_ref
):
    step = pl.program_id(0)

    @pl.when(step == 0)
    def _():
        dw_ref[...] = jnp.zeros_like(dw_ref)
        in_ref[...] = jnp.zeros_like(in_ref)
        rows_ref[...] = jnp.zeros_like(rows_ref)

    unit, spread = first_state(noisy_ref, win_ref, timed_ref)
    gain = norm_ref[0:1]
    grads = d_ref[...]
    dw_ref[...] += rows_product((unit * gain + norm_ref[1:2]).astype(LOW), grads)
    grad_normed = times_transposed(grads, w_ref[...])
    scaled = grad_normed * gain
    grad_hidden = spread * (
        scaled
        - jnp.mean(scaled, axis=1, keepdims=True)
        - unit * jnp.mean(scaled * unit, axis=1, keepdims=True)
    )
    high = grad_hidden.astype(LOW)
    low = (grad_hidden - high.astype(jnp.float32)).astype(LOW)
    in_ref[...] += rows_product(noisy_ref[...], high) + rows_product(noisy_ref[...], low)
    item = step // (pl.num_programs(0) // items)
    at = lax.broadcasted_iota(jnp.int32, rows_ref.shape, 0)
    rows_ref[...] += (
        jnp.where(at == 0, jnp.sum(grad_normed * unit, axis=0, keepdims=True), 0.0)
        + jnp.where(at == 1, jnp.sum(grad_normed, axis=0, keepdims=True), 0.0)
        + jnp.where(at == 2 + item, jnp.sum(grad_hidden, axis=0, keepdims=True), 0.0)
    )


def first_specs(noisy, timed, weight):
    tokens, latent_dim = noisy.shape
    items = timed.shape[0]
    block = 256
    each = tokens // items // block
    rows = lambda lanes: pl.BlockSpec((block, lanes), lambda i: (i, 0))
    whole = lambda shape: pl.BlockSpec(shape, lambda i: (0, 0))
    specs = [
        rows(latent_dim),
        whole((latent_dim, D)),
        pl.BlockSpec((1, 1, D), lambda i: (i // each, 0, 0)),
        whole((2, D)),
        whole(weight.shape),
    ]
    return tokens // block, rows, whole, specs


def first_forward(noisy, win, timed, norm, weight):
    steps, rows, _, specs = first_specs(noisy, timed, weight)
    width = weight.shape[1]
    return pl.pallas_call(
        first_kernel,
        grid=(steps,),
        out_shape=jax.ShapeDtypeStruct((noisy.shape[0], width), jnp.float32),
        in_specs=specs,
        out_specs=rows(width),
        compiler_params=pltpu.CompilerParams(vmem_limit_bytes=40 << 20),
        cost_estimate=pl.CostEstimate(
            flops=2 * noisy.shape[0] * D * width, bytes_accessed=8 << 20, transcendentals=0
        ),
    )(noisy, win, timed, norm, weight)


def first_backward(noisy, win, timed, norm, weight, grads):
    steps, rows, whole, specs = first_specs(noisy, timed, weight)
    width = weight.shape[1]
    f32 = jnp.float32
    return pl.pallas_call(
        functools.partial(first_back_kernel, timed.shape[0]),
        grid=(steps,),
        out_shape=(
            jax.ShapeDtypeStruct((D, width), f32),
            jax.ShapeDtypeStruct((noisy.shape[1], D), f32),
            jax.ShapeDtypeStruct((8, D), f32),
        ),
        in_specs=specs + [rows(width)],
        out_specs=(whole((D, width)), whole((noisy.shape[1], D)), whole((8, D))),
        compiler_params=pltpu.CompilerParams(vmem_limit_bytes=40 << 20),
        cost_estimate=pl.CostEstimate(
            flops=8 * noisy.shape[0] * D * width, bytes_accessed=8 << 20, transcendentals=0
        ),
    )(noisy, win, timed, norm, weight, grads)


def cross_probs(query, key):
    scores = lax.dot_general(
        query, key, (((1,), (1,)), ((), ())), preferred_element_type=jnp.float32
    ) * (1.0 / math.sqrt(HEAD_DIM))
    grown = jnp.exp(scores - jnp.max(scores, axis=1, keepdims=True))
    return grown / jnp.sum(grown, axis=1, keepdims=True)


def cross_kernel(q_ref, pair_ref, two_ref, self_ref, o_ref, *by_owner):
    for head in range(HEADS):
        rank, local = head // LOCAL_HEADS, head % LOCAL_HEADS
        at = slice(head * HEAD_DIM, (head + 1) * HEAD_DIM)
        own = slice(local * HEAD_DIM, (local + 1) * HEAD_DIM)
        probs = cross_probs(q_ref[0, :, at], pair_ref[rank, 0, 0, :, own]).astype(LOW)
        o_ref[0, :, at] = jnp.dot(
            probs, pair_ref[rank, 1, 0, :, own], preferred_element_type=jnp.float32
        ).astype(LOW)
    planes = 4
    share = D // (planes * RANKS)
    for x_ref, out_ref in zip((self_ref, two_ref, o_ref), by_owner):
        for rank in range(RANKS):
            out_ref[rank, 0] = jnp.concatenate(
                [
                    x_ref[0, :, (plane * RANKS + rank) * share : (plane * RANKS + rank + 1) * share]
                    for plane in range(planes)
                ],
                axis=1,
            )


def cross_back_kernel(q_ref, pair_ref, do_ref, dq_ref, dpair_ref):
    scale = 1.0 / math.sqrt(HEAD_DIM)
    for head in range(HEADS):
        rank, local = head // LOCAL_HEADS, head % LOCAL_HEADS
        at = slice(head * HEAD_DIM, (head + 1) * HEAD_DIM)
        own = slice(local * HEAD_DIM, (local + 1) * HEAD_DIM)
        query, grads = q_ref[0, :, at], do_ref[0, :, at]
        key = pair_ref[rank, 0, 0, :, own]
        probs = cross_probs(query, key)
        pulled = lax.dot_general(
            grads,
            pair_ref[rank, 1, 0, :, own],
            (((1,), (1,)), ((), ())),
            preferred_element_type=jnp.float32,
        )
        delta = jnp.sum(probs * pulled, axis=1, keepdims=True)
        pushed = (probs * (pulled - delta)).astype(LOW)
        dq_ref[0, :, at] = (
            jnp.dot(pushed, key, preferred_element_type=jnp.float32) * scale
        ).astype(LOW)
        dpair_ref[rank, 0, 0, :, own] = rows_product(pushed, query) * scale
        dpair_ref[rank, 1, 0, :, own] = rows_product(probs.astype(LOW), grads)


def cross_specs(count, span, context_len):
    rows = pl.BlockSpec((1, span, D), lambda i: (i, 0, 0))
    pair = pl.BlockSpec((RANKS, 2, 1, context_len, COLS), lambda i: (0, 0, i, 0, 0))
    cost = pl.CostEstimate(
        flops=10 * count * span * context_len * D,
        bytes_accessed=8 * count * span * D,
        transcendentals=count * HEADS * span * context_len,
    )
    return rows, pair, cost


def cross_forward(queries, pair, two, own):
    count, span, _ = queries.shape
    rows, pair_spec, cost = cross_specs(count, span, pair.shape[3])
    owned = jax.ShapeDtypeStruct((RANKS, count, span, COLS), LOW)
    return pl.pallas_call(
        cross_kernel,
        grid=(count,),
        out_shape=(jax.ShapeDtypeStruct(queries.shape, LOW),) + (owned,) * 3,
        in_specs=[rows, pair_spec, rows, rows],
        out_specs=(rows,) + (pl.BlockSpec((RANKS, 1, span, COLS), lambda i: (0, i, 0, 0)),) * 3,
        compiler_params=pltpu.CompilerParams(vmem_limit_bytes=40 << 20),
        cost_estimate=cost,
    )(queries, pair, two, own)


def cross_backward(queries, pair, grads):
    count, span, _ = queries.shape
    rows, pair_spec, cost = cross_specs(count, span, pair.shape[3])
    return pl.pallas_call(
        cross_back_kernel,
        grid=(count,),
        out_shape=(
            jax.ShapeDtypeStruct(queries.shape, LOW),
            jax.ShapeDtypeStruct(pair.shape, jnp.float32),
        ),
        in_specs=[rows, pair_spec, rows],
        out_specs=(rows, pair_spec),
        compiler_params=pltpu.CompilerParams(vmem_limit_bytes=40 << 20),
        cost_estimate=cost,
    )(queries, pair, grads)


def fast_body(
    latents,
    gaussian_noise,
    timesteps,
    lengths,
    buckets,
    context,
    attention_weights,
    attention_moment,
    cross_weights,
    cross_moment,
    gate_up_weights,
    gate_up_first,
    gate_up_second,
    down_weights,
    down_first,
    down_second,
    latent_weights,
    latent_first,
    latent_second,
    timing_weights,
    timing_first,
    timing_second,
    norm_params,
    norm_first,
    norm_second,
):
    f32 = jnp.float32
    planes = lax.axis_size("z")
    z_at = lax.axis_index("z")
    rank = lax.axis_index("y") * lax.axis_size("f") + lax.axis_index("f")
    item_count, span, latent_dim = latents.shape
    frames = span * RANKS
    tokens = item_count * span
    group_tokens = item_count * frames
    flip = lambda array: jnp.swapaxes(array, 1, 2)

    attention_t = flip(attention_weights)
    cross_t = flip(cross_weights)
    attention_low = attention_t.astype(LOW)
    cross_low_t = cross_t.astype(LOW)
    small_low = jnp.concatenate(
        [
            latent_weights.reshape(-1, latent_weights.shape[2]),
            timing_weights,
            norm_params,
        ],
        axis=0,
    ).T.astype(LOW)
    signal = jnp.cos(0.5 * math.pi * timesteps)[:, None, None]
    noise_level = jnp.sin(0.5 * math.pi * timesteps)[:, None, None]
    noisy_own = (signal * latents + noise_level * gaussian_noise).astype(LOW)
    target_own = signal * gaussian_noise - noise_level * latents
    local_meta = jnp.stack([timesteps, lengths.astype(f32), buckets.astype(f32)])
    slab_of = lambda array: jnp.swapaxes(array.reshape(-1, RANKS, COLS), 0, 1)
    slab_all, cross_slab, small_all, noisy_all, meta_all = setup_exchange(
        slab_of(attention_low[:3]),
        slab_of(cross_low_t),
        small_low,
        noisy_own.reshape(-1, latent_dim),
        jnp.pad(local_meta, ((0, 5), (0, 128 - item_count))),
        16,
    )
    attention_rest, slab_all = lax.optimization_barrier((attention_low[3:], slab_all))
    small_all = small_all.reshape(D, -1)
    latent_in = small_all[:, :LAT].T
    latent_out = small_all[:, LAT : 2 * LAT].T
    timing = small_all[:, 2 * LAT : 2 * LAT + FOUR].T
    norms = small_all[:, 2 * LAT + FOUR :].astype(f32).T
    qkv_slab = slab_all.reshape(planes * RANKS, 3, -1, COLS)
    qkv_t = jnp.concatenate([qkv_slab[:, i].reshape(D, COLS) for i in range(3)], axis=1)
    meta = jnp.swapaxes(meta_all[:, :3, :item_count], 0, 1).reshape(3, -1)
    times_all = meta[0]
    lengths_all = meta[1]
    onehot_all = (meta[2][:, None] == jnp.arange(NBUCK, dtype=f32)[None, :]).astype(f32)
    counts = jnp.dot(lengths_all, onehot_all, precision=HIGHEST)
    present = jnp.sum((counts > 0).astype(f32))
    bucket_scale = 1.0 / (present * LAT * jnp.maximum(counts, 1.0))
    own_at = z_at * item_count
    onehot = lax.dynamic_slice_in_dim(onehot_all, own_at, item_count, 0)
    item_scale = jnp.dot(onehot, bucket_scale, precision=HIGHEST)
    own_lengths = lax.dynamic_slice_in_dim(lengths_all, own_at, item_count, 0).astype(jnp.int32)
    features_all = time_features(times_all).astype(LOW)
    features = lax.dynamic_slice_in_dim(features_all, own_at, item_count, 0)

    noisy_low = jnp.swapaxes(
        noisy_all.reshape(RANKS, item_count, span, latent_dim), 0, 1
    ).reshape(item_count, frames, latent_dim)
    target = lax.ppermute(
        target_own, ALL, [(4 * s + g, RANKS * g + s) for s in range(RANKS) for g in range(planes)]
    ).reshape(tokens, latent_dim)
    context_all = lax.all_gather(context, "f", axis=0, tiled=True)
    context_own = lax.dynamic_slice_in_dim(context_all, own_at, item_count, 0).reshape(-1, E)
    context_len = context.shape[1]

    rest_t = lax.all_gather(attention_rest, ALL, axis=1, tiled=True)
    gate_up = lax.all_gather(gate_up_weights.astype(LOW), "z", axis=0, tiled=True)
    down_pairs = []
    for p in range(planes):
        for r in range(RANKS):
            down_pairs.append((2 * RANKS * (p // 2) + 2 * r + p % 2, RANKS * p + r))
    down = lax.all_gather(
        lax.ppermute(down_weights.astype(LOW), ALL, down_pairs), "z", axis=0, tiled=True
    )

    half_dim = HEAD_DIM // 2
    inverse = 10000.0 ** (-jnp.arange(half_dim, dtype=f32) / half_dim)
    angles = jnp.arange(frames, dtype=f32)[:, None] * inverse[None, :]
    cosine = jnp.concatenate([jnp.cos(angles)] * 2, axis=1)
    sine_table = jnp.concatenate([-jnp.sin(angles), jnp.sin(angles)], axis=1)

    timed = matmul_low(features, timing)
    noisy_mine = lax.dynamic_slice_in_dim(noisy_low, rank * span, span, 1)
    start_own = (
        matmul_low(noisy_mine.reshape(tokens, latent_dim), latent_in).reshape(item_count, span, D)
        + timed[:, None, :]
    ).reshape(tokens, D)
    noisy_mine = noisy_mine.reshape(tokens, latent_dim)
    first = (
        noisy_low.reshape(group_tokens, latent_dim),
        latent_in,
        timed[:, None, :],
        norms[:2],
        qkv_t,
    )
    queries, key_rows, values, mixed, mixed_heads, log_total = attend(
        first_forward(*first).reshape(item_count, frames, 3 * COLS),
        cosine,
        sine_table,
        own_lengths,
        span,
    )
    mixed_heads = mixed_heads.reshape(RANKS, tokens, COLS)
    cross_slab = cross_slab.reshape(-1, COLS)
    mixed_low, cross_slabs = plane_step(1, 25, swaps=[mixed_heads], carry=[cross_slab])
    mixed_low = jnp.swapaxes(mixed_low, 0, 1).reshape(tokens, D)
    cross_slabs = jnp.concatenate([cross_slab[None], cross_slabs], axis=0)
    cross_slabs = jnp.take(cross_slabs, jnp.arange(planes) ^ z_at, axis=0, mode="clip")
    cross_slabs = cross_slabs.reshape(planes * RANKS, 2, -1, COLS)
    cross_w = [cross_slabs[:, i].reshape(E, COLS) for i in range(2)]
    after_self = start_own + matmul_low(mixed_low, rest_t[0])
    normed_two, back_two = jax.vjp(layer_norm, after_self, norms[2], norms[3])
    normed_two = normed_two.astype(LOW)
    cross_query = matmul_low(normed_two, rest_t[1]).astype(LOW).reshape(item_count, span, D)
    pair_own = jnp.stack(
        [matmul_low(context_own, cross_w[0]), matmul_low(context_own, cross_w[1])]
    ).astype(LOW)
    (pair_all,) = plane_step(3, 12, gathers=[pair_own.reshape(-1, COLS)])
    pair_all = pair_all.reshape(RANKS, 2, item_count, context_len, COLS)
    cross_out, *owned = cross_forward(
        cross_query,
        pair_all,
        normed_two.reshape(item_count, span, D),
        mixed_low.reshape(item_count, span, D),
    )
    cross_out = cross_out.reshape(tokens, D)
    owned = [array.reshape(RANKS, tokens, COLS) for array in owned]
    after_cross = after_self + matmul_low(cross_out, rest_t[2])
    normed_three, back_three = jax.vjp(layer_norm, after_cross, norms[4], norms[5])
    normed_three = normed_three.astype(LOW)
    normed_group, self_heads, two_heads, out_heads = plane_step(
        4, 70, gathers=[normed_three], swaps=owned
    )
    normed_group = normed_group.reshape(group_tokens, D)
    gate_both = times_transposed(normed_group, gate_up)
    units = gate_both.shape[1] // 2
    gate_half, up_half = (gate_both[:, :units], gate_both[:, units:])
    inner_act = (jax.nn.silu(gate_half) * up_half).astype(LOW)
    final_state = (
        after_cross
        + plane_step(5, 65, sums=[matmul_low(inner_act, down).reshape(RANKS, tokens, D)])[0]
    ).astype(LOW)
    predicted = times_transposed(final_state, latent_out)

    position = rank * span + jnp.arange(span)
    live_mask = position[None, :] < own_lengths[:, None]
    difference = predicted - target
    errors = jnp.sum(difference * difference, axis=1).reshape(item_count, span)
    per_item = jnp.sum(jnp.where(live_mask, errors, 0.0), axis=1)
    partial_loss = jnp.sum(per_item * item_scale)
    frame_scale = jnp.where(live_mask, item_scale[:, None], 0.0).reshape(tokens, 1)
    grad_pred = (2.0 * difference * frame_scale).astype(LOW)

    grad_out_proj = rows_product(grad_pred, final_state)
    grad_state = matmul_low(grad_pred, latent_out)
    (grad_group,) = plane_step(6, 30, gathers=[grad_state.astype(LOW)])
    grad_group = grad_group.reshape(group_tokens, D)
    down_part = rows_product(inner_act, grad_group)
    grad_inner = times_transposed(grad_group, down)
    sigmoid_gate = jax.nn.sigmoid(gate_half)
    grad_gate = grad_inner * up_half * sigmoid_gate * (1.0 + gate_half * (1.0 - sigmoid_gate))
    grad_both = jnp.concatenate([grad_gate, grad_inner * gate_half * sigmoid_gate], axis=1).astype(
        LOW
    )
    gate_up_part = rows_product(grad_both, normed_group)
    gate_up_part = gate_up_part.reshape(planes, -1, D)
    early = gate_up_part.shape[1] // 3
    early_tops, early_words = line_pack(gate_up_part[:, :early])
    late_tops, late_words = line_pack(gate_up_part[:, early:])
    grad_three, early_tops, early_words = plane_step(
        8,
        65,
        sums=[matmul_low(grad_both, gate_up).reshape(RANKS, tokens, D)],
        carry=[early_tops, early_words],
    )
    residual_part, gain_three, shift_three = back_three(grad_three)
    grad_state = grad_state + residual_part
    grad_branch = grad_state.astype(LOW)
    cross_branch = grad_branch
    grad_mix = times_transposed(grad_branch, rest_t[2]).astype(LOW).reshape(item_count, span, D)
    grad_cross_query, grad_pair = cross_backward(cross_query, pair_all, grad_mix)
    grad_cross_query = grad_cross_query.reshape(tokens, D)
    (
        grad_pair,
        cross_branch,
        query_branch,
        late_tops,
        late_words,
    ) = plane_step(
        9,
        90,
        sums=[grad_pair.reshape(RANKS, -1, COLS)],
        gathers=[cross_branch, grad_cross_query],
        carry=[late_tops, late_words],
    )
    down_part, grad_pair = lax.optimization_barrier((down_part, grad_pair))
    down_sum = lax.psum_scatter(down_part, "z", scatter_dimension=0, tiled=True)
    gate_up_grad = jnp.concatenate(
        [
            line_total(gate_up_part[:, :early], early_tops, early_words),
            line_total(gate_up_part[:, early:], late_tops, late_words),
        ],
        axis=0,
    )
    grad_pair = grad_pair.reshape(2, item_count * context_len, COLS)
    cross_part = rows_precise(
        context_own.astype(f32), jnp.concatenate([grad_pair[0], grad_pair[1]], axis=1)
    ).reshape(planes, -1, 2 * COLS)
    by_plane = lambda parts: parts.reshape(planes, -1, D)
    cross_out_part = by_plane(
        rows_product(out_heads.reshape(group_tokens, COLS), cross_branch.reshape(group_tokens, D))
    )
    cross_q_part = by_plane(
        rows_product(two_heads.reshape(group_tokens, COLS), query_branch.reshape(group_tokens, D))
    )
    residual_part, gain_two, shift_two = back_two(times_transposed(grad_cross_query, rest_t[1]))
    grad_state = grad_state + residual_part
    grad_branch = grad_state.astype(LOW)
    (
        branch_group,
        cq_tops,
        cq_words,
        co_tops,
        co_words,
        cross_tops,
        cross_words,
    ) = plane_step(
        2,
        35,
        gathers=[grad_branch],
        carry=line_pack(cross_q_part) + line_pack(cross_out_part) + line_pack(cross_part),
    )
    branch_group = branch_group.reshape(group_tokens, D)
    cross_sums = jnp.stack(
        [
            line_total(cross_q_part, cq_tops, cq_words),
            line_total(cross_out_part, co_tops, co_words),
        ]
    )
    out_rows = lax.dynamic_slice_in_dim(rest_t[0], rank * COLS, COLS, 0)
    self_out_sum = lax.psum_scatter(
        rows_product(self_heads.reshape(group_tokens, COLS), branch_group),
        "z",
        scatter_dimension=0,
        tiled=True,
    )
    grad_mixed = times_transposed(branch_group, out_rows).astype(LOW)
    grad_triple = attend_back(
        queries,
        key_rows,
        values,
        mixed,
        log_total,
        grad_mixed.reshape(RANKS, item_count, span, COLS),
        cosine,
        sine_table,
        own_lengths,
    ).reshape(group_tokens, 3 * COLS)
    qkv_part, grad_in_proj, first_rows = first_backward(*first, grad_triple)
    qkv_part = qkv_part.reshape(planes, -1, 3 * COLS)
    gain_one, shift_one = (first_rows[0], first_rows[1])
    grad_in_proj = grad_in_proj + rows_precise(noisy_mine.astype(f32), grad_state)
    grad_timed = first_rows[2 : 2 + item_count] + jnp.sum(
        grad_state.reshape(item_count, span, D), axis=1
    )
    timed_slots = lax.dynamic_update_slice(
        jnp.zeros((item_count * planes, D), f32), grad_timed, (own_at, 0)
    )
    small_grad = jnp.concatenate(
        [
            grad_in_proj,
            grad_out_proj,
            timed_slots,
            jnp.stack([gain_one, shift_one, gain_two, shift_two, gain_three, shift_three]),
            jnp.zeros((2, D), f32),
        ],
        axis=0,
    )
    small_grad, down_sum, self_out_sum = lax.optimization_barrier(
        (small_grad, down_sum, self_out_sum)
    )
    by_target = small_grad.T.reshape(planes, 2, 2, 2, -1, small_grad.shape[0])
    small_grad, qkv_tops, qkv_words = full_scatter(
        jnp.transpose(by_target, (3, 2, 1, 0, 4, 5)),
        17,
        line_pack(qkv_part),
    )
    small_grad = small_grad.T
    rest_grad = jnp.concatenate([self_out_sum[None], cross_sums], axis=0)
    qkv_grad = line_total(qkv_part, qkv_tops, qkv_words)
    cross_grad = line_total(cross_part, cross_tops, cross_words)
    latent_grad = small_grad[: 2 * LAT].reshape(2, LAT, -1)
    timed_end = 2 * LAT + timed_slots.shape[0]
    norm_grad = small_grad[timed_end : timed_end + 6]
    timing_grad = rows_precise(features_all.astype(f32), small_grad[2 * LAT : timed_end])
    everything = (
        qkv_grad,
        self_out_sum,
        cross_sums,
        cross_grad,
        latent_grad,
        timing_grad,
        norm_grad,
        gate_up_grad,
        down_sum,
    )
    squares = sum((jnp.sum(grad * grad) for grad in everything))
    down_tops, down_words = line_pack(down_sum[None])
    qkv_grad, cross_grad, totals, down_tops, down_words = plane_step(
        14,
        30,
        swaps=[
            qkv_grad.reshape(RANKS, -1, 3 * COLS),
            cross_grad.reshape(RANKS, -1, 2 * COLS),
        ],
        everyone=[lanes_of([squares, partial_loss])],
        moves=[down_tops, down_words[0]],
    )
    down_grad = jnp.concatenate(
        [
            lax.shift_right_arithmetic(down_words, 16),
            lax.shift_right_arithmetic(lax.shift_left(down_words, 16), 16),
        ],
        axis=0,
    ).astype(f32) * (down_tops[0] * (1.0 / LEVELS))[:, None]
    totals = jnp.sum(totals, axis=0)
    squares, loss_value = (totals[0, 0], totals[0, 1])
    qkv_grad = jnp.transpose(qkv_grad.reshape(RANKS, -1, 3, COLS), (2, 1, 0, 3)).reshape(3, -1, D)
    cross_grad = jnp.transpose(cross_grad.reshape(RANKS, -1, 2, COLS), (2, 1, 0, 3)).reshape(
        2, -1, D
    )
    attention_grad = jnp.concatenate([qkv_grad, rest_grad], axis=0)

    clip_norm = jnp.sqrt(squares)
    factor = CLIP_AT / jnp.maximum(clip_norm, CLIP_AT)

    moment_t = 0.95 * flip(attention_moment) + attention_grad * factor
    cross_moment_t = 0.95 * flip(cross_moment) + cross_grad * factor
    pair = 2 * HEAD_DIM
    blocks = [
        moment.reshape(moment.shape[0], moment.shape[1], D // pair, pair)
        for moment in (moment_t, cross_moment_t)
    ]
    left_lane = jnp.arange(pair) < HEAD_DIM
    grams = jnp.concatenate(
        [
            jnp.einsum("skbi,skbj->sbij", block, block, precision=HIGHEST).reshape(-1, pair, pair)
            for block in blocks
        ]
    )
    grams = jnp.where(left_lane, grams[:, :HEAD_DIM], grams[:, HEAD_DIM:])
    mixers = full_newton(grams.reshape(2, 2, 2, planes, -1, pair), 18)
    mixers = mixers.reshape(-1, D // pair, HEAD_DIM, pair)
    mixers = jnp.concatenate(
        [jnp.where(left_lane, mixers, 0.0), jnp.where(left_lane, 0.0, mixers)], axis=2
    )
    stacks = attention_t.shape[0]
    orth = [
        jnp.einsum("skbj,sbji->skbi", block, mixer, precision=HIGHEST).reshape(moment.shape)
        for block, mixer, moment in zip(
            blocks, (mixers[:stacks], mixers[stacks:]), (moment_t, cross_moment_t)
        )
    ]
    attention_new = attention_t * (1.0 - MUON_RATE * DECAY_RATE) - MUON_RATE * orth[0]
    cross_new = cross_t * (1.0 - MUON_RATE * DECAY_RATE) - MUON_RATE * orth[1]
    gate_up_new, gate_up_first_new, gate_up_second_new = adam_update(
        gate_up_weights, gate_up_first, gate_up_second, gate_up_grad * factor, ADAM_RATE, DECAY_RATE
    )
    down_new, down_first_new, down_second_new = adam_update(
        down_weights, down_first, down_second, down_grad * factor, ADAM_RATE, DECAY_RATE
    )
    latent_new, latent_first_new, latent_second_new = adam_update(
        latent_weights, latent_first, latent_second, latent_grad * factor, ADAM_RATE, DECAY_RATE
    )
    timing_new, timing_first_new, timing_second_new = adam_update(
        timing_weights, timing_first, timing_second, timing_grad * factor, ADAM_RATE, DECAY_RATE
    )
    norm_new, norm_first_new, norm_second_new = adam_update(
        norm_params, norm_first, norm_second, norm_grad * factor, GAIN_RATE, 0.0
    )
    return (
        loss_value,
        clip_norm,
        flip(attention_new),
        flip(moment_t),
        flip(attention_new.astype(LOW)),
        flip(cross_new),
        flip(cross_moment_t),
        flip(cross_new.astype(LOW)),
        gate_up_new,
        gate_up_first_new,
        gate_up_second_new,
        gate_up_new.astype(LOW),
        down_new,
        down_first_new,
        down_second_new,
        down_new.astype(LOW),
        latent_new,
        latent_first_new,
        latent_second_new,
        latent_new.astype(LOW),
        timing_new,
        timing_first_new,
        timing_second_new,
        timing_new.astype(LOW),
        norm_new,
        norm_first_new,
        norm_second_new,
    )


def solution(mesh):
    if tuple(mesh.devices.shape) != (RANKS, 4):
        return general(mesh)
    mesh3 = jax.sharding.Mesh(mesh.devices.reshape(4, 2, 4), ALL)
    seq = ("z", "y")
    row = P(ALL, None)
    col2 = P(None, ALL)
    col3 = P(None, None, ALL)
    return jax.shard_map(
        fast_body,
        mesh=mesh3,
        in_specs=(P("f", seq, None),) * 2
        + (P("f"),) * 3
        + (P("f", None, None),)
        + (col3,) * 4
        + (row,) * 6
        + (col3,) * 3
        + (col2,) * 6,
        out_specs=(P(),) * 2 + (col3,) * 6 + (row,) * 8 + (col3,) * 4 + (col2,) * 7,
        check_vma=False,
    )
```
